32 devices in a mesh: cfg: 2 (over core), patch: 8 (over z, x), req: 2 (over y).
Axes of the slice: x: 2, y: 2, z: 4, core: 2. Of those that a mesh axis runs over, the one named last changes fastest.
Arguments:
- latents: bfloat16 [2, 2, 32, 256, 320], P('cfg', 'req', 'patch'), may hold values from -60 to 60
- time_embed: bfloat16 [2, 1280], P('req'), may hold values from -6 to 6
- steer_scale: float32 [2], P('req'), may hold values from 0.5 to 4
- gain_one: float32 [320], replicated, may hold values from 0.5 to 1.5
- shift_one: float32 [320], replicated, may hold values from -3 to 3
- conv_one: bfloat16 [3, 3, 320, 320], replicated, may hold values from -0.109375 to 0.109375
- bias_one: float32 [320], replicated, may hold values from -3 to 3
- time_weight: bfloat16 [1280, 320], P('patch'), may hold values from -0.15625 to 0.15625
- time_bias: float32 [320], replicated, may hold values from -3 to 3
- gain_two: float32 [320], replicated, may hold values from 0.5 to 1.5
- shift_two: float32 [320], replicated, may hold values from -3 to 3
- conv_two: bfloat16 [3, 3, 320, 320], replicated, may hold values from -0.109375 to 0.109375
- bias_two: float32 [320], replicated, may hold values from -3 to 3
Outputs:
- block_out: bfloat16 [2, 2, 32, 256, 320], P('cfg', 'req', 'patch')
The draws below stay inside these ranges and needn't reach their ends.
All inputs are finite; a program needn't handle non-finite values.
Results may differ from the reference program's by a relative error of at most 0.0034.
Values may be sent and summed in bfloat16 or wider, within the bound.
No kernel may reach another device: no remote copies, remote signals or barrier semaphores. Data moves between devices by JAX's collectives and lax.ppermute only.
A program may use at most 64 MiB of HBM per device.

```python
import math
import jax
import jax.numpy as jnp
from jax import lax

C = 320
TEMB = 1280
GROUPS = 32
COLS = 256
HEIGHT = 32
BATCH = 2


def draw_latents(key, part):
    key = jax.random.fold_in(key, 11)
    keys = jax.random.split(key, 4)
    spread = math.log(3.2)
    positions = jnp.arange(HEIGHT).astype(jnp.float32) / max(HEIGHT - 1, 1)
    row_factor = jnp.exp(positions * math.log(3.0) + jax.random.uniform(keys[0], (HEIGHT,), jnp.float32, 0.0, spread))
    col_factor = jnp.exp(jax.random.uniform(keys[1], (COLS,), jnp.float32, 0.0, spread))
    chan_factor = jnp.exp(jax.random.uniform(keys[2], (C,), jnp.float32, 0.0, spread))
    scale = 0.15 * row_factor[:, None, None] * col_factor[None, :, None] * chan_factor[None, None, :]
    shape = (2, BATCH, HEIGHT, COLS, C)
    base = jax.random.truncated_normal(keys[3], -4.0, 4.0, shape, jnp.float32)
    return (base * scale).astype(jnp.bfloat16)


def level_of(own_key, extent, shards, smallest, top_value):
    level, own = 1.0, jax.random.fold_in(own_key, 6)
    for axis_at, parts in shards:
        draws = jnp.exp(jax.random.uniform(jax.random.fold_in(own, axis_at), (parts,), jnp.float32, smallest / len(shards), top_value / len(shards)))
        level = level * jnp.repeat(draws, extent[axis_at] // parts).reshape([-1 if axis == axis_at else 1 for axis in range(len(extent))])
    return level


def scatter_about(stream_key, extent, scale, reach, cuts=(), kind=jnp.bfloat16):
    result = scale * jax.random.normal(stream_key, extent, jnp.float32)
    if cuts:
        result = result * level_of(stream_key, extent, cuts, -0.22, 0.18)
    return jnp.clip(result, -reach, reach).astype(kind)


def setup_inputs(seed: int = 0) -> dict:
    arg_keys = jax.random.split(jax.random.key(seed), 14)
    latents = draw_latents(jax.random.fold_in(arg_keys[13], 71), 0)
    time_embed = scatter_about(arg_keys[1], (BATCH, TEMB), 1.0, 6.0, ((0, 2),))
    steer_scale = jnp.clip(jnp.exp(math.log(4.0) - 2.0794415 * jax.random.uniform(arg_keys[2], (BATCH,), jnp.float32) ** level_of(arg_keys[2], (BATCH,), ((0, 2),), -0.2, 0.2)), 0.5, 4.0)
    gain_one = jnp.clip(jax.random.uniform(arg_keys[3], (C,), jnp.float32, 0.5, 1.5), 0.5, 1.5)
    shift_one = scatter_about(arg_keys[4], (C,), 0.5, 3.0, (), jnp.float32)
    conv_one = scatter_about(arg_keys[5], (3, 3, C, C), (9 * C) ** -0.5, 0.109375)
    bias_one = scatter_about(arg_keys[6], (C,), 0.5, 3.0, (), jnp.float32)
    time_weight = scatter_about(arg_keys[7], (TEMB, C), TEMB ** -0.5, 0.15625, ((0, 8),))
    time_bias = scatter_about(arg_keys[8], (C,), 0.5, 3.0, (), jnp.float32)
    gain_two = jnp.clip(jax.random.uniform(arg_keys[9], (C,), jnp.float32, 0.5, 1.5), 0.5, 1.5)
    shift_two = scatter_about(arg_keys[10], (C,), 0.5, 3.0, (), jnp.float32)
    conv_two = scatter_about(arg_keys[11], (3, 3, C, C), (9 * C) ** -0.5, 0.109375)
    bias_two = scatter_about(arg_keys[12], (C,), 0.5, 3.0, (), jnp.float32)
    return {"latents": latents, "time_embed": time_embed, "steer_scale": steer_scale, "gain_one": gain_one, "shift_one": shift_one, "conv_one": conv_one, "bias_one": bias_one, "time_weight": time_weight, "time_bias": time_bias, "gain_two": gain_two, "shift_two": shift_two, "conv_two": conv_two, "bias_two": bias_two}


EPS = 1e-05

def norm_silu(values, gain, shift):
    branches, rows, cols, chans = values.shape
    view = values.reshape(branches, rows, cols, GROUPS, chans // GROUPS)
    mean = lax.optimization_barrier(jnp.mean(view, axis=(1, 2, 4), keepdims=True))
    centred = view - mean
    spread = lax.optimization_barrier(jnp.mean(centred * centred, axis=(1, 2, 4), keepdims=True))
    normed = (centred * lax.rsqrt(spread + EPS)).reshape(values.shape) * gain + shift
    return jax.nn.silu(normed)

def convolve(acts, weight):
    branches, rows, cols, chans = acts.shape
    padded = jnp.pad(acts.astype(jnp.float32), ((0, 0), (1, 1), (1, 1), (0, 0)))
    total = jnp.zeros((branches, rows, cols, weight.shape[3]), jnp.float32)
    for shift_y in range(3):
        for shift_x in range(3):
            window = padded[:, shift_y:shift_y + rows, shift_x:shift_x + cols]
            total = total + jnp.einsum('nhwc,cd->nhwd', window, weight[shift_y, shift_x].astype(jnp.float32), precision=lax.Precision.HIGHEST)
    return total

def reference(latents, time_embed, steer_scale, gain_one, shift_one, conv_one, bias_one, time_weight, time_bias, gain_two, shift_two, conv_two, bias_two):
    time_act = jax.nn.silu(time_embed.astype(jnp.float32)).astype(jnp.bfloat16)
    time_shift = jnp.dot(time_act, time_weight, preferred_element_type=jnp.float32) + time_bias

    def one_request(items):
        latent_pair, shift_row, scale_value = items
        source = latent_pair.astype(jnp.float32)
        act_one = norm_silu(source, gain_one, shift_one).astype(jnp.bfloat16)
        hidden = (convolve(act_one, conv_one) + bias_one + shift_row).astype(jnp.bfloat16)
        wide = hidden.astype(jnp.float32)
        steered = wide + scale_value * (wide[0] - wide[1])
        act_two = norm_silu(steered, gain_two, shift_two).astype(jnp.bfloat16)
        return (source + convolve(act_two, conv_two) + bias_two).astype(jnp.bfloat16)
    outputs = lax.map(one_request, (jnp.moveaxis(latents, 1, 0), time_shift, steer_scale))
    return jnp.moveaxis(outputs, 0, 1)
```

```python
import jax
import jax.numpy as jnp
from jax import lax
from jax.sharding import PartitionSpec as P

GROUPS = 32


EPS = 1e-05


def extended(array, sides, width):
    for axis, dim in sides:
        peers, length = (lax.axis_size(axis), array.shape[dim])
        up = [(i, (i + 1) % peers) for i in range(peers - 1)]
        down = [(j, i) for i, j in up]
        last = lax.slice_in_dim(array, length - width, length, axis=dim)
        first = lax.slice_in_dim(array, 0, width, axis=dim)
        before = lax.ppermute(last, axis, up)
        after = lax.ppermute(first, axis, down)
        array = jnp.concatenate([before, array, after], axis=dim)
    return array


def from_partner(value, axis, stride):
    mask = 2**stride
    pairs = [(source, source ^ mask) for source in range(lax.axis_size(axis))]
    return lax.ppermute(value, axis, pairs)


def gathered(rows, axes):
    peers = lax.axis_size(axes)
    return lax.all_to_all(jnp.broadcast_to(rows[None], (peers,) + rows.shape), axes, 0, 0)


def local_moments(values):
    batch_rows, rows, cols, chans = values.shape
    view = values.reshape(batch_rows, rows, cols, GROUPS, chans // GROUPS)
    count = float(rows * cols * (chans // GROUPS))
    mean = jnp.sum(view, axis=(1, 2, 4)) / count
    centred = view - mean[:, None, None, :, None]
    return (mean, jnp.sum(centred * centred, axis=(1, 2, 4)), count)


def combined(means, squares, count):
    mean = jnp.mean(means, axis=0)
    off = means - mean
    spread = jnp.sum(squares + count * off * off, axis=0) / (count * means.shape[0])
    return (mean, spread)


def activate(values, mean, spread, gain, shift):
    batch_rows, rows, cols, chans = values.shape
    view = values.reshape(batch_rows, rows, cols, GROUPS, chans // GROUPS)
    normed = (view - mean[:, None, None, :, None]) * lax.rsqrt(spread + EPS)[:, None, None, :, None]
    return jax.nn.silu(normed.reshape(values.shape) * gain + shift)


def pad_columns(acts):
    return jnp.pad(acts, ((0, 0), (0, 0), (1, 1), (0, 0)))


def surround(acts):
    return pad_columns(extended(acts, (("patch", 1),), 1))


def convolve(padded, weight):
    rows = padded.shape[1] - 2
    cols = padded.shape[2] - 2
    total = None
    for shift_y in range(3):
        for shift_x in range(3):
            term = jnp.einsum(
                "rhwc,cd->rhwd",
                padded[:, shift_y : shift_y + rows, shift_x : shift_x + cols],
                weight[shift_y, shift_x],
                preferred_element_type=jnp.float32,
            )
            total = term if total is None else total + term
    return total


def body(
    latents,
    time_embed,
    steer_scale,
    gain_one,
    shift_one,
    conv_one,
    bias_one,
    time_weight,
    time_bias,
    gain_two,
    shift_two,
    conv_two,
    bias_two,
):
    latent_rows = latents[0]
    batch_rows, own_rows, cols, chans = latent_rows.shape
    time_act = jax.nn.silu(time_embed.astype(jnp.float32)).astype(jnp.bfloat16)
    embed_rows = time_weight.shape[0]
    own_embed = lax.dynamic_slice_in_dim(
        time_act, lax.axis_index("patch") * embed_rows, embed_rows, 1
    )
    time_part = jnp.dot(own_embed, time_weight, preferred_element_type=jnp.float32)
    is_cond = lax.axis_index("cfg") == 0
    steer = steer_scale[:, None, None, None]
    source = latent_rows.astype(jnp.float32)
    mean_part, square_part, count = local_moments(source)
    seen = gathered(jnp.concatenate([mean_part, square_part, time_part], axis=1), "patch")
    mean_one, spread_one = combined(seen[:, :, :GROUPS], seen[:, :, GROUPS : 2 * GROUPS], count)
    time_shift = (jnp.sum(seen[:, :, 2 * GROUPS :], axis=0) + time_bias)[:, None, None, :]
    act_one = activate(source, mean_one, spread_one, gain_one, shift_one).astype(jnp.bfloat16)
    hidden = (convolve(surround(act_one), conv_one) + bias_one + time_shift).astype(jnp.bfloat16)
    partner_rows = from_partner(hidden, "cfg", 0)
    own_vals = hidden.astype(jnp.float32)
    far_vals = partner_rows.astype(jnp.float32)
    steered = own_vals + steer * jnp.where(is_cond, own_vals - far_vals, far_vals - own_vals)
    mean_part, square_part, count = local_moments(steered)
    seen = gathered(jnp.concatenate([mean_part, square_part], axis=1), "patch")
    mean_two, spread_two = combined(seen[:, :, :GROUPS], seen[:, :, GROUPS:], count)
    act_two = activate(steered, mean_two, spread_two, gain_two, shift_two).astype(jnp.bfloat16)
    image = convolve(surround(act_two), conv_two)
    block_out = (source + image + bias_two).astype(jnp.bfloat16)
    return block_out[None]


def solution(mesh):
    placed = (
        P("cfg", "req", "patch", None, None),
        P("req", None),
        P("req"),
        P(),
        P(),
        P(),
        P(),
        P("patch", None),
        P(),
        P(),
        P(),
        P(),
        P(),
    )
    return jax.shard_map(
        body,
        mesh=mesh,
        in_specs=placed,
        out_specs=P("cfg", "req", "patch", None, None),
        check_vma=False,
    )
```

```python
import jax
import jax.numpy as jnp
from jax import lax
from jax.sharding import PartitionSpec as P

GROUPS = 32


EPS = 1e-05


def extended(array, sides, width):
    for axis, dim in sides:
        peers, length = (lax.axis_size(axis), array.shape[dim])
        up = [(i, (i + 1) % peers) for i in range(peers - 1)]
        down = [(j, i) for i, j in up]
        last = lax.slice_in_dim(array, length - width, length, axis=dim)
        first = lax.slice_in_dim(array, 0, width, axis=dim)
        before = lax.ppermute(last, axis, up)
        after = lax.ppermute(first, axis, down)
        array = jnp.concatenate([before, array, after], axis=dim)
    return array


def from_partner(value, axis, stride):
    mask = 2**stride
    pairs = [(source, source ^ mask) for source in range(lax.axis_size(axis))]
    return lax.ppermute(value, axis, pairs)


def gathered(rows, axes):
    return lax.all_gather(rows, axes)


def local_moments(values):
    batch_rows, rows, cols, chans = values.shape
    view = values.reshape(batch_rows, rows, cols, GROUPS, chans // GROUPS)
    count = float(rows * cols * (chans // GROUPS))
    mean = jnp.sum(view, axis=(1, 2, 4)) / count
    centred = view - mean[:, None, None, :, None]
    return (mean, jnp.sum(centred * centred, axis=(1, 2, 4)), count)


def combined(means, squares, count):
    mean = jnp.mean(means, axis=0)
    off = means - mean
    spread = jnp.sum(squares + count * off * off, axis=0) / (count * means.shape[0])
    return (mean, spread)


def activate(values, mean, spread, gain, shift):
    batch_rows, rows, cols, chans = values.shape
    view = values.reshape(batch_rows, rows, cols, GROUPS, chans // GROUPS)
    normed = (view - mean[:, None, None, :, None]) * lax.rsqrt(spread + EPS)[:, None, None, :, None]
    return jax.nn.silu(normed.reshape(values.shape) * gain + shift)


def pad_columns(acts):
    return jnp.pad(acts, ((0, 0), (0, 0), (1, 1), (0, 0)))


def surround(acts):
    return pad_columns(extended(acts, (("patch", 1),), 1))


def convolve(padded, weight):
    rows = padded.shape[1] - 2
    cols = padded.shape[2] - 2
    total = None
    for shift_y in range(3):
        for shift_x in range(3):
            term = jnp.einsum(
                "rhwc,cd->rhwd",
                padded[:, shift_y : shift_y + rows, shift_x : shift_x + cols],
                weight[shift_y, shift_x],
                preferred_element_type=jnp.float32,
            )
            total = term if total is None else total + term
    return total


def body(
    latents,
    time_embed,
    steer_scale,
    gain_one,
    shift_one,
    conv_one,
    bias_one,
    time_weight,
    time_bias,
    gain_two,
    shift_two,
    conv_two,
    bias_two,
):
    latent_rows = latents[0]
    batch_rows, own_rows, cols, chans = latent_rows.shape
    time_act = jax.nn.silu(time_embed.astype(jnp.float32)).astype(jnp.bfloat16)
    embed_rows = time_weight.shape[0]
    own_embed = lax.dynamic_slice_in_dim(
        time_act, lax.axis_index("patch") * embed_rows, embed_rows, 1
    )
    time_part = jnp.dot(own_embed, time_weight, preferred_element_type=jnp.float32)
    is_cond = lax.axis_index("cfg") == 0
    steer = steer_scale[:, None, None, None]
    source = latent_rows.astype(jnp.float32)
    mean_part, square_part, count = local_moments(source)
    seen = gathered(jnp.concatenate([mean_part, square_part, time_part], axis=1), "patch")
    mean_one, spread_one = combined(seen[:, :, :GROUPS], seen[:, :, GROUPS : 2 * GROUPS], count)
    time_shift = (jnp.sum(seen[:, :, 2 * GROUPS :], axis=0) + time_bias)[:, None, None, :]
    act_one = activate(source, mean_one, spread_one, gain_one, shift_one).astype(jnp.bfloat16)
    hidden = (convolve(surround(act_one), conv_one) + bias_one + time_shift).astype(jnp.bfloat16)
    partner_rows = from_partner(hidden, "cfg", 0)
    own_vals = hidden.astype(jnp.float32)
    far_vals = partner_rows.astype(jnp.float32)
    steered = own_vals + steer * jnp.where(is_cond, own_vals - far_vals, far_vals - own_vals)
    mean_part, square_part, count = local_moments(steered)
    seen = gathered(jnp.concatenate([mean_part, square_part], axis=1), "patch")
    mean_two, spread_two = combined(seen[:, :, :GROUPS], seen[:, :, GROUPS:], count)
    act_two = activate(steered, mean_two, spread_two, gain_two, shift_two).astype(jnp.bfloat16)
    image = convolve(surround(act_two), conv_two)
    block_out = (source + image + bias_two).astype(jnp.bfloat16)
    return block_out[None]


def solution(mesh):
    placed = (
        P("cfg", "req", "patch", None, None),
        P("req", None),
        P("req"),
        P(),
        P(),
        P(),
        P(),
        P("patch", None),
        P(),
        P(),
        P(),
        P(),
        P(),
    )
    return jax.shard_map(
        body,
        mesh=mesh,
        in_specs=placed,
        out_specs=P("cfg", "req", "patch", None, None),
        check_vma=False,
    )
```

```python
import functools

import jax
import jax.numpy as jnp
from jax import lax
from jax.experimental import pallas as pl
from jax.experimental.pallas import tpu as pltpu
from jax.sharding import PartitionSpec as P

GROUPS = 32
EPS = 1e-05
REACH = 2
LANES = 128
F32 = jnp.float32
BF16 = jnp.bfloat16


def padded_lanes(chans):
    return -(-chans // LANES) * LANES


def widen(row, wide):
    short = wide - row.shape[1]
    if not short:
        return row
    return jnp.concatenate([row, jnp.zeros((row.shape[0], short), row.dtype)], axis=1)


def same_group(wide, size):
    left = lax.broadcasted_iota(jnp.int32, (wide, wide), 0).astype(F32)
    right = lax.broadcasted_iota(jnp.int32, (wide, wide), 1).astype(F32)
    group = lambda at: jnp.floor((at + 0.5) * (1.0 / size))
    return jnp.where(group(left) == group(right), 1.0, 0.0).astype(BF16)


def group_sum(rows, mask):
    high = rows.astype(BF16).astype(F32)
    rest = rows - high
    middle = rest.astype(BF16).astype(F32)
    pieces = jnp.concatenate([high, middle, rest - middle, jnp.zeros_like(rows)], axis=0).astype(BF16)
    sums = jnp.dot(pieces, mask, preferred_element_type=F32)
    return sums[0:8] + sums[8:16] + sums[16:24]


def stack_rows(rows, wide):
    filler = [jnp.zeros((8 - len(rows), wide), F32)] if len(rows) < 8 else []
    return jnp.concatenate(list(rows) + filler, axis=0)


def group_stats(means, squares, count, mask, size):
    wide = mask.shape[0]
    peers = means[0].shape[0]
    mean_rows = [jnp.sum(m, axis=0, keepdims=True) * (1.0 / peers) for m in means]
    mean_rows = group_sum(stack_rows(mean_rows, wide), mask) * (1.0 / size)
    spread = []
    for k, (m, q) in enumerate(zip(means, squares)):
        off = m - mean_rows[k : k + 1]
        spread.append(jnp.sum(q + count * (off * off), axis=0, keepdims=True))
    var_rows = group_sum(stack_rows(spread, wide), mask) * (1.0 / (size * count * peers))
    return mean_rows, var_rows


def fold(values):
    total = values[:, :LANES]
    for at in range(LANES, values.shape[1], LANES):
        total = total + values[:, at : at + LANES]
    return total


def channel_moments(rows, chans):
    count = 0
    total = None
    for row in rows():
        part = fold(row)
        count += row.shape[1]
        total = part if total is None else total + part
    mean = jnp.sum(total, axis=1, keepdims=True) * (1.0 / count)
    squares = None
    for row in rows():
        off = row - mean
        part = fold(off * off)
        squares = part if squares is None else squares + part
    squares = jnp.sum(squares, axis=1, keepdims=True)
    lane = lax.broadcasted_iota(jnp.int32, (chans, LANES), 1)
    both = jnp.where(lane == 0, mean, jnp.where(lane == 1, squares, 0.0))
    wide = padded_lanes(chans)
    both = jnp.concatenate([both, jnp.zeros((wide - chans, LANES), F32)], axis=0)
    turned = both.T
    return turned[0:1], turned[1:2]


def put_rows(tile_rows, out_ref):
    peers, height, _ = out_ref.shape
    lines = [row[:, at : at + LANES] for row in tile_rows for at in range(0, row.shape[1], LANES)]
    if len(lines) < height:
        lines.append(jnp.zeros((height - len(lines), LANES), F32))
    tile = jnp.concatenate(lines, axis=0)
    out_ref[...] = jnp.broadcast_to(tile[None], out_ref.shape)


def get_rows(seen_ref, first, peers, which, wide):
    lines = wide // LANES
    return jnp.concatenate(
        [seen_ref[pl.ds(first, peers), which * lines + k, :] for k in range(lines)], axis=1
    )


def stats_kernel(lat_ref, embed_ref, weight_ref, out_ref):
    rows, chans, _ = lat_ref.shape
    wide = padded_lanes(chans)
    mean, squares = channel_moments(lambda: (lat_ref[k].astype(F32) for k in range(rows)), chans)
    own = weight_ref.shape[0]
    length = embed_ref.shape[1]
    embed = jnp.broadcast_to(embed_ref[...].astype(F32), (8, length))
    embed = pltpu.roll(embed, length - lax.axis_index("patch") * own, 1)[:, :own]
    act = (embed / (1.0 + jnp.exp(-embed))).astype(BF16)
    time_part = jnp.dot(act, weight_ref[...], preferred_element_type=F32)[0:1]
    put_rows([mean, squares, widen(time_part, wide)], out_ref)


def turn_kernel(one_ref, two_ref, one_out, two_out):
    for source, target in ((one_ref, one_out), (two_ref, two_out)):
        deep = source.shape[0]
        step = 320 if deep % 320 == 0 else deep
        step = 2 * step if deep % (2 * step) == 0 else step
        for at in range(0, deep, 640):
            target[:, at : min(at + 640, deep)] = source[at : min(at + 640, deep), :].T


def spread_columns(rows, chans, cols_ref):
    turned = stack_rows(rows, rows[0].shape[1]).T
    for k in range(len(rows)):
        cols_ref[k] = jnp.broadcast_to(turned[:chans, k : k + 1], (chans, LANES))


def half_act(values, mean, scale, shift):
    half = (values - mean) * scale + shift
    return half * jnp.tanh(half) + half


def twice(column):
    return jnp.concatenate([column, column], axis=1)


def put_taps(taps_ref, at, row):
    chans, cols = row.shape
    lane = lax.broadcasted_iota(jnp.int32, (chans, cols), 1)
    before = jnp.where(lane == 0, 0.0, pltpu.roll(row, 1, 1))
    after = jnp.where(lane == cols - 1, 0.0, pltpu.roll(row, cols - 1, 1))
    for k, value in enumerate((before, row, after)):
        taps_ref[pl.ds((at * 3 + k) * chans, chans), :] = value.astype(BF16)


def edge_keep(at, rows, reach):
    patch, patches = lax.axis_index("patch"), lax.axis_size("patch")
    if at < reach:
        return jnp.where(patch == 0, 0.0, 1.0).astype(F32)
    if at >= reach + rows:
        return jnp.where(patch == patches - 1, 0.0, 1.0).astype(F32)
    return None


def first_kernel(
    own_ref, far_ref, near_ref, next_ref, far_near_ref, far_next_ref, seen_ref, steer_ref,
    gain_ref, shift_ref, bias_ref, time_bias_ref, weight_hbm,
    steered_ref, out_ref,
    weight_ref, taps_ref, cols_ref, edge_ref, sem,
):
    copy = pltpu.make_async_copy(weight_hbm, weight_ref, sem)
    copy.start()
    rows, chans, cols = own_ref.shape
    reach = near_ref.shape[0]
    wide = padded_lanes(chans)
    size = chans // GROUPS
    cfg, patches = lax.axis_index("cfg"), lax.axis_size("patch")
    even = lax.rem(lax.axis_index("patch"), 2) == 0
    mask = same_group(wide, size)
    peers = patches
    starts = (cfg * peers, (1 - cfg) * peers)
    means = [get_rows(seen_ref, s, peers, 0, wide) for s in starts]
    squares = [get_rows(seen_ref, s, peers, 1, wide) for s in starts]
    mean_rows, var_rows = group_stats(means, squares, float(rows * cols), mask, size)
    scale_rows = lax.rsqrt(var_rows + EPS) * (0.5 * widen(gain_ref[...], wide))
    times = jnp.sum(get_rows(seen_ref, 0, peers, 2, wide), axis=0, keepdims=True)
    added = times + widen(time_bias_ref[...] + bias_ref[...], wide)
    spread_columns(
        [mean_rows[0:1], scale_rows[0:1], mean_rows[1:2], scale_rows[1:2],
         0.5 * widen(shift_ref[...], wide), added],
        chans, cols_ref,
    )
    above = jnp.where(even, reach, 0)
    edge_ref[0, pl.ds(reach - above, reach)] = near_ref[...]
    edge_ref[0, pl.ds(above, reach)] = next_ref[...]
    edge_ref[1, pl.ds(reach - above, reach)] = far_near_ref[...]
    edge_ref[1, pl.ds(above, reach)] = far_next_ref[...]
    sign = jnp.where(cfg == 0, 1.0, -1.0).astype(F32) * steer_ref[0]

    def inputs(at):
        if at < reach:
            return edge_ref[0, reach + at], edge_ref[1, reach + at]
        if at >= reach + rows:
            return edge_ref[0, at - reach - rows], edge_ref[1, at - reach - rows]
        return own_ref[at - reach], far_ref[at - reach]

    for at in range(rows + 2 * reach):
        mine, other = inputs(at)
        shift = twice(cols_ref[4])
        mine = half_act(mine.astype(F32), twice(cols_ref[0]), twice(cols_ref[1]), shift)
        other = half_act(other.astype(F32), twice(cols_ref[2]), twice(cols_ref[3]), shift)
        mixed = mine + sign * (mine - other)
        keep = edge_keep(at, rows, reach)
        put_taps(taps_ref, at, mixed if keep is None else mixed * keep)
    copy.wait()
    deep = 9 * chans
    for at in range(rows + 2 * reach - 2):
        total = jnp.dot(
            weight_ref[...], taps_ref[pl.ds(at * 3 * chans, deep), :], preferred_element_type=F32
        )
        steered_ref[at] = total + twice(cols_ref[5])
    skip = reach - 1
    mean, square = channel_moments(lambda: (steered_ref[skip + k] for k in range(rows)), chans)
    put_rows([mean, square], out_ref)


def second_kernel(
    steered_ref, lat_ref, seen_ref, gain_ref, shift_ref, bias_ref, weight_hbm,
    out_ref,
    weight_ref, taps_ref, cols_ref, sem,
):
    copy = pltpu.make_async_copy(weight_hbm, weight_ref, sem)
    copy.start()
    rows, chans, cols = lat_ref.shape
    wide = padded_lanes(chans)
    size = chans // GROUPS
    peers = lax.axis_size("patch")
    mask = same_group(wide, size)
    mean_rows, var_rows = group_stats(
        [get_rows(seen_ref, 0, peers, 0, wide)], [get_rows(seen_ref, 0, peers, 1, wide)],
        float(rows * cols), mask, size,
    )
    scale_rows = lax.rsqrt(var_rows + EPS) * (0.5 * widen(gain_ref[...], wide))
    spread_columns(
        [mean_rows[0:1], scale_rows[0:1], 0.5 * widen(shift_ref[...], wide), widen(bias_ref[...], wide)],
        chans, cols_ref,
    )
    for at in range(rows + 2):
        value = half_act(steered_ref[at], twice(cols_ref[0]), twice(cols_ref[1]), twice(cols_ref[2]))
        keep = edge_keep(at, rows, 1)
        put_taps(taps_ref, at, value if keep is None else value * keep)
    copy.wait()
    deep = 9 * chans
    for at in range(rows):
        total = jnp.dot(
            weight_ref[...], taps_ref[pl.ds(at * 3 * chans, deep), :], preferred_element_type=F32
        )
        out_ref[at] = (lat_ref[at].astype(F32) + (total + twice(cols_ref[3]))).astype(BF16)


def everyone(tiles, axes):
    return lax.all_to_all(tiles, axes, 0, 0)


VMEM = pl.BlockSpec(memory_space=pltpu.VMEM)
SMEM = pl.BlockSpec(memory_space=pltpu.SMEM)
ANY = pl.BlockSpec(memory_space=pl.ANY)
LIMIT = pltpu.CompilerParams(vmem_limit_bytes=48 * 1024 * 1024)


def body(
    latents, time_embed, steer_scale, gain_one, shift_one, conv_one, bias_one,
    time_weight, time_bias, gain_two, shift_two, conv_two, bias_two,
):
    own = jnp.swapaxes(latents[0, 0], 1, 2)
    rows, chans, cols = own.shape
    wide = padded_lanes(chans)
    deep = 9 * chans
    patches = lax.axis_size("patch")
    even = lax.rem(lax.axis_index("patch"), 2) == 0
    near_edge = lax.dynamic_slice_in_dim(own, jnp.where(even, rows - REACH, 0), REACH, 0)
    next_edge = lax.dynamic_slice_in_dim(own, jnp.where(even, 0, rows - REACH), REACH, 0)
    near = lax.ppermute(near_edge, "patch", [(i, i ^ 1) for i in range(patches)])
    steps = [(i, i + 1) for i in range(1, patches - 1, 2)]
    following = lax.ppermute(next_edge, "patch", steps + [(j, i) for i, j in steps])
    swap = [(0, 1), (1, 0)]
    far = lax.ppermute(own, "cfg", swap)
    far_near = lax.ppermute(near, "cfg", swap)
    far_next = lax.ppermute(following, "cfg", swap)
    line = lambda vector: vector.reshape(1, chans)

    tile_one = -(-3 * wide // LANES // 8) * 8
    sent = pl.pallas_call(
        stats_kernel,
        out_shape=jax.ShapeDtypeStruct((2 * patches, tile_one, LANES), F32),
        in_specs=[VMEM] * 3,
        out_specs=VMEM,
        compiler_params=LIMIT,
        name="stats",
    )(own, time_embed, time_weight)
    seen = everyone(sent, ("cfg", "patch"))

    turned_one, turned_two = pl.pallas_call(
        turn_kernel,
        out_shape=[jax.ShapeDtypeStruct((chans, deep), BF16)] * 2,
        in_specs=[VMEM] * 2,
        out_specs=[VMEM] * 2,
        compiler_params=LIMIT,
        name="turn",
    )(conv_one.reshape(deep, chans), conv_two.reshape(deep, chans))

    tile_two = -(-2 * wide // LANES // 8) * 8
    inside = rows + 2 * REACH - 2
    steered, sent = pl.pallas_call(
        first_kernel,
        out_shape=[
            jax.ShapeDtypeStruct((inside, chans, cols), F32),
            jax.ShapeDtypeStruct((patches, tile_two, LANES), F32),
        ],
        in_specs=[VMEM] * 7 + [SMEM] + [VMEM] * 4 + [ANY],
        out_specs=[VMEM] * 2,
        scratch_shapes=[
            pltpu.VMEM((chans, deep), BF16),
            pltpu.VMEM(((rows + 2 * REACH) * 3 * chans, cols), BF16),
            pltpu.VMEM((6, chans, LANES), F32),
            pltpu.VMEM((2, 2 * REACH, chans, cols), BF16),
            pltpu.SemaphoreType.DMA,
        ],
        compiler_params=LIMIT,
        name="first",
    )(
        own, far, near, following, far_near, far_next, seen, steer_scale,
        line(gain_one), line(shift_one), line(bias_one), line(time_bias), turned_one,
    )
    seen = everyone(sent, "patch")
    image = pl.pallas_call(
        second_kernel,
        out_shape=jax.ShapeDtypeStruct((rows, chans, cols), BF16),
        in_specs=[VMEM] * 6 + [ANY],
        out_specs=VMEM,
        scratch_shapes=[
            pltpu.VMEM((chans, deep), BF16),
            pltpu.VMEM(((rows + 2) * 3 * chans, cols), BF16),
            pltpu.VMEM((4, chans, LANES), F32),
            pltpu.SemaphoreType.DMA,
        ],
        compiler_params=LIMIT,
        name="second",
    )(steered, own, seen, line(gain_two), line(shift_two), line(bias_two), turned_two)
    return jnp.swapaxes(image, 1, 2)[None, None]


def solution(mesh):
    placed = (
        P("cfg", "req", "patch", None, None), P("req", None), P("req"), P(), P(), P(), P(),
        P("patch", None), P(), P(), P(), P(), P(),
    )
    return jax.shard_map(
        body,
        mesh=mesh,
        in_specs=placed,
        out_specs=P("cfg", "req", "patch", None, None),
        check_vma=False,
    )
```

```python
import functools

import jax
import jax.numpy as jnp
from jax import lax
from jax.experimental import pallas as pl
from jax.experimental.pallas import tpu as pltpu
from jax.sharding import PartitionSpec as P

GROUPS = 32
EPS = 1e-05
REACH = 2
LANES = 128
F32 = jnp.float32
BF16 = jnp.bfloat16


def padded_lanes(chans):
    return -(-chans // LANES) * LANES


def widen(row, wide):
    short = wide - row.shape[1]
    if not short:
        return row
    return jnp.concatenate([row, jnp.zeros((row.shape[0], short), row.dtype)], axis=1)


def same_group(wide, size):
    left = lax.broadcasted_iota(jnp.int32, (wide, wide), 0).astype(F32)
    right = lax.broadcasted_iota(jnp.int32, (wide, wide), 1).astype(F32)
    group = lambda at: jnp.floor((at + 0.5) * (1.0 / size))
    return jnp.where(group(left) == group(right), 1.0, 0.0).astype(BF16)


def group_sum(rows, mask):
    high = rows.astype(BF16).astype(F32)
    rest = rows - high
    middle = rest.astype(BF16).astype(F32)
    pieces = jnp.concatenate([high, middle, rest - middle, jnp.zeros_like(rows)], axis=0).astype(BF16)
    sums = jnp.dot(pieces, mask, preferred_element_type=F32)
    return sums[0:8] + sums[8:16] + sums[16:24]


def stack_rows(rows, wide):
    filler = [jnp.zeros((8 - len(rows), wide), F32)] if len(rows) < 8 else []
    return jnp.concatenate(list(rows) + filler, axis=0)


def group_stats(means, squares, count, mask, size):
    wide = mask.shape[0]
    peers = means[0].shape[0]
    mean_rows = [jnp.sum(m, axis=0, keepdims=True) * (1.0 / peers) for m in means]
    mean_rows = group_sum(stack_rows(mean_rows, wide), mask) * (1.0 / size)
    spread = []
    for k, (m, q) in enumerate(zip(means, squares)):
        off = m - mean_rows[k : k + 1]
        spread.append(jnp.sum(q + count * (off * off), axis=0, keepdims=True))
    var_rows = group_sum(stack_rows(spread, wide), mask) * (1.0 / (size * count * peers))
    return mean_rows, var_rows


def fold(values):
    total = values[:, :LANES]
    for at in range(LANES, values.shape[1], LANES):
        total = total + values[:, at : at + LANES]
    return total


def channel_moments(rows, chans):
    count = 0
    total = None
    for row in rows():
        part = fold(row)
        count += row.shape[1]
        total = part if total is None else total + part
    mean = jnp.sum(total, axis=1, keepdims=True) * (1.0 / count)
    squares = None
    for row in rows():
        off = row - mean
        part = fold(off * off)
        squares = part if squares is None else squares + part
    squares = jnp.sum(squares, axis=1, keepdims=True)
    lane = lax.broadcasted_iota(jnp.int32, (chans, LANES), 1)
    both = jnp.where(lane == 0, mean, jnp.where(lane == 1, squares, 0.0))
    wide = padded_lanes(chans)
    both = jnp.concatenate([both, jnp.zeros((wide - chans, LANES), F32)], axis=0)
    turned = both.T
    return turned[0:1], turned[1:2]


def put_rows(tile_rows, out_ref):
    peers, height, _ = out_ref.shape
    lines = [row[:, at : at + LANES] for row in tile_rows for at in range(0, row.shape[1], LANES)]
    if len(lines) < height:
        lines.append(jnp.zeros((height - len(lines), LANES), F32))
    tile = jnp.concatenate(lines, axis=0)
    out_ref[...] = jnp.broadcast_to(tile[None], out_ref.shape)


def get_rows(seen_ref, first, peers, which, wide):
    lines = wide // LANES
    return jnp.concatenate(
        [seen_ref[pl.ds(first, peers), which * lines + k, :] for k in range(lines)], axis=1
    )


def stats_kernel(lat_hbm, embed_hbm, weight_hbm, lat_ref, out_ref, embed_ref, weight_ref, sems):
    rows, chans, _ = lat_ref.shape
    copies = [
        pltpu.make_async_copy(lat_hbm.at[k], lat_ref.at[k], sems.at[k]) for k in range(rows)
    ]
    copies.append(pltpu.make_async_copy(embed_hbm, embed_ref, sems.at[rows]))
    copies.append(pltpu.make_async_copy(weight_hbm, weight_ref, sems.at[rows + 1]))
    for copy in copies:
        copy.start()
    waits = list(copies[:rows])

    def values():
        for k in range(rows):
            if waits:
                waits.pop(0).wait()
            yield lat_ref[k].astype(F32)

    wide = padded_lanes(chans)
    mean, squares = channel_moments(values, chans)
    copies[rows].wait()
    copies[rows + 1].wait()
    own = weight_ref.shape[0]
    length = embed_ref.shape[1]
    embed = jnp.broadcast_to(embed_ref[...].astype(F32), (8, length))
    embed = pltpu.roll(embed, length - lax.axis_index("patch") * own, 1)[:, :own]
    act = (embed / (1.0 + jnp.exp(-embed))).astype(BF16)
    time_part = jnp.dot(act, weight_ref[...], preferred_element_type=F32)[0:1]
    put_rows([mean, squares, widen(time_part, wide)], out_ref)


PARTS = 3


def prepare_kernel(
    one_hbm, two_hbm, gain_one, shift_one, bias_one, time_bias, gain_two, shift_two, bias_two, steer,
    one_out, two_out, rows_ref, one_ref, two_ref, sems,
):
    deep = one_ref.shape[0]
    part = deep // PARTS
    jobs = []
    for k, (source, held, target) in enumerate(((one_hbm, one_ref, one_out), (two_hbm, two_ref, two_out))):
        for at in range(PARTS):
            here = pl.ds(at * part, part)
            copy = pltpu.make_async_copy(source.at[here], held.at[here], sems.at[k * PARTS + at])
            copy.start()
            jobs.append((copy, held, target, at * part))
    wide = rows_ref.shape[1]
    vectors = (gain_one, shift_one, bias_one, time_bias, gain_two, shift_two, bias_two)
    lines = [widen(v[...], wide) for v in vectors]
    rows_ref[...] = jnp.concatenate(lines + [jnp.broadcast_to(steer[...], (1, wide))], axis=0)
    for copy, held, target, at in jobs:
        copy.wait()
        target[:, at : at + part] = held[at : at + part, :].T


def spread_columns(rows, chans, cols_ref):
    turned = stack_rows(rows, rows[0].shape[1]).T
    for k in range(len(rows)):
        cols_ref[k] = jnp.broadcast_to(turned[:chans, k : k + 1], (chans, LANES))


def half_act(values, mean, scale, shift):
    half = (values - mean) * scale + shift
    return half * jnp.tanh(half) + half


def twice(column):
    return jnp.concatenate([column, column], axis=1)


def put_taps(taps_ref, at, row):
    chans, cols = row.shape
    lane = lax.broadcasted_iota(jnp.int32, (chans, cols), 1)
    before = jnp.where(lane == 0, 0.0, pltpu.roll(row, 1, 1))
    after = jnp.where(lane == cols - 1, 0.0, pltpu.roll(row, cols - 1, 1))
    for k, value in enumerate((before, row, after)):
        taps_ref[pl.ds((at * 3 + k) * chans, chans), :] = value.astype(BF16)


def edge_keep(at, rows, reach):
    patch, patches = lax.axis_index("patch"), lax.axis_size("patch")
    if at < reach:
        return jnp.where(patch == 0, 0.0, 1.0).astype(F32)
    if at >= reach + rows:
        return jnp.where(patch == patches - 1, 0.0, 1.0).astype(F32)
    return None


def mixer(cols_ref, rows_ref, chans):
    sign = jnp.where(lax.axis_index("cfg") == 0, 1.0, -1.0).astype(F32)
    steer = rows_ref[7:8, 0:1] * sign

    def mix(mine, other):
        shift = twice(cols_ref[4])
        mine = half_act(mine.astype(F32), twice(cols_ref[0]), twice(cols_ref[1]), shift)
        other = half_act(other.astype(F32), twice(cols_ref[2]), twice(cols_ref[3]), shift)
        return mine + steer * (mine - other)

    return mix


def matmul(weight_ref, taps, first_tap):
    depth = taps.shape[0]
    start = first_tap * (weight_ref.shape[1] // 3)
    return jnp.dot(weight_ref[:, start : start + depth], taps, preferred_element_type=F32)


def inner_kernel(
    own_ref, far_ref, seen_ref, rows_ref, weight_ref,
    steered_ref, taps_ref, cols_ref,
):
    rows, chans, cols = own_ref.shape
    wide = padded_lanes(chans)
    size = chans // GROUPS
    cfg, peers = lax.axis_index("cfg"), lax.axis_size("patch")
    mask = same_group(wide, size)
    starts = (cfg * peers, (1 - cfg) * peers)
    means = [get_rows(seen_ref, s, peers, 0, wide) for s in starts]
    squares = [get_rows(seen_ref, s, peers, 1, wide) for s in starts]
    mean_rows, var_rows = group_stats(means, squares, float(rows * cols), mask, size)
    scale_rows = lax.rsqrt(var_rows + EPS) * (0.5 * rows_ref[0:1])
    times = jnp.sum(get_rows(seen_ref, 0, peers, 2, wide), axis=0, keepdims=True)
    added = times + (rows_ref[3:4] + rows_ref[2:3])
    spread_columns(
        [mean_rows[0:1], scale_rows[0:1], mean_rows[1:2], scale_rows[1:2], 0.5 * rows_ref[1:2], added],
        chans, cols_ref,
    )
    mix = mixer(cols_ref, rows_ref, chans)
    line = 3 * chans
    if rows < 3:
        steered_ref[...] = jnp.zeros_like(steered_ref)
    for at in range(rows):
        put_taps(taps_ref, at, mix(own_ref[at], far_ref[at]))
        if at >= 2:
            total = matmul(weight_ref, taps_ref[(at - 2) * line : (at + 1) * line, :], 0)
            steered_ref[at - 2] = total + twice(cols_ref[5])


def outer_kernel(
    near_ref, next_ref, far_near_ref, far_next_ref, inner_ref, inner_taps_ref, cols_ref, rows_ref, weight_ref,
    steered_ref, out_ref,
    taps_ref, edge_ref,
):
    reach, chans, cols = near_ref.shape
    line = 3 * chans
    rows = inner_taps_ref.shape[0] // line
    above = jnp.where(lax.rem(lax.axis_index("patch"), 2) == 0, reach, 0)
    edge_ref[0, pl.ds(above, reach)] = next_ref[...]
    edge_ref[1, pl.ds(above, reach)] = far_next_ref[...]
    edge_ref[0, pl.ds(reach - above, reach)] = near_ref[...]
    edge_ref[1, pl.ds(reach - above, reach)] = far_near_ref[...]
    mix = mixer(cols_ref, rows_ref, chans)

    def taps(at):
        if reach <= at < reach + rows:
            return inner_taps_ref, at - reach
        return taps_ref, at if at < reach else at - rows

    def rows_of(first, count):
        ref, at = taps(first)
        return ref[at * line : (at + count) * line, :]

    def conv(at):
        total, tap = None, 0
        while tap < 3:
            ref, _ = taps(at + tap)
            count = 1
            while tap + count < 3 and taps(at + tap + count)[0] is ref:
                count += 1
            part = matmul(weight_ref, rows_of(at + tap, count), tap)
            total = part if total is None else total + part
            tap += count
        return total

    def enter(at):
        k = reach + at if at < reach else at - reach - rows
        keep = edge_keep(at, rows, reach)
        put_taps(taps_ref, taps(at)[1], mix(edge_ref[0, k], edge_ref[1, k]) * keep)

    for at in range(reach):
        enter(at)
    outside = [at for at in range(rows + 2 * reach - 2) if not reach <= at < reach + rows - 2]
    place = {at: k for k, at in enumerate(outside)}
    ready = reach + rows
    for at in outside:
        while ready < at + 3:
            enter(ready)
            ready += 1
        steered_ref[place[at]] = conv(at) + twice(cols_ref[5])

    def own_rows():
        for k in range(rows):
            at = reach - 1 + k
            yield steered_ref[place[at]] if at in place else inner_ref[at - reach]

    mean, square = channel_moments(own_rows, chans)
    put_rows([mean, square], out_ref)


def second_kernel(
    inner_ref, outer_ref, lat_ref, seen_ref, rows_ref, weight_ref,
    out_ref,
    taps_ref, cols_ref,
):
    rows, chans, cols = lat_ref.shape
    wide = padded_lanes(chans)
    size = chans // GROUPS
    peers = lax.axis_size("patch")
    mask = same_group(wide, size)
    mean_rows, var_rows = group_stats(
        [get_rows(seen_ref, 0, peers, 0, wide)], [get_rows(seen_ref, 0, peers, 1, wide)],
        float(rows * cols), mask, size,
    )
    scale_rows = lax.rsqrt(var_rows + EPS) * (0.5 * rows_ref[4:5])
    spread_columns(
        [mean_rows[0:1], scale_rows[0:1], 0.5 * rows_ref[5:6], rows_ref[6:7]], chans, cols_ref
    )
    line = 3 * chans
    inside = max(rows - 2, 0)
    half = outer_ref.shape[0] // 2
    for at in range(rows + 2):
        if half <= at < half + inside:
            value = inner_ref[at - half]
        else:
            value = outer_ref[at if at < half else at - inside]
        value = half_act(value, twice(cols_ref[0]), twice(cols_ref[1]), twice(cols_ref[2]))
        keep = edge_keep(at, rows, 1)
        put_taps(taps_ref, at, value if keep is None else value * keep)
        if at >= 2:
            total = matmul(weight_ref, taps_ref[(at - 2) * line : (at + 1) * line, :], 0)
            out_ref[at - 2] = (lat_ref[at - 2].astype(F32) + (total + twice(cols_ref[3]))).astype(BF16)


def everyone(tiles, axes):
    return lax.all_to_all(tiles, axes, 0, 0)


VMEM = pl.BlockSpec(memory_space=pltpu.VMEM)
ANY = pl.BlockSpec(memory_space=pl.ANY)
LIMIT = pltpu.CompilerParams(vmem_limit_bytes=12 * 1024 * 1024)


def in_hbm(value):
    return pltpu.with_memory_space_constraint(value, pltpu.HBM)


def body(
    latents, time_embed, steer_scale, gain_one, shift_one, conv_one, bias_one,
    time_weight, time_bias, gain_two, shift_two, conv_two, bias_two,
):
    own = jnp.swapaxes(latents[0, 0], 1, 2)
    rows, chans, cols = own.shape
    wide = padded_lanes(chans)
    deep = 9 * chans
    patches = lax.axis_size("patch")
    even = lax.rem(lax.axis_index("patch"), 2) == 0
    near_edge = lax.dynamic_slice_in_dim(own, jnp.where(even, rows - REACH, 0), REACH, 0)
    next_edge = lax.dynamic_slice_in_dim(own, jnp.where(even, 0, rows - REACH), REACH, 0)
    near = lax.ppermute(near_edge, "patch", [(i, i ^ 1) for i in range(patches)])
    steps = [(i, i + 1) for i in range(1, patches - 1, 2)]
    following = lax.ppermute(next_edge, "patch", steps + [(j, i) for i, j in steps])
    swap = [(0, 1), (1, 0)]
    far = lax.ppermute(own, "cfg", swap)
    line = lambda vector: vector.reshape(1, -1)

    tile_one = -(-3 * wide // LANES // 8) * 8
    held, sent = pl.pallas_call(
        stats_kernel,
        out_shape=[
            pltpu.VMEM((rows, chans, cols), BF16),
            pltpu.VMEM((2 * patches, tile_one, LANES), F32),
        ],
        in_specs=[ANY] * 3,
        out_specs=[VMEM] * 2,
        scratch_shapes=[
            pltpu.VMEM(time_embed.shape, BF16),
            pltpu.VMEM(time_weight.shape, BF16),
            pltpu.SemaphoreType.DMA((rows + 2,)),
        ],
        compiler_params=LIMIT,
        name="stats",
    )(in_hbm(own), in_hbm(time_embed), in_hbm(time_weight))
    seen = everyone(sent, ("cfg", "patch"))

    weights = (conv_one.reshape(deep, chans), conv_two.reshape(deep, chans))
    *weights, _ = lax.optimization_barrier((*weights, sent))
    turned_one, turned_two, vectors = pl.pallas_call(
        prepare_kernel,
        out_shape=[pltpu.VMEM((chans, deep), BF16)] * 2 + [pltpu.VMEM((8, wide), F32)],
        in_specs=[ANY] * 2 + [VMEM] * 8,
        out_specs=[VMEM] * 3,
        scratch_shapes=[pltpu.VMEM((deep, chans), BF16)] * 2 + [pltpu.SemaphoreType.DMA((2 * PARTS,))],
        compiler_params=LIMIT,
        name="prepare",
    )(
        in_hbm(weights[0]), in_hbm(weights[1]), line(gain_one), line(shift_one), line(bias_one),
        line(time_bias), line(gain_two), line(shift_two), line(bias_two), line(steer_scale),
    )
    near, following, vectors, seen = lax.optimization_barrier((near, following, vectors, seen))
    far_near = lax.ppermute(near, "cfg", swap)
    far_next = lax.ppermute(following, "cfg", swap)

    inner, taps, columns = pl.pallas_call(
        inner_kernel,
        out_shape=[
            pltpu.VMEM((max(rows - 2, 1), chans, cols), F32),
            pltpu.VMEM((rows * 3 * chans, cols), BF16),
            pltpu.VMEM((6, chans, LANES), F32),
        ],
        in_specs=[VMEM] * 5,
        out_specs=[VMEM] * 3,
        compiler_params=LIMIT,
        name="inner",
    )(held, far, seen, vectors, turned_one)
    tile_two = -(-2 * wide // LANES // 8) * 8
    outer, sent = pl.pallas_call(
        outer_kernel,
        out_shape=[
            pltpu.VMEM((2 * REACH, chans, cols), F32),
            pltpu.VMEM((patches, tile_two, LANES), F32),
        ],
        in_specs=[VMEM] * 9,
        out_specs=[VMEM] * 2,
        scratch_shapes=[
            pltpu.VMEM((2 * REACH * 3 * chans, cols), BF16),
            pltpu.VMEM((2, 2 * REACH, chans, cols), BF16),
        ],
        compiler_params=LIMIT,
        name="outer",
    )(near, following, far_near, far_next, inner, taps, columns, vectors, turned_one)
    seen = everyone(sent, "patch")
    image = pl.pallas_call(
        second_kernel,
        out_shape=jax.ShapeDtypeStruct((rows, chans, cols), BF16),
        in_specs=[VMEM] * 6,
        out_specs=VMEM,
        scratch_shapes=[
            pltpu.VMEM(((rows + 2) * 3 * chans, cols), BF16),
            pltpu.VMEM((4, chans, LANES), F32),
        ],
        compiler_params=LIMIT,
        name="second",
    )(inner, outer, held, seen, vectors, turned_two)
    return jnp.swapaxes(image, 1, 2)[None, None]


def solution(mesh):
    placed = (
        P("cfg", "req", "patch", None, None), P("req", None), P("req"), P(), P(), P(), P(),
        P("patch", None), P(), P(), P(), P(), P(),
    )
    return jax.shard_map(
        body,
        mesh=mesh,
        in_specs=placed,
        out_specs=P("cfg", "req", "patch", None, None),
        check_vma=False,
    )
```

```python
import functools

import jax
import jax.numpy as jnp
from jax import lax
from jax.experimental import pallas as pl
from jax.experimental.pallas import tpu as pltpu
from jax.sharding import PartitionSpec as P

GROUPS = 32
EPS = 1e-05
REACH = 2
LANES = 128
F32 = jnp.float32
BF16 = jnp.bfloat16


def padded_lanes(chans):
    return -(-chans // LANES) * LANES


def widen(row, wide):
    short = wide - row.shape[1]
    if not short:
        return row
    return jnp.concatenate([row, jnp.zeros((row.shape[0], short), row.dtype)], axis=1)


def same_group(wide, size):
    left = lax.broadcasted_iota(jnp.int32, (wide, wide), 0).astype(F32)
    right = lax.broadcasted_iota(jnp.int32, (wide, wide), 1).astype(F32)
    group = lambda at: jnp.floor((at + 0.5) * (1.0 / size))
    return jnp.where(group(left) == group(right), 1.0, 0.0).astype(BF16)


def group_sum(rows, mask):
    high = rows.astype(BF16).astype(F32)
    rest = rows - high
    middle = rest.astype(BF16).astype(F32)
    pieces = jnp.concatenate([high, middle, rest - middle, jnp.zeros_like(rows)], axis=0).astype(BF16)
    sums = jnp.dot(pieces, mask, preferred_element_type=F32)
    return sums[0:8] + sums[8:16] + sums[16:24]


def stack_rows(rows, wide):
    filler = [jnp.zeros((8 - len(rows), wide), F32)] if len(rows) < 8 else []
    return jnp.concatenate(list(rows) + filler, axis=0)


def group_stats(means, squares, count, mask, size):
    wide = mask.shape[0]
    peers = means[0].shape[0]
    mean_rows = [jnp.sum(m, axis=0, keepdims=True) * (1.0 / peers) for m in means]
    mean_rows = group_sum(stack_rows(mean_rows, wide), mask) * (1.0 / size)
    spread = []
    for k, (m, q) in enumerate(zip(means, squares)):
        off = m - mean_rows[k : k + 1]
        spread.append(jnp.sum(q + count * (off * off), axis=0, keepdims=True))
    var_rows = group_sum(stack_rows(spread, wide), mask) * (1.0 / (size * count * peers))
    return mean_rows, var_rows


def fold(values):
    total = values[:, :LANES]
    for at in range(LANES, values.shape[1], LANES):
        total = total + values[:, at : at + LANES]
    return total


def channel_moments(rows, chans):
    count = 0
    total = None
    for row in rows():
        part = fold(row)
        count += row.shape[1]
        total = part if total is None else total + part
    mean = jnp.sum(total, axis=1, keepdims=True) * (1.0 / count)
    squares = None
    for row in rows():
        off = row - mean
        part = fold(off * off)
        squares = part if squares is None else squares + part
    squares = jnp.sum(squares, axis=1, keepdims=True)
    lane = lax.broadcasted_iota(jnp.int32, (chans, LANES), 1)
    both = jnp.where(lane == 0, mean, jnp.where(lane == 1, squares, 0.0))
    wide = padded_lanes(chans)
    both = jnp.concatenate([both, jnp.zeros((wide - chans, LANES), F32)], axis=0)
    turned = both.T
    return turned[0:1], turned[1:2]


def put_rows(tile_rows, out_ref):
    peers, height, _ = out_ref.shape
    lines = [row[:, at : at + LANES] for row in tile_rows for at in range(0, row.shape[1], LANES)]
    if len(lines) < height:
        lines.append(jnp.zeros((height - len(lines), LANES), F32))
    tile = jnp.concatenate(lines, axis=0)
    out_ref[...] = jnp.broadcast_to(tile[None], out_ref.shape)


def get_rows(seen_ref, first, peers, which, wide):
    lines = wide // LANES
    return jnp.concatenate(
        [seen_ref[pl.ds(first, peers), which * lines + k, :] for k in range(lines)], axis=1
    )


def stats_kernel(lat_hbm, embed_hbm, weight_hbm, lat_ref, out_ref, embed_ref, weight_ref, sems):
    rows, chans, _ = lat_ref.shape
    copies = [
        pltpu.make_async_copy(lat_hbm.at[k], lat_ref.at[k], sems.at[k]) for k in range(rows)
    ]
    copies.append(pltpu.make_async_copy(embed_hbm, embed_ref, sems.at[rows]))
    copies.append(pltpu.make_async_copy(weight_hbm, weight_ref, sems.at[rows + 1]))
    for copy in copies:
        copy.start()
    waits = list(copies[:rows])

    def values():
        for k in range(rows):
            if waits:
                waits.pop(0).wait()
            yield lat_ref[k].astype(F32)

    wide = padded_lanes(chans)
    mean, squares = channel_moments(values, chans)
    copies[rows].wait()
    copies[rows + 1].wait()
    own = weight_ref.shape[0]
    length = embed_ref.shape[1]
    embed = jnp.broadcast_to(embed_ref[...].astype(F32), (8, length))
    embed = pltpu.roll(embed, length - lax.axis_index("patch") * own, 1)[:, :own]
    act = (embed / (1.0 + jnp.exp(-embed))).astype(BF16)
    time_part = jnp.dot(act, weight_ref[...], preferred_element_type=F32)[0:1]
    put_rows([mean, squares, widen(time_part, wide)], out_ref)


PARTS = 3


def edges_kernel(lat_hbm, near_ref, next_ref, sems):
    reach = near_ref.shape[0]
    last = lat_hbm.shape[0] - reach
    near_at = jnp.where(lax.rem(lax.axis_index("patch"), 2) == 0, last, 0)
    copies = [
        pltpu.make_async_copy(lat_hbm.at[pl.ds(near_at, reach)], near_ref, sems.at[0]),
        pltpu.make_async_copy(lat_hbm.at[pl.ds(last - near_at, reach)], next_ref, sems.at[1]),
    ]
    for copy in copies:
        copy.start()
    for copy in copies:
        copy.wait()


def turn(source, held, target, sems):
    part = held.shape[0] // PARTS
    jobs = []
    for k in range(PARTS):
        here = pl.ds(k * part, part)
        copy = pltpu.make_async_copy(source.at[here], held.at[here], sems.at[k])
        copy.start()
        jobs.append((copy, k * part))

    def finish():
        for copy, at in jobs:
            copy.wait()
            target[:, at : at + part] = held[at : at + part, :].T

    return finish


def prepare_kernel(
    weight_hbm, gain_one, shift_one, bias_one, time_bias, gain_two, shift_two, bias_two, steer,
    out_ref, rows_ref, held_ref, sems,
):
    finish = turn(weight_hbm, held_ref, out_ref, sems)
    wide = rows_ref.shape[1]
    vectors = (gain_one, shift_one, bias_one, time_bias, gain_two, shift_two, bias_two)
    lines = [widen(v[...], wide) for v in vectors]
    rows_ref[...] = jnp.concatenate(lines + [jnp.broadcast_to(steer[...], (1, wide))], axis=0)
    finish()


def turn_kernel(weight_hbm, out_ref, held_ref, sems):
    turn(weight_hbm, held_ref, out_ref, sems)()


def spread_columns(rows, chans, cols_ref):
    turned = stack_rows(rows, rows[0].shape[1]).T
    for k in range(len(rows)):
        cols_ref[k] = jnp.broadcast_to(turned[:chans, k : k + 1], (chans, LANES))


def half_act(values, mean, scale, shift):
    half = (values - mean) * scale + shift
    return half * jnp.tanh(half) + half


def twice(column):
    return jnp.concatenate([column, column], axis=1)


def put_taps(taps_ref, at, row):
    chans, cols = row.shape
    lane = lax.broadcasted_iota(jnp.int32, (chans, cols), 1)
    before = jnp.where(lane == 0, 0.0, pltpu.roll(row, 1, 1))
    after = jnp.where(lane == cols - 1, 0.0, pltpu.roll(row, cols - 1, 1))
    for k, value in enumerate((before, row, after)):
        taps_ref[pl.ds((at * 3 + k) * chans, chans), :] = value.astype(BF16)


def edge_keep(at, rows, reach):
    patch, patches = lax.axis_index("patch"), lax.axis_size("patch")
    if at < reach:
        return jnp.where(patch == 0, 0.0, 1.0).astype(F32)
    if at >= reach + rows:
        return jnp.where(patch == patches - 1, 0.0, 1.0).astype(F32)
    return None


def mixer(cols_ref, rows_ref, chans):
    sign = jnp.where(lax.axis_index("cfg") == 0, 1.0, -1.0).astype(F32)
    steer = rows_ref[7:8, 0:1] * sign

    def mix(mine, other):
        shift = twice(cols_ref[4])
        mine = half_act(mine.astype(F32), twice(cols_ref[0]), twice(cols_ref[1]), shift)
        other = half_act(other.astype(F32), twice(cols_ref[2]), twice(cols_ref[3]), shift)
        return mine + steer * (mine - other)

    return mix


def matmul(weight_ref, taps, first_tap):
    depth = taps.shape[0]
    start = first_tap * (weight_ref.shape[1] // 3)
    return jnp.dot(weight_ref[:, start : start + depth], taps, preferred_element_type=F32)


def inner_kernel(
    own_ref, far_ref, seen_ref, rows_ref, weight_ref,
    steered_ref, taps_ref, cols_ref,
):
    rows, chans, cols = own_ref.shape
    wide = padded_lanes(chans)
    size = chans // GROUPS
    cfg, peers = lax.axis_index("cfg"), lax.axis_size("patch")
    mask = same_group(wide, size)
    starts = (cfg * peers, (1 - cfg) * peers)
    means = [get_rows(seen_ref, s, peers, 0, wide) for s in starts]
    squares = [get_rows(seen_ref, s, peers, 1, wide) for s in starts]
    mean_rows, var_rows = group_stats(means, squares, float(rows * cols), mask, size)
    scale_rows = lax.rsqrt(var_rows + EPS) * (0.5 * rows_ref[0:1])
    times = jnp.sum(get_rows(seen_ref, 0, peers, 2, wide), axis=0, keepdims=True)
    added = times + (rows_ref[3:4] + rows_ref[2:3])
    spread_columns(
        [mean_rows[0:1], scale_rows[0:1], mean_rows[1:2], scale_rows[1:2], 0.5 * rows_ref[1:2], added],
        chans, cols_ref,
    )
    mix = mixer(cols_ref, rows_ref, chans)
    line = 3 * chans
    if rows < 3:
        steered_ref[...] = jnp.zeros_like(steered_ref)
    for at in range(rows):
        put_taps(taps_ref, at, mix(own_ref[at], far_ref[at]))
        if at >= 2:
            total = matmul(weight_ref, taps_ref[(at - 2) * line : (at + 1) * line, :], 0)
            steered_ref[at - 2] = total + twice(cols_ref[5])


def outer_kernel(
    near_ref, next_ref, far_near_ref, far_next_ref, inner_ref, inner_taps_ref, cols_ref, rows_ref, weight_ref,
    steered_ref, out_ref,
    taps_ref, edge_ref,
):
    reach, chans, cols = near_ref.shape
    line = 3 * chans
    rows = inner_taps_ref.shape[0] // line
    above = jnp.where(lax.rem(lax.axis_index("patch"), 2) == 0, reach, 0)
    edge_ref[0, pl.ds(above, reach)] = next_ref[...]
    edge_ref[1, pl.ds(above, reach)] = far_next_ref[...]
    edge_ref[0, pl.ds(reach - above, reach)] = near_ref[...]
    edge_ref[1, pl.ds(reach - above, reach)] = far_near_ref[...]
    mix = mixer(cols_ref, rows_ref, chans)

    def taps(at):
        if reach <= at < reach + rows:
            return inner_taps_ref, at - reach
        return taps_ref, at if at < reach else at - rows

    def rows_of(first, count):
        ref, at = taps(first)
        return ref[at * line : (at + count) * line, :]

    def conv(at):
        total, tap = None, 0
        while tap < 3:
            ref, _ = taps(at + tap)
            count = 1
            while tap + count < 3 and taps(at + tap + count)[0] is ref:
                count += 1
            part = matmul(weight_ref, rows_of(at + tap, count), tap)
            total = part if total is None else total + part
            tap += count
        return total

    def enter(at):
        k = reach + at if at < reach else at - reach - rows
        keep = edge_keep(at, rows, reach)
        put_taps(taps_ref, taps(at)[1], mix(edge_ref[0, k], edge_ref[1, k]) * keep)

    for at in range(reach):
        enter(at)
    outside = [at for at in range(rows + 2 * reach - 2) if not reach <= at < reach + rows - 2]
    place = {at: k for k, at in enumerate(outside)}
    ready = reach + rows
    for at in outside:
        while ready < at + 3:
            enter(ready)
            ready += 1
        steered_ref[place[at]] = conv(at) + twice(cols_ref[5])

    def own_rows():
        for k in range(rows):
            at = reach - 1 + k
            yield steered_ref[place[at]] if at in place else inner_ref[at - reach]

    mean, square = channel_moments(own_rows, chans)
    put_rows([mean, square], out_ref)


def second_kernel(
    inner_ref, outer_ref, lat_ref, seen_ref, rows_ref, weight_ref,
    out_ref,
    taps_ref, cols_ref,
):
    rows, chans, cols = lat_ref.shape
    wide = padded_lanes(chans)
    size = chans // GROUPS
    peers = lax.axis_size("patch")
    mask = same_group(wide, size)
    mean_rows, var_rows = group_stats(
        [get_rows(seen_ref, 0, peers, 0, wide)], [get_rows(seen_ref, 0, peers, 1, wide)],
        float(rows * cols), mask, size,
    )
    scale_rows = lax.rsqrt(var_rows + EPS) * (0.5 * rows_ref[4:5])
    spread_columns(
        [mean_rows[0:1], scale_rows[0:1], 0.5 * rows_ref[5:6], rows_ref[6:7]], chans, cols_ref
    )
    line = 3 * chans
    inside = max(rows - 2, 0)
    half = outer_ref.shape[0] // 2
    for at in range(rows + 2):
        if half <= at < half + inside:
            value = inner_ref[at - half]
        else:
            value = outer_ref[at if at < half else at - inside]
        value = half_act(value, twice(cols_ref[0]), twice(cols_ref[1]), twice(cols_ref[2]))
        keep = edge_keep(at, rows, 1)
        put_taps(taps_ref, at, value if keep is None else value * keep)
        if at >= 2:
            total = matmul(weight_ref, taps_ref[(at - 2) * line : (at + 1) * line, :], 0)
            out_ref[at - 2] = (lat_ref[at - 2].astype(F32) + (total + twice(cols_ref[3]))).astype(BF16)


def everyone(tiles, axes):
    return lax.all_to_all(tiles, axes, 0, 0)


VMEM = pl.BlockSpec(memory_space=pltpu.VMEM)
ANY = pl.BlockSpec(memory_space=pl.ANY)
LIMIT = pltpu.CompilerParams(vmem_limit_bytes=12 * 1024 * 1024)


def in_hbm(value):
    return pltpu.with_memory_space_constraint(value, pltpu.HBM)


def body(
    latents, time_embed, steer_scale, gain_one, shift_one, conv_one, bias_one,
    time_weight, time_bias, gain_two, shift_two, conv_two, bias_two,
):
    own = jnp.swapaxes(latents[0, 0], 1, 2)
    rows, chans, cols = own.shape
    wide = padded_lanes(chans)
    deep = 9 * chans
    patches = lax.axis_size("patch")
    near_edge, next_edge = pl.pallas_call(
        edges_kernel,
        out_shape=[pltpu.VMEM((REACH, chans, cols), BF16)] * 2,
        in_specs=[ANY],
        out_specs=[VMEM] * 2,
        scratch_shapes=[pltpu.SemaphoreType.DMA((2,))],
        compiler_params=LIMIT,
        name="edges",
    )(in_hbm(own))
    near = lax.ppermute(near_edge, "patch", [(i, i ^ 1) for i in range(patches)])
    steps = [(i, i + 1) for i in range(1, patches - 1, 2)]
    following = lax.ppermute(next_edge, "patch", steps + [(j, i) for i, j in steps])
    swap = [(0, 1), (1, 0)]
    line = lambda vector: vector.reshape(1, -1)

    tile_one = -(-3 * wide // LANES // 8) * 8
    held, sent = pl.pallas_call(
        stats_kernel,
        out_shape=[
            pltpu.VMEM((rows, chans, cols), BF16),
            pltpu.VMEM((2 * patches, tile_one, LANES), F32),
        ],
        in_specs=[ANY] * 3,
        out_specs=[VMEM] * 2,
        scratch_shapes=[
            pltpu.VMEM(time_embed.shape, BF16),
            pltpu.VMEM(time_weight.shape, BF16),
            pltpu.SemaphoreType.DMA((rows + 2,)),
        ],
        compiler_params=LIMIT,
        name="stats",
    )(in_hbm(own), in_hbm(time_embed), in_hbm(time_weight))
    seen = everyone(sent, ("cfg", "patch"))

    source, weight_one, _ = lax.optimization_barrier((own, conv_one.reshape(deep, chans), sent))
    far = lax.ppermute(source, "cfg", swap)
    turned_one, vectors = pl.pallas_call(
        prepare_kernel,
        out_shape=[pltpu.VMEM((chans, deep), BF16), pltpu.VMEM((8, wide), F32)],
        in_specs=[ANY] + [VMEM] * 8,
        out_specs=[VMEM] * 2,
        scratch_shapes=[
            pltpu.VMEM((deep, chans), BF16), pltpu.SemaphoreType.DMA((PARTS,)),
        ],
        compiler_params=LIMIT,
        name="prepare",
    )(
        in_hbm(weight_one), line(gain_one), line(shift_one), line(bias_one),
        line(time_bias), line(gain_two), line(shift_two), line(bias_two), line(steer_scale),
    )
    near, following, vectors, seen = lax.optimization_barrier((near, following, vectors, seen))
    far_near = lax.ppermute(near, "cfg", swap)
    far_next = lax.ppermute(following, "cfg", swap)

    inner, taps, columns = pl.pallas_call(
        inner_kernel,
        out_shape=[
            pltpu.VMEM((max(rows - 2, 1), chans, cols), F32),
            pltpu.VMEM((rows * 3 * chans, cols), BF16),
            pltpu.VMEM((6, chans, LANES), F32),
        ],
        in_specs=[VMEM] * 5,
        out_specs=[VMEM] * 3,
        compiler_params=LIMIT,
        name="inner",
    )(held, far, seen, vectors, turned_one)
    tile_two = -(-2 * wide // LANES // 8) * 8
    outer, sent = pl.pallas_call(
        outer_kernel,
        out_shape=[
            pltpu.VMEM((2 * REACH, chans, cols), F32),
            pltpu.VMEM((patches, tile_two, LANES), F32),
        ],
        in_specs=[VMEM] * 9,
        out_specs=[VMEM] * 2,
        scratch_shapes=[
            pltpu.VMEM((2 * REACH * 3 * chans, cols), BF16),
            pltpu.VMEM((2, 2 * REACH, chans, cols), BF16),
        ],
        compiler_params=LIMIT,
        name="outer",
    )(near, following, far_near, far_next, inner, taps, columns, vectors, turned_one)
    seen = everyone(sent, "patch")
    weight_two, _ = lax.optimization_barrier((conv_two.reshape(deep, chans), sent))
    turned_two = pl.pallas_call(
        turn_kernel,
        out_shape=pltpu.VMEM((chans, deep), BF16),
        in_specs=[ANY],
        out_specs=VMEM,
        scratch_shapes=[pltpu.VMEM((deep, chans), BF16), pltpu.SemaphoreType.DMA((PARTS,))],
        compiler_params=LIMIT,
        name="turn",
    )(in_hbm(weight_two))
    image = pl.pallas_call(
        second_kernel,
        out_shape=jax.ShapeDtypeStruct((rows, chans, cols), BF16),
        in_specs=[VMEM] * 6,
        out_specs=VMEM,
        scratch_shapes=[
            pltpu.VMEM(((rows + 2) * 3 * chans, cols), BF16),
            pltpu.VMEM((4, chans, LANES), F32),
        ],
        compiler_params=LIMIT,
        name="second",
    )(inner, outer, held, seen, vectors, turned_two)
    return jnp.swapaxes(image, 1, 2)[None, None]


def solution(mesh):
    placed = (
        P("cfg", "req", "patch", None, None), P("req", None), P("req"), P(), P(), P(), P(),
        P("patch", None), P(), P(), P(), P(), P(),
    )
    return jax.shard_map(
        body,
        mesh=mesh,
        in_specs=placed,
        out_specs=P("cfg", "req", "patch", None, None),
        check_vma=False,
    )
```

```python
import functools

import jax
import jax.numpy as jnp
from jax import lax
from jax.experimental import pallas as pl
from jax.experimental.pallas import tpu as pltpu
from jax.sharding import PartitionSpec as P

GROUPS = 32
EPS = 1e-05
REACH = 2
LANES = 128
F32 = jnp.float32
BF16 = jnp.bfloat16


def padded_lanes(chans):
    return -(-chans // LANES) * LANES


def widen(row, wide):
    short = wide - row.shape[1]
    if not short:
        return row
    return jnp.concatenate([row, jnp.zeros((row.shape[0], short), row.dtype)], axis=1)


def same_group(wide, size):
    left = lax.broadcasted_iota(jnp.int32, (wide, wide), 0).astype(F32)
    right = lax.broadcasted_iota(jnp.int32, (wide, wide), 1).astype(F32)
    group = lambda at: jnp.floor((at + 0.5) * (1.0 / size))
    return jnp.where(group(left) == group(right), 1.0, 0.0).astype(BF16)


def group_sum(rows, mask):
    high = rows.astype(BF16).astype(F32)
    rest = rows - high
    middle = rest.astype(BF16).astype(F32)
    pieces = jnp.concatenate([high, middle, rest - middle, jnp.zeros_like(rows)], axis=0).astype(BF16)
    sums = jnp.dot(pieces, mask, preferred_element_type=F32)
    return sums[0:8] + sums[8:16] + sums[16:24]


def stack_rows(rows, wide):
    filler = [jnp.zeros((8 - len(rows), wide), F32)] if len(rows) < 8 else []
    return jnp.concatenate(list(rows) + filler, axis=0)


def group_stats(means, squares, count, mask, size):
    wide = mask.shape[0]
    peers = means[0].shape[0]
    mean_rows = [jnp.sum(m, axis=0, keepdims=True) * (1.0 / peers) for m in means]
    mean_rows = group_sum(stack_rows(mean_rows, wide), mask) * (1.0 / size)
    spread = []
    for k, (m, q) in enumerate(zip(means, squares)):
        off = m - mean_rows[k : k + 1]
        spread.append(jnp.sum(q + count * (off * off), axis=0, keepdims=True))
    var_rows = group_sum(stack_rows(spread, wide), mask) * (1.0 / (size * count * peers))
    return mean_rows, var_rows


def fold(values):
    total = values[:, :LANES]
    for at in range(LANES, values.shape[1], LANES):
        total = total + values[:, at : at + LANES]
    return total


def channel_moments(rows, chans):
    count = 0
    total = None
    for row in rows():
        part = fold(row)
        count += row.shape[1]
        total = part if total is None else total + part
    mean = jnp.sum(total, axis=1, keepdims=True) * (1.0 / count)
    squares = None
    for row in rows():
        off = row - mean
        part = fold(off * off)
        squares = part if squares is None else squares + part
    squares = jnp.sum(squares, axis=1, keepdims=True)
    lane = lax.broadcasted_iota(jnp.int32, (chans, LANES), 1)
    both = jnp.where(lane == 0, mean, jnp.where(lane == 1, squares, 0.0))
    wide = padded_lanes(chans)
    both = jnp.concatenate([both, jnp.zeros((wide - chans, LANES), F32)], axis=0)
    turned = both.T
    return turned[0:1], turned[1:2]


def put_rows(tile_rows, out_ref):
    peers, height, _ = out_ref.shape
    lines = [row[:, at : at + LANES] for row in tile_rows for at in range(0, row.shape[1], LANES)]
    if len(lines) < height:
        lines.append(jnp.zeros((height - len(lines), LANES), F32))
    tile = jnp.concatenate(lines, axis=0)
    out_ref[...] = jnp.broadcast_to(tile[None], out_ref.shape)


def get_rows(seen_ref, first, peers, which, wide):
    lines = wide // LANES
    return jnp.concatenate(
        [seen_ref[pl.ds(first, peers), which * lines + k, :] for k in range(lines)], axis=1
    )


def stats_kernel(
    lat_hbm, embed_hbm, weight_hbm,
    lat_ref, out_ref, near_hbm, next_hbm,
    embed_ref, weight_ref, sems, edge_sems,
):
    rows, chans, _ = lat_ref.shape
    copies = [
        pltpu.make_async_copy(lat_hbm.at[k], lat_ref.at[k], sems.at[k]) for k in range(rows)
    ]
    copies.append(pltpu.make_async_copy(embed_hbm, embed_ref, sems.at[rows]))
    copies.append(pltpu.make_async_copy(weight_hbm, weight_ref, sems.at[rows + 1]))
    reach = near_hbm.shape[0]
    last = rows - reach
    near_at = jnp.where(lax.rem(lax.axis_index("patch"), 2) == 0, last, 0)
    edges = [
        pltpu.make_async_copy(lat_hbm.at[pl.ds(near_at, reach)], near_hbm, edge_sems.at[0]),
        pltpu.make_async_copy(lat_hbm.at[pl.ds(last - near_at, reach)], next_hbm, edge_sems.at[1]),
    ]
    for copy in copies + edges:
        copy.start()
    waits = list(copies[:rows])

    def values():
        for k in range(rows):
            if waits:
                waits.pop(0).wait()
            yield lat_ref[k].astype(F32)

    wide = padded_lanes(chans)
    mean, squares = channel_moments(values, chans)
    copies[rows].wait()
    copies[rows + 1].wait()
    own = weight_ref.shape[0]
    length = embed_ref.shape[1]
    embed = jnp.broadcast_to(embed_ref[...].astype(F32), (8, length))
    embed = pltpu.roll(embed, length - lax.axis_index("patch") * own, 1)[:, :own]
    act = (embed / (1.0 + jnp.exp(-embed))).astype(BF16)
    time_part = jnp.dot(act, weight_ref[...], preferred_element_type=F32)[0:1]
    put_rows([mean, squares, widen(time_part, wide)], out_ref)
    for copy in edges:
        copy.wait()


def turn(source, target, held_ref, turned_ref, sems):
    part = held_ref.shape[0] // 3
    copies = []
    for k in range(3):
        here = pl.ds(k * part, part)
        copies.append(pltpu.make_async_copy(source.at[here], held_ref.at[here], sems.at[k]))
        copies[k].start()

    def finish():
        out = []
        for k in range(3):
            copies[k].wait()
            turned_ref[k] = held_ref[k * part : (k + 1) * part, :].T
            out.append(pltpu.make_async_copy(turned_ref.at[k], target.at[k], sems.at[3 + k]))
            out[k].start()
        for copy in out:
            copy.wait()

    return finish


def prepare_kernel(
    weight_hbm, gain_one, shift_one, bias_one, time_bias, gain_two, shift_two, bias_two, steer,
    out_hbm, rows_ref, held_ref, turned_ref, sems, row_sems, *vector_refs,
):
    finish = turn(weight_hbm, out_hbm, held_ref, turned_ref, sems)
    wide = rows_ref.shape[1]
    vectors = (gain_one, shift_one, bias_one, time_bias, gain_two, shift_two, bias_two)
    for copy in fetch(zip(vectors, vector_refs), row_sems):
        copy.wait()
    rows = [widen(v[...].reshape(1, -1), wide) for v in vector_refs]
    rows_ref[...] = jnp.concatenate(rows + [jnp.broadcast_to(steer[...], (1, wide))], axis=0)
    finish()


def turn_kernel(weight_hbm, out_hbm, held_ref, turned_ref, sems):
    turn(weight_hbm, out_hbm, held_ref, turned_ref, sems)()


def fetch(pairs, sems):
    copies = [pltpu.make_async_copy(a, b, sems.at[k]) for k, (a, b) in enumerate(pairs)]
    for copy in copies:
        copy.start()
    return copies


def spread_columns(rows, chans, cols_ref):
    turned = stack_rows(rows, rows[0].shape[1]).T
    for k in range(len(rows)):
        cols_ref[k] = jnp.broadcast_to(turned[:chans, k : k + 1], (chans, LANES))


def half_act(values, mean, scale, shift):
    half = (values - mean) * scale + shift
    return half * jnp.tanh(half) + half


def twice(column):
    return jnp.concatenate([column, column], axis=1)


def put_taps(taps_ref, at, row):
    chans, cols = row.shape
    lane = lax.broadcasted_iota(jnp.int32, (chans, cols), 1)
    before = jnp.where(lane == 0, 0.0, pltpu.roll(row, 1, 1))
    after = jnp.where(lane == cols - 1, 0.0, pltpu.roll(row, cols - 1, 1))
    for k, value in enumerate((before, row, after)):
        taps_ref[pl.ds((at * 3 + k) * chans, chans), :] = value.astype(BF16)


def edge_keep(at, rows, reach):
    patch, patches = lax.axis_index("patch"), lax.axis_size("patch")
    if at < reach:
        return jnp.where(patch == 0, 0.0, 1.0).astype(F32)
    if at >= reach + rows:
        return jnp.where(patch == patches - 1, 0.0, 1.0).astype(F32)
    return None


def mixer(cols_ref, rows_ref, chans):
    sign = jnp.where(lax.axis_index("cfg") == 0, 1.0, -1.0).astype(F32)
    steer = rows_ref[7:8, 0:1] * sign

    def mix(mine, other):
        shift = twice(cols_ref[4])
        mine = half_act(mine.astype(F32), twice(cols_ref[0]), twice(cols_ref[1]), shift)
        other = half_act(other.astype(F32), twice(cols_ref[2]), twice(cols_ref[3]), shift)
        return mine + steer * (mine - other)

    return mix


def conv_row(weight_ref, taps):
    total = None
    for k, tap in enumerate(taps):
        part = jnp.dot(weight_ref[k], tap, preferred_element_type=F32)
        total = part if total is None else total + part
    return total


def line_of(taps_ref, at, chans):
    return taps_ref[at * 3 * chans : (at + 1) * 3 * chans, :]


def inner_kernel(
    own_ref, far_hbm, seen_ref, rows_ref, weight_hbm,
    steered_ref, taps_ref, cols_ref,
    far_ref, weight_ref, sems,
):
    rows, chans, cols = own_ref.shape
    copies = fetch(
        [(far_hbm.at[k], far_ref.at[k]) for k in range(rows)]
        + [(weight_hbm.at[k], weight_ref.at[k]) for k in range(3)],
        sems,
    )
    wide = padded_lanes(chans)
    size = chans // GROUPS
    cfg, peers = lax.axis_index("cfg"), lax.axis_size("patch")
    mask = same_group(wide, size)
    starts = (cfg * peers, (1 - cfg) * peers)
    means = [get_rows(seen_ref, s, peers, 0, wide) for s in starts]
    squares = [get_rows(seen_ref, s, peers, 1, wide) for s in starts]
    mean_rows, var_rows = group_stats(means, squares, float(rows * cols), mask, size)
    scale_rows = lax.rsqrt(var_rows + EPS) * (0.5 * rows_ref[0:1])
    times = jnp.sum(get_rows(seen_ref, 0, peers, 2, wide), axis=0, keepdims=True)
    added = times + (rows_ref[3:4] + rows_ref[2:3])
    spread_columns(
        [mean_rows[0:1], scale_rows[0:1], mean_rows[1:2], scale_rows[1:2], 0.5 * rows_ref[1:2], added],
        chans, cols_ref,
    )
    mix = mixer(cols_ref, rows_ref, chans)
    if rows < 3:
        steered_ref[...] = jnp.zeros_like(steered_ref)
    for at in range(rows):
        copies[at].wait()
        put_taps(taps_ref, at, mix(own_ref[at], far_ref[at]))
        if at == min(1, rows - 1):
            for copy in copies[rows:]:
                copy.wait()
        if at >= 2:
            total = conv_row(weight_ref, [line_of(taps_ref, at - 2 + k, chans) for k in range(3)])
            steered_ref[at - 2] = total + twice(cols_ref[5])


def outer_kernel(
    near_hbm, next_hbm, far_near_hbm, far_next_hbm, inner_ref, inner_taps_ref, cols_ref, rows_ref, weight_hbm,
    steered_ref, out_ref,
    taps_ref, edge_ref, weight_ref, sems,
):
    reach, chans, cols = near_hbm.shape
    rows = inner_taps_ref.shape[0] // (3 * chans)
    above = jnp.where(lax.rem(lax.axis_index("patch"), 2) == 0, reach, 0)
    below = reach - above
    copies = fetch(
        [
            (next_hbm, edge_ref.at[0, pl.ds(above, reach)]),
            (far_next_hbm, edge_ref.at[1, pl.ds(above, reach)]),
            (near_hbm, edge_ref.at[0, pl.ds(below, reach)]),
            (far_near_hbm, edge_ref.at[1, pl.ds(below, reach)]),
        ]
        + [(weight_hbm.at[k], weight_ref.at[k]) for k in range(3)],
        sems,
    )
    mix = mixer(cols_ref, rows_ref, chans)

    def taps(at):
        if reach <= at < reach + rows:
            return line_of(inner_taps_ref, at - reach, chans)
        return line_of(taps_ref, at if at < reach else at - rows, chans)

    def enter(at):
        k = reach + at if at < reach else at - reach - rows
        keep = edge_keep(at, rows, reach)
        put_taps(taps_ref, at if at < reach else at - rows, mix(edge_ref[0, k], edge_ref[1, k]) * keep)

    for copy in copies[:4]:
        copy.wait()
    for at in range(reach):
        enter(at)
    for copy in copies[4:]:
        copy.wait()
    outside = [at for at in range(rows + 2 * reach - 2) if not reach <= at < reach + rows - 2]
    place = {at: k for k, at in enumerate(outside)}
    ready = reach + rows
    for at in outside:
        while ready < at + 3:
            enter(ready)
            ready += 1
        total = conv_row(weight_ref, [taps(at + k) for k in range(3)])
        steered_ref[place[at]] = total + twice(cols_ref[5])

    def own_rows():
        for k in range(rows):
            at = reach - 1 + k
            yield steered_ref[place[at]] if at in place else inner_ref[at - reach]

    mean, square = channel_moments(own_rows, chans)
    put_rows([mean, square], out_ref)


def second_kernel(
    inner_ref, outer_ref, lat_ref, seen_ref, rows_ref, weight_hbm,
    out_ref,
    taps_ref, cols_ref, weight_ref, sems,
):
    copies = fetch([(weight_hbm.at[k], weight_ref.at[k]) for k in range(3)], sems)
    rows, chans, cols = lat_ref.shape
    wide = padded_lanes(chans)
    size = chans // GROUPS
    peers = lax.axis_size("patch")
    mask = same_group(wide, size)
    mean_rows, var_rows = group_stats(
        [get_rows(seen_ref, 0, peers, 0, wide)], [get_rows(seen_ref, 0, peers, 1, wide)],
        float(rows * cols), mask, size,
    )
    scale_rows = lax.rsqrt(var_rows + EPS) * (0.5 * rows_ref[4:5])
    spread_columns(
        [mean_rows[0:1], scale_rows[0:1], 0.5 * rows_ref[5:6], rows_ref[6:7]], chans, cols_ref
    )
    inside = max(rows - 2, 0)
    half = outer_ref.shape[0] // 2
    for at in range(rows + 2):
        if half <= at < half + inside:
            value = inner_ref[at - half]
        else:
            value = outer_ref[at if at < half else at - inside]
        value = half_act(value, twice(cols_ref[0]), twice(cols_ref[1]), twice(cols_ref[2]))
        keep = edge_keep(at, rows, 1)
        put_taps(taps_ref, at, value if keep is None else value * keep)
        if at == 1:
            for copy in copies:
                copy.wait()
        if at >= 2:
            total = conv_row(weight_ref, [line_of(taps_ref, at - 2 + k, chans) for k in range(3)])
            out_ref[at - 2] = (lat_ref[at - 2].astype(F32) + (total + twice(cols_ref[3]))).astype(BF16)


def everyone(tiles, axes):
    return lax.all_to_all(tiles, axes, 0, 0)


VMEM = pl.BlockSpec(memory_space=pltpu.VMEM)
ANY = pl.BlockSpec(memory_space=pl.ANY)
LIMIT = pltpu.CompilerParams(vmem_limit_bytes=12 * 1024 * 1024)


def in_hbm(value):
    return pltpu.with_memory_space_constraint(value, pltpu.HBM)


def body(
    latents, time_embed, steer_scale, gain_one, shift_one, conv_one, bias_one,
    time_weight, time_bias, gain_two, shift_two, conv_two, bias_two,
):
    own = jnp.swapaxes(latents[0, 0], 1, 2)
    rows, chans, cols = own.shape
    wide = padded_lanes(chans)
    deep = 9 * chans
    patches = lax.axis_size("patch")
    swap = [(0, 1), (1, 0)]
    dma = pltpu.SemaphoreType.DMA
    turned = (3, chans, 3 * chans)

    tile_one = -(-3 * wide // LANES // 8) * 8
    held, sent, near_edge, next_edge = pl.pallas_call(
        stats_kernel,
        out_shape=[
            pltpu.VMEM((rows, chans, cols), BF16),
            pltpu.VMEM((2 * patches, tile_one, LANES), F32),
            pltpu.HBM((REACH, chans, cols), BF16),
            pltpu.HBM((REACH, chans, cols), BF16),
        ],
        in_specs=[ANY] * 3,
        out_specs=[VMEM] * 2 + [ANY] * 2,
        scratch_shapes=[
            pltpu.VMEM(time_embed.shape, BF16),
            pltpu.VMEM(time_weight.shape, BF16),
            dma((rows + 2,)),
            dma((2,)),
        ],
        compiler_params=LIMIT,
        name="stats",
    )(in_hbm(own), in_hbm(time_embed), in_hbm(time_weight))
    near = lax.ppermute(near_edge, "patch", [(i, i ^ 1) for i in range(patches)])
    steps = [(i, i + 1) for i in range(1, patches - 1, 2)]
    following = lax.ppermute(next_edge, "patch", steps + [(j, i) for i, j in steps])
    seen = everyone(sent, ("cfg", "patch"))

    weight_one, _ = lax.optimization_barrier((conv_one.reshape(deep, chans), sent))
    turning = [pltpu.VMEM((deep, chans), BF16), pltpu.VMEM(turned, BF16)]
    turned_one, vectors = pl.pallas_call(
        prepare_kernel,
        out_shape=[pltpu.HBM(turned, BF16), pltpu.VMEM((8, wide), F32)],
        in_specs=[ANY] * 8 + [VMEM],
        out_specs=[ANY, VMEM],
        scratch_shapes=turning + [dma((6,)), dma((7,))] + [pltpu.VMEM((chans,), F32)] * 7,
        compiler_params=LIMIT,
        name="prepare",
    )(
        in_hbm(weight_one), *(in_hbm(v) for v in (gain_one, shift_one, bias_one,
        time_bias, gain_two, shift_two, bias_two)), steer_scale.reshape(1, 1),
    )
    source, vectors = lax.optimization_barrier((own, vectors))
    far = lax.ppermute(source, "cfg", swap)
    near, following, vectors, seen = lax.optimization_barrier((near, following, vectors, seen))
    far_near = lax.ppermute(near, "cfg", swap)
    far_next = lax.ppermute(following, "cfg", swap)

    inner, taps, columns = pl.pallas_call(
        inner_kernel,
        out_shape=[
            pltpu.VMEM((max(rows - 2, 1), chans, cols), F32),
            pltpu.VMEM((rows * 3 * chans, cols), BF16),
            pltpu.VMEM((6, chans, LANES), F32),
        ],
        in_specs=[VMEM, ANY, VMEM, VMEM, ANY],
        out_specs=[VMEM] * 3,
        scratch_shapes=[
            pltpu.VMEM((rows, chans, cols), BF16), pltpu.VMEM(turned, BF16), dma((rows + 3,)),
        ],
        compiler_params=LIMIT,
        name="inner",
    )(held, far, seen, vectors, in_hbm(turned_one))
    tile_two = -(-2 * wide // LANES // 8) * 8
    outer, sent = pl.pallas_call(
        outer_kernel,
        out_shape=[
            pltpu.VMEM((2 * REACH, chans, cols), F32),
            pltpu.VMEM((patches, tile_two, LANES), F32),
        ],
        in_specs=[ANY] * 4 + [VMEM] * 4 + [ANY],
        out_specs=[VMEM] * 2,
        scratch_shapes=[
            pltpu.VMEM((2 * REACH * 3 * chans, cols), BF16),
            pltpu.VMEM((2, 2 * REACH, chans, cols), BF16),
            pltpu.VMEM(turned, BF16),
            dma((7,)),
        ],
        compiler_params=LIMIT,
        name="outer",
    )(
        near, following, far_near, far_next, inner, taps, columns, vectors, in_hbm(turned_one),
    )
    seen = everyone(sent, "patch")
    weight_two, _ = lax.optimization_barrier((conv_two.reshape(deep, chans), sent))
    turned_two = pl.pallas_call(
        turn_kernel,
        out_shape=pltpu.HBM(turned, BF16),
        in_specs=[ANY],
        out_specs=ANY,
        scratch_shapes=turning + [dma((6,))],
        compiler_params=LIMIT,
        name="turn",
    )(in_hbm(weight_two))
    image = pl.pallas_call(
        second_kernel,
        out_shape=jax.ShapeDtypeStruct((rows, chans, cols), BF16),
        in_specs=[VMEM] * 5 + [ANY],
        out_specs=VMEM,
        scratch_shapes=[
            pltpu.VMEM(((rows + 2) * 3 * chans, cols), BF16),
            pltpu.VMEM((4, chans, LANES), F32),
            pltpu.VMEM(turned, BF16),
            dma((3,)),
        ],
        compiler_params=LIMIT,
        name="second",
    )(inner, outer, held, seen, vectors, in_hbm(turned_two))
    return jnp.swapaxes(image, 1, 2)[None, None]


def solution(mesh):
    placed = (
        P("cfg", "req", "patch", None, None), P("req", None), P("req"), P(), P(), P(), P(),
        P("patch", None), P(), P(), P(), P(), P(),
    )
    return jax.shard_map(
        body,
        mesh=mesh,
        in_specs=placed,
        out_specs=P("cfg", "req", "patch", None, None),
        check_vma=False,
    )
```

```python
import functools

import jax
import jax.numpy as jnp
from jax import lax
from jax.experimental import pallas as pl
from jax.experimental.pallas import tpu as pltpu
from jax.sharding import PartitionSpec as P

GROUPS = 32
EPS = 1e-05
REACH = 2
LANES = 128
F32 = jnp.float32
BF16 = jnp.bfloat16


def padded_lanes(chans):
    return -(-chans // LANES) * LANES


def widen(row, wide):
    short = wide - row.shape[1]
    if not short:
        return row
    return jnp.concatenate([row, jnp.zeros((row.shape[0], short), row.dtype)], axis=1)


def same_group(wide, size):
    left = lax.broadcasted_iota(jnp.int32, (wide, wide), 0).astype(F32)
    right = lax.broadcasted_iota(jnp.int32, (wide, wide), 1).astype(F32)
    group = lambda at: jnp.floor((at + 0.5) * (1.0 / size))
    return jnp.where(group(left) == group(right), 1.0, 0.0).astype(BF16)


def group_sum(rows, mask):
    high = rows.astype(BF16).astype(F32)
    rest = rows - high
    middle = rest.astype(BF16).astype(F32)
    pieces = jnp.concatenate([high, middle, rest - middle, jnp.zeros_like(rows)], axis=0).astype(BF16)
    sums = jnp.dot(pieces, mask, preferred_element_type=F32)
    return sums[0:8] + sums[8:16] + sums[16:24]


def stack_rows(rows, wide):
    filler = [jnp.zeros((8 - len(rows), wide), F32)] if len(rows) < 8 else []
    return jnp.concatenate(list(rows) + filler, axis=0)


def group_stats(means, squares, count, mask, size):
    wide = mask.shape[0]
    peers = means[0].shape[0]
    mean_rows = [jnp.sum(m, axis=0, keepdims=True) * (1.0 / peers) for m in means]
    mean_rows = group_sum(stack_rows(mean_rows, wide), mask) * (1.0 / size)
    spread = []
    for k, (m, q) in enumerate(zip(means, squares)):
        off = m - mean_rows[k : k + 1]
        spread.append(jnp.sum(q + count * (off * off), axis=0, keepdims=True))
    var_rows = group_sum(stack_rows(spread, wide), mask) * (1.0 / (size * count * peers))
    return mean_rows, var_rows


def fold(values):
    total = values[:, :LANES]
    for at in range(LANES, values.shape[1], LANES):
        total = total + values[:, at : at + LANES]
    return total


def channel_moments(rows, chans):
    count = 0
    total = None
    for row in rows():
        part = fold(row)
        count += row.shape[1]
        total = part if total is None else total + part
    mean = jnp.sum(total, axis=1, keepdims=True) * (1.0 / count)
    squares = None
    for row in rows():
        off = row - mean
        part = fold(off * off)
        squares = part if squares is None else squares + part
    squares = jnp.sum(squares, axis=1, keepdims=True)
    lane = lax.broadcasted_iota(jnp.int32, (chans, LANES), 1)
    both = jnp.where(lane == 0, mean, jnp.where(lane == 1, squares, 0.0))
    wide = padded_lanes(chans)
    both = jnp.concatenate([both, jnp.zeros((wide - chans, LANES), F32)], axis=0)
    turned = both.T
    return turned[0:1], turned[1:2]


def put_rows(tile_rows, out_ref):
    peers, height, _ = out_ref.shape
    lines = [row[:, at : at + LANES] for row in tile_rows for at in range(0, row.shape[1], LANES)]
    if len(lines) < height:
        lines.append(jnp.zeros((height - len(lines), LANES), F32))
    tile = jnp.concatenate(lines, axis=0)
    out_ref[...] = jnp.broadcast_to(tile[None], out_ref.shape)


def get_rows(seen_ref, first, peers, which, wide):
    lines = wide // LANES
    return jnp.concatenate(
        [seen_ref[pl.ds(first, peers), which * lines + k, :] for k in range(lines)], axis=1
    )


def stats_kernel(
    lat_hbm, embed_hbm, weight_hbm,
    lat_ref, out_ref, near_ref, next_ref,
    embed_ref, weight_ref, sems, edge_sems,
):
    rows, chans, _ = lat_ref.shape
    copies = [
        pltpu.make_async_copy(lat_hbm.at[k], lat_ref.at[k], sems.at[k]) for k in range(rows)
    ]
    copies.append(pltpu.make_async_copy(embed_hbm, embed_ref, sems.at[rows]))
    copies.append(pltpu.make_async_copy(weight_hbm, weight_ref, sems.at[rows + 1]))
    reach = near_ref.shape[0]
    last = rows - reach
    near_at = jnp.where(lax.rem(lax.axis_index("patch"), 2) == 0, last, 0)
    edges = [
        pltpu.make_async_copy(lat_hbm.at[pl.ds(near_at, reach)], near_ref, edge_sems.at[0]),
        pltpu.make_async_copy(lat_hbm.at[pl.ds(last - near_at, reach)], next_ref, edge_sems.at[1]),
    ]
    for copy in copies + edges:
        copy.start()
    waits = list(copies[:rows])

    def values():
        for k in range(rows):
            if waits:
                waits.pop(0).wait()
            yield lat_ref[k].astype(F32)

    wide = padded_lanes(chans)
    mean, squares = channel_moments(values, chans)
    copies[rows].wait()
    copies[rows + 1].wait()
    own = weight_ref.shape[0]
    length = embed_ref.shape[1]
    embed = jnp.broadcast_to(embed_ref[...].astype(F32), (8, length))
    embed = pltpu.roll(embed, length - lax.axis_index("patch") * own, 1)[:, :own]
    act = (embed / (1.0 + jnp.exp(-embed))).astype(BF16)
    time_part = jnp.dot(act, weight_ref[...], preferred_element_type=F32)[0:1]
    put_rows([mean, squares, widen(time_part, wide)], out_ref)
    for copy in edges:
        copy.wait()


PARTS = 3


def prepare_kernel(
    one_hbm, two_hbm, gain_one, shift_one, bias_one, time_bias, gain_two, shift_two, bias_two, steer,
    one_out, two_out, rows_ref, one_ref, two_ref, sems,
):
    deep = one_ref.shape[0]
    part = deep // PARTS
    jobs = []
    for k, (source, held, target) in enumerate(((one_hbm, one_ref, one_out), (two_hbm, two_ref, two_out))):
        for at in range(PARTS):
            here = pl.ds(at * part, part)
            copy = pltpu.make_async_copy(source.at[here], held.at[here], sems.at[k * PARTS + at])
            copy.start()
            jobs.append((copy, held, target, at * part))
    wide = rows_ref.shape[1]
    vectors = (gain_one, shift_one, bias_one, time_bias, gain_two, shift_two, bias_two)
    lines = [widen(v[...], wide) for v in vectors]
    rows_ref[...] = jnp.concatenate(lines + [jnp.broadcast_to(steer[...], (1, wide))], axis=0)
    for copy, held, target, at in jobs:
        copy.wait()
        target[:, at : at + part] = held[at : at + part, :].T


def spread_columns(rows, chans, cols_ref):
    turned = stack_rows(rows, rows[0].shape[1]).T
    for k in range(len(rows)):
        cols_ref[k] = jnp.broadcast_to(turned[:chans, k : k + 1], (chans, LANES))


def half_act(values, mean, scale, shift):
    half = (values - mean) * scale + shift
    return half * jnp.tanh(half) + half


def twice(column):
    return jnp.concatenate([column, column], axis=1)


def put_taps(taps_ref, at, row):
    chans, cols = row.shape
    lane = lax.broadcasted_iota(jnp.int32, (chans, cols), 1)
    before = jnp.where(lane == 0, 0.0, pltpu.roll(row, 1, 1))
    after = jnp.where(lane == cols - 1, 0.0, pltpu.roll(row, cols - 1, 1))
    for k, value in enumerate((before, row, after)):
        taps_ref[pl.ds((at * 3 + k) * chans, chans), :] = value.astype(BF16)


def edge_keep(at, rows, reach):
    patch, patches = lax.axis_index("patch"), lax.axis_size("patch")
    if at < reach:
        return jnp.where(patch == 0, 0.0, 1.0).astype(F32)
    if at >= reach + rows:
        return jnp.where(patch == patches - 1, 0.0, 1.0).astype(F32)
    return None


def mixer(cols_ref, rows_ref, chans):
    sign = jnp.where(lax.axis_index("cfg") == 0, 1.0, -1.0).astype(F32)
    steer = rows_ref[7:8, 0:1] * sign

    def mix(mine, other):
        shift = twice(cols_ref[4])
        mine = half_act(mine.astype(F32), twice(cols_ref[0]), twice(cols_ref[1]), shift)
        other = half_act(other.astype(F32), twice(cols_ref[2]), twice(cols_ref[3]), shift)
        return mine + steer * (mine - other)

    return mix


def matmul(weight_ref, taps, first_tap):
    depth = taps.shape[0]
    start = first_tap * (weight_ref.shape[1] // 3)
    return jnp.dot(weight_ref[:, start : start + depth], taps, preferred_element_type=F32)


def inner_kernel(
    own_ref, far_ref, seen_ref, rows_ref, weight_ref,
    steered_ref, taps_ref, cols_ref,
):
    rows, chans, cols = own_ref.shape
    wide = padded_lanes(chans)
    size = chans // GROUPS
    cfg, peers = lax.axis_index("cfg"), lax.axis_size("patch")
    mask = same_group(wide, size)
    starts = (cfg * peers, (1 - cfg) * peers)
    means = [get_rows(seen_ref, s, peers, 0, wide) for s in starts]
    squares = [get_rows(seen_ref, s, peers, 1, wide) for s in starts]
    mean_rows, var_rows = group_stats(means, squares, float(rows * cols), mask, size)
    scale_rows = lax.rsqrt(var_rows + EPS) * (0.5 * rows_ref[0:1])
    times = jnp.sum(get_rows(seen_ref, 0, peers, 2, wide), axis=0, keepdims=True)
    added = times + (rows_ref[3:4] + rows_ref[2:3])
    spread_columns(
        [mean_rows[0:1], scale_rows[0:1], mean_rows[1:2], scale_rows[1:2], 0.5 * rows_ref[1:2], added],
        chans, cols_ref,
    )
    mix = mixer(cols_ref, rows_ref, chans)
    line = 3 * chans
    if rows < 3:
        steered_ref[...] = jnp.zeros_like(steered_ref)
    for at in range(rows):
        put_taps(taps_ref, at, mix(own_ref[at], far_ref[at]))
        if at >= 2:
            total = matmul(weight_ref, taps_ref[(at - 2) * line : (at + 1) * line, :], 0)
            steered_ref[at - 2] = total + twice(cols_ref[5])


def outer_kernel(
    near_ref, next_ref, far_near_ref, far_next_ref, inner_ref, inner_taps_ref, cols_ref, rows_ref, weight_ref,
    steered_ref, out_ref,
    taps_ref, edge_ref,
):
    reach, chans, cols = near_ref.shape
    line = 3 * chans
    rows = inner_taps_ref.shape[0] // line
    above = jnp.where(lax.rem(lax.axis_index("patch"), 2) == 0, reach, 0)
    edge_ref[0, pl.ds(above, reach)] = next_ref[...]
    edge_ref[1, pl.ds(above, reach)] = far_next_ref[...]
    edge_ref[0, pl.ds(reach - above, reach)] = near_ref[...]
    edge_ref[1, pl.ds(reach - above, reach)] = far_near_ref[...]
    mix = mixer(cols_ref, rows_ref, chans)

    def taps(at):
        if reach <= at < reach + rows:
            return inner_taps_ref, at - reach
        return taps_ref, at if at < reach else at - rows

    def rows_of(first, count):
        ref, at = taps(first)
        return ref[at * line : (at + count) * line, :]

    def conv(at):
        total, tap = None, 0
        while tap < 3:
            ref, _ = taps(at + tap)
            count = 1
            while tap + count < 3 and taps(at + tap + count)[0] is ref:
                count += 1
            part = matmul(weight_ref, rows_of(at + tap, count), tap)
            total = part if total is None else total + part
            tap += count
        return total

    def enter(at):
        k = reach + at if at < reach else at - reach - rows
        keep = edge_keep(at, rows, reach)
        put_taps(taps_ref, taps(at)[1], mix(edge_ref[0, k], edge_ref[1, k]) * keep)

    for at in range(reach):
        enter(at)
    outside = [at for at in range(rows + 2 * reach - 2) if not reach <= at < reach + rows - 2]
    place = {at: k for k, at in enumerate(outside)}
    ready = reach + rows
    for at in outside:
        while ready < at + 3:
            enter(ready)
            ready += 1
        steered_ref[place[at]] = conv(at) + twice(cols_ref[5])

    def own_rows():
        for k in range(rows):
            at = reach - 1 + k
            yield steered_ref[place[at]] if at in place else inner_ref[at - reach]

    mean, square = channel_moments(own_rows, chans)
    put_rows([mean, square], out_ref)


def second_kernel(
    inner_ref, outer_ref, lat_ref, seen_ref, rows_ref, weight_ref,
    out_ref,
    taps_ref, cols_ref,
):
    rows, chans, cols = lat_ref.shape
    wide = padded_lanes(chans)
    size = chans // GROUPS
    peers = lax.axis_size("patch")
    mask = same_group(wide, size)
    mean_rows, var_rows = group_stats(
        [get_rows(seen_ref, 0, peers, 0, wide)], [get_rows(seen_ref, 0, peers, 1, wide)],
        float(rows * cols), mask, size,
    )
    scale_rows = lax.rsqrt(var_rows + EPS) * (0.5 * rows_ref[4:5])
    spread_columns(
        [mean_rows[0:1], scale_rows[0:1], 0.5 * rows_ref[5:6], rows_ref[6:7]], chans, cols_ref
    )
    line = 3 * chans
    inside = max(rows - 2, 0)
    half = outer_ref.shape[0] // 2
    for at in range(rows + 2):
        if half <= at < half + inside:
            value = inner_ref[at - half]
        else:
            value = outer_ref[at if at < half else at - inside]
        value = half_act(value, twice(cols_ref[0]), twice(cols_ref[1]), twice(cols_ref[2]))
        keep = edge_keep(at, rows, 1)
        put_taps(taps_ref, at, value if keep is None else value * keep)
        if at >= 2:
            total = matmul(weight_ref, taps_ref[(at - 2) * line : (at + 1) * line, :], 0)
            out_ref[at - 2] = (lat_ref[at - 2].astype(F32) + (total + twice(cols_ref[3]))).astype(BF16)


def everyone(tiles, axes):
    return lax.all_to_all(tiles, axes, 0, 0)


VMEM = pl.BlockSpec(memory_space=pltpu.VMEM)
ANY = pl.BlockSpec(memory_space=pl.ANY)
LIMIT = pltpu.CompilerParams(vmem_limit_bytes=12 * 1024 * 1024)


def in_hbm(value):
    return pltpu.with_memory_space_constraint(value, pltpu.HBM)


def body(
    latents, time_embed, steer_scale, gain_one, shift_one, conv_one, bias_one,
    time_weight, time_bias, gain_two, shift_two, conv_two, bias_two,
):
    own = jnp.swapaxes(latents[0, 0], 1, 2)
    rows, chans, cols = own.shape
    wide = padded_lanes(chans)
    deep = 9 * chans
    patches = lax.axis_size("patch")
    swap = [(0, 1), (1, 0)]
    line = lambda vector: vector.reshape(1, -1)

    tile_one = -(-3 * wide // LANES // 8) * 8
    held, sent, near_edge, next_edge = pl.pallas_call(
        stats_kernel,
        out_shape=[
            pltpu.VMEM((rows, chans, cols), BF16),
            pltpu.VMEM((2 * patches, tile_one, LANES), F32),
            pltpu.VMEM((REACH, chans, cols), BF16),
            pltpu.VMEM((REACH, chans, cols), BF16),
        ],
        in_specs=[ANY] * 3,
        out_specs=[VMEM] * 4,
        scratch_shapes=[
            pltpu.VMEM(time_embed.shape, BF16),
            pltpu.VMEM(time_weight.shape, BF16),
            pltpu.SemaphoreType.DMA((rows + 2,)),
            pltpu.SemaphoreType.DMA((2,)),
        ],
        compiler_params=LIMIT,
        name="stats",
    )(in_hbm(own), in_hbm(time_embed), in_hbm(time_weight))
    near = lax.ppermute(near_edge, "patch", [(i, i ^ 1) for i in range(patches)])
    steps = [(i, i + 1) for i in range(1, patches - 1, 2)]
    following = lax.ppermute(next_edge, "patch", steps + [(j, i) for i, j in steps])
    seen = everyone(sent, ("cfg", "patch"))

    weights = (conv_one.reshape(deep, chans), conv_two.reshape(deep, chans))
    *weights, _ = lax.optimization_barrier((*weights, sent))
    turned_one, turned_two, vectors = pl.pallas_call(
        prepare_kernel,
        out_shape=[pltpu.VMEM((chans, deep), BF16)] * 2 + [pltpu.VMEM((8, wide), F32)],
        in_specs=[ANY] * 2 + [VMEM] * 8,
        out_specs=[VMEM] * 3,
        scratch_shapes=[pltpu.VMEM((deep, chans), BF16)] * 2 + [pltpu.SemaphoreType.DMA((2 * PARTS,))],
        compiler_params=LIMIT,
        name="prepare",
    )(
        in_hbm(weights[0]), in_hbm(weights[1]), line(gain_one), line(shift_one), line(bias_one),
        line(time_bias), line(gain_two), line(shift_two), line(bias_two), line(steer_scale),
    )
    source, vectors = lax.optimization_barrier((own, vectors))
    far = lax.ppermute(source, "cfg", swap)
    near, following, vectors, seen = lax.optimization_barrier((near, following, vectors, seen))
    far_near = lax.ppermute(near, "cfg", swap)
    far_next = lax.ppermute(following, "cfg", swap)

    inner, taps, columns = pl.pallas_call(
        inner_kernel,
        out_shape=[
            pltpu.VMEM((max(rows - 2, 1), chans, cols), F32),
            pltpu.VMEM((rows * 3 * chans, cols), BF16),
            pltpu.VMEM((6, chans, LANES), F32),
        ],
        in_specs=[VMEM] * 5,
        out_specs=[VMEM] * 3,
        compiler_params=LIMIT,
        name="inner",
    )(held, far, seen, vectors, turned_one)
    tile_two = -(-2 * wide // LANES // 8) * 8
    outer, sent = pl.pallas_call(
        outer_kernel,
        out_shape=[
            pltpu.VMEM((2 * REACH, chans, cols), F32),
            pltpu.VMEM((patches, tile_two, LANES), F32),
        ],
        in_specs=[VMEM] * 9,
        out_specs=[VMEM] * 2,
        scratch_shapes=[
            pltpu.VMEM((2 * REACH * 3 * chans, cols), BF16),
            pltpu.VMEM((2, 2 * REACH, chans, cols), BF16),
        ],
        compiler_params=LIMIT,
        name="outer",
    )(near, following, far_near, far_next, inner, taps, columns, vectors, turned_one)
    seen = everyone(sent, "patch")
    image = pl.pallas_call(
        second_kernel,
        out_shape=jax.ShapeDtypeStruct((rows, chans, cols), BF16),
        in_specs=[VMEM] * 6,
        out_specs=VMEM,
        scratch_shapes=[
            pltpu.VMEM(((rows + 2) * 3 * chans, cols), BF16),
            pltpu.VMEM((4, chans, LANES), F32),
        ],
        compiler_params=LIMIT,
        name="second",
    )(inner, outer, held, seen, vectors, turned_two)
    return jnp.swapaxes(image, 1, 2)[None, None]


def solution(mesh):
    placed = (
        P("cfg", "req", "patch", None, None), P("req", None), P("req"), P(), P(), P(), P(),
        P("patch", None), P(), P(), P(), P(), P(),
    )
    return jax.shard_map(
        body,
        mesh=mesh,
        in_specs=placed,
        out_specs=P("cfg", "req", "patch", None, None),
        check_vma=False,
    )
```

```python
import functools

import jax
import jax.numpy as jnp
from jax import lax
from jax.experimental import pallas as pl
from jax.experimental.pallas import tpu as pltpu
from jax.sharding import PartitionSpec as P

GROUPS = 32
EPS = 1e-05
REACH = 2
LANES = 128
F32 = jnp.float32
BF16 = jnp.bfloat16


def padded_lanes(chans):
    return -(-chans // LANES) * LANES


def widen(row, wide):
    short = wide - row.shape[1]
    if not short:
        return row
    return jnp.concatenate([row, jnp.zeros((row.shape[0], short), row.dtype)], axis=1)


def same_group(wide, size):
    left = lax.broadcasted_iota(jnp.int32, (wide, wide), 0).astype(F32)
    right = lax.broadcasted_iota(jnp.int32, (wide, wide), 1).astype(F32)
    group = lambda at: jnp.floor((at + 0.5) * (1.0 / size))
    return jnp.where(group(left) == group(right), 1.0, 0.0).astype(BF16)


def group_sum(rows, mask):
    high = rows.astype(BF16).astype(F32)
    rest = rows - high
    middle = rest.astype(BF16).astype(F32)
    pieces = jnp.concatenate([high, middle, rest - middle, jnp.zeros_like(rows)], axis=0).astype(BF16)
    sums = jnp.dot(pieces, mask, preferred_element_type=F32)
    return sums[0:8] + sums[8:16] + sums[16:24]


def stack_rows(rows, wide):
    filler = [jnp.zeros((8 - len(rows), wide), F32)] if len(rows) < 8 else []
    return jnp.concatenate(list(rows) + filler, axis=0)


def group_stats(means, squares, count, mask, size):
    wide = mask.shape[0]
    peers = means[0].shape[0]
    mean_rows = [jnp.sum(m, axis=0, keepdims=True) * (1.0 / peers) for m in means]
    mean_rows = group_sum(stack_rows(mean_rows, wide), mask) * (1.0 / size)
    spread = []
    for k, (m, q) in enumerate(zip(means, squares)):
        off = m - mean_rows[k : k + 1]
        spread.append(jnp.sum(q + count * (off * off), axis=0, keepdims=True))
    var_rows = group_sum(stack_rows(spread, wide), mask) * (1.0 / (size * count * peers))
    return mean_rows, var_rows


def fold(values):
    total = values[:, :LANES]
    for at in range(LANES, values.shape[1], LANES):
        total = total + values[:, at : at + LANES]
    return total


def channel_moments(rows, chans):
    count = 0
    total = None
    for row in rows():
        part = fold(row)
        count += row.shape[1]
        total = part if total is None else total + part
    mean = jnp.sum(total, axis=1, keepdims=True) * (1.0 / count)
    squares = None
    for row in rows():
        off = row - mean
        part = fold(off * off)
        squares = part if squares is None else squares + part
    squares = jnp.sum(squares, axis=1, keepdims=True)
    lane = lax.broadcasted_iota(jnp.int32, (chans, LANES), 1)
    both = jnp.where(lane == 0, mean, jnp.where(lane == 1, squares, 0.0))
    wide = padded_lanes(chans)
    both = jnp.concatenate([both, jnp.zeros((wide - chans, LANES), F32)], axis=0)
    turned = both.T
    return turned[0:1, :chans], turned[1:2, :chans]


def put_rows(tile_rows, out_ref):
    height = out_ref.shape[1]
    flat = widen(jnp.concatenate(tile_rows, axis=1), height * LANES)
    tile = jnp.concatenate([flat[:, at : at + LANES] for at in range(0, height * LANES, LANES)], axis=0)
    out_ref[...] = jnp.broadcast_to(tile[None], out_ref.shape)


def get_rows(seen_ref, first, peers, which, chans):
    start, end = which * chans, (which + 1) * chans
    lines = range(start // LANES, -(-end // LANES))
    flat = jnp.concatenate([seen_ref[pl.ds(first, peers), k, :] for k in lines], axis=1)
    start -= lines[0] * LANES
    return widen(flat[:, start : start + chans], padded_lanes(chans))


def tile_height(chans, rows):
    return -(-rows * chans // LANES // 8) * 8


def stats_kernel(
    lat_hbm, embed_hbm, weight_hbm,
    lat_ref, out_ref, near_ref, next_ref,
    embed_ref, weight_ref, sems, edge_sems,
):
    rows, chans, _ = lat_ref.shape
    copies = [
        pltpu.make_async_copy(lat_hbm.at[k], lat_ref.at[k], sems.at[k]) for k in range(rows)
    ]
    copies.append(pltpu.make_async_copy(embed_hbm, embed_ref, sems.at[rows]))
    copies.append(pltpu.make_async_copy(weight_hbm, weight_ref, sems.at[rows + 1]))
    reach = near_ref.shape[0]
    last = rows - reach
    near_at = jnp.where(lax.rem(lax.axis_index("patch"), 2) == 0, last, 0)
    edges = [
        pltpu.make_async_copy(lat_hbm.at[pl.ds(near_at, reach)], near_ref, edge_sems.at[0]),
        pltpu.make_async_copy(lat_hbm.at[pl.ds(last - near_at, reach)], next_ref, edge_sems.at[1]),
    ]
    for copy in copies + edges:
        copy.start()
    waits = list(copies[:rows])

    def values():
        for k in range(rows):
            if waits:
                waits.pop(0).wait()
            yield lat_ref[k].astype(F32)

    mean, squares = channel_moments(values, chans)
    copies[rows].wait()
    copies[rows + 1].wait()
    own = weight_ref.shape[0]
    length = embed_ref.shape[1]
    embed = jnp.broadcast_to(embed_ref[...].astype(F32), (8, length))
    embed = pltpu.roll(embed, length - lax.axis_index("patch") * own, 1)[:, :own]
    act = (embed / (1.0 + jnp.exp(-embed))).astype(BF16)
    time_part = jnp.dot(act, weight_ref[...], preferred_element_type=F32)[0:1]
    put_rows([mean, squares, time_part], out_ref)
    for copy in edges:
        copy.wait()


def parts_of(deep, part=8 * LANES):
    return [(at, min(part, deep - at)) for at in range(0, deep, part)]


def fetch(pairs, sems, first=0):
    copies = [pltpu.make_async_copy(a, b, sems.at[first + k]) for k, (a, b) in enumerate(pairs)]
    for copy in copies:
        copy.start()
    return copies


def prepare_kernel(
    one_hbm, two_hbm, gain_one, shift_one, bias_one, time_bias, gain_two, shift_two, bias_two, steer,
    one_out, two_out, rows_ref, one_ref, two_ref, sems, row_sems, *vector_refs,
):
    vectors = (gain_one, shift_one, bias_one, time_bias, gain_two, shift_two, bias_two)
    lines = fetch(zip(vectors, vector_refs), row_sems)
    parts = parts_of(one_ref.shape[0])
    sides = ((one_hbm, one_ref, one_out), (two_hbm, two_ref, two_out))
    copies = [
        fetch([(a.at[pl.ds(*p)], b.at[pl.ds(*p)]) for p in parts], sems, k * len(parts))
        for k, (a, b, _) in enumerate(sides)
    ]
    for line in lines:
        line.wait()
    wide = rows_ref.shape[1]
    rows = [widen(v[...].reshape(1, -1), wide) for v in vector_refs]
    rows_ref[...] = jnp.concatenate(rows + [jnp.broadcast_to(steer[...], (1, wide))], axis=0)
    for waits, (_, held, target) in zip(copies, sides):
        for wait, (at, size) in zip(waits, parts):
            wait.wait()
            target[:, at : at + size] = held[at : at + size, :].T


def spread_columns(rows, chans, cols_ref):
    turned = stack_rows(rows, rows[0].shape[1]).T
    for k in range(len(rows)):
        cols_ref[k] = jnp.broadcast_to(turned[:chans, k : k + 1], (chans, LANES))


def half_act(values, mean, scale, shift):
    half = (values - mean) * scale + shift
    return half * jnp.tanh(half) + half


def twice(column):
    return jnp.concatenate([column, column], axis=1)


def put_taps(taps_ref, at, row):
    chans, cols = row.shape
    lane = lax.broadcasted_iota(jnp.int32, (chans, cols), 1)
    before = jnp.where(lane == 0, 0.0, pltpu.roll(row, 1, 1))
    after = jnp.where(lane == cols - 1, 0.0, pltpu.roll(row, cols - 1, 1))
    for k, value in enumerate((before, row, after)):
        taps_ref[pl.ds((at * 3 + k) * chans, chans), :] = value.astype(BF16)


def edge_keep(at, rows, reach):
    patch, patches = lax.axis_index("patch"), lax.axis_size("patch")
    if at < reach:
        return jnp.where(patch == 0, 0.0, 1.0).astype(F32)
    if at >= reach + rows:
        return jnp.where(patch == patches - 1, 0.0, 1.0).astype(F32)
    return None


def mixer(cols_ref, rows_ref, chans):
    sign = jnp.where(lax.axis_index("cfg") == 0, 1.0, -1.0).astype(F32)
    steer = rows_ref[7:8, 0:1] * sign

    def mix(mine, other):
        shift = twice(cols_ref[4])
        mine = half_act(mine.astype(F32), twice(cols_ref[0]), twice(cols_ref[1]), shift)
        other = half_act(other.astype(F32), twice(cols_ref[2]), twice(cols_ref[3]), shift)
        return mine + steer * (mine - other)

    return mix


def matmul(weight_ref, taps, first_tap):
    depth = taps.shape[0]
    start = first_tap * (weight_ref.shape[1] // 3)
    return jnp.dot(weight_ref[:, start : start + depth], taps, preferred_element_type=F32)


def inner_kernel(
    own_ref, far_ref, seen_ref, rows_ref, weight_ref,
    steered_ref, taps_ref, cols_ref,
):
    rows, chans, cols = own_ref.shape
    wide = padded_lanes(chans)
    size = chans // GROUPS
    cfg, peers = lax.axis_index("cfg"), lax.axis_size("patch")
    mask = same_group(wide, size)
    starts = (cfg * peers, (1 - cfg) * peers)
    means = [get_rows(seen_ref, s, peers, 0, chans) for s in starts]
    squares = [get_rows(seen_ref, s, peers, 1, chans) for s in starts]
    mean_rows, var_rows = group_stats(means, squares, float(rows * cols), mask, size)
    scale_rows = lax.rsqrt(var_rows + EPS) * (0.5 * rows_ref[0:1])
    times = jnp.sum(get_rows(seen_ref, 0, peers, 2, chans), axis=0, keepdims=True)
    added = times + (rows_ref[3:4] + rows_ref[2:3])
    spread_columns(
        [mean_rows[0:1], scale_rows[0:1], mean_rows[1:2], scale_rows[1:2], 0.5 * rows_ref[1:2], added],
        chans, cols_ref,
    )
    mix = mixer(cols_ref, rows_ref, chans)
    line = 3 * chans
    if rows < 3:
        steered_ref[...] = jnp.zeros_like(steered_ref)
    for at in range(rows):
        put_taps(taps_ref, at, mix(own_ref[at], far_ref[at]))
        if at >= 2:
            total = matmul(weight_ref, taps_ref[(at - 2) * line : (at + 1) * line, :], 0)
            steered_ref[at - 2] = total + twice(cols_ref[5])


def outer_kernel(
    near_ref, next_ref, far_near_ref, far_next_ref, inner_ref, inner_taps_ref, cols_ref, rows_ref, weight_ref,
    steered_ref, out_ref,
    taps_ref, edge_ref,
):
    reach, chans, cols = near_ref.shape
    line = 3 * chans
    rows = inner_taps_ref.shape[0] // line
    above = jnp.where(lax.rem(lax.axis_index("patch"), 2) == 0, reach, 0)
    edge_ref[0, pl.ds(above, reach)] = next_ref[...]
    edge_ref[1, pl.ds(above, reach)] = far_next_ref[...]
    edge_ref[0, pl.ds(reach - above, reach)] = near_ref[...]
    edge_ref[1, pl.ds(reach - above, reach)] = far_near_ref[...]
    mix = mixer(cols_ref, rows_ref, chans)

    def taps(at):
        if reach <= at < reach + rows:
            return inner_taps_ref, at - reach
        return taps_ref, at if at < reach else at - rows

    def rows_of(first, count):
        ref, at = taps(first)
        return ref[at * line : (at + count) * line, :]

    def conv(at):
        total, tap = None, 0
        while tap < 3:
            ref, _ = taps(at + tap)
            count = 1
            while tap + count < 3 and taps(at + tap + count)[0] is ref:
                count += 1
            part = matmul(weight_ref, rows_of(at + tap, count), tap)
            total = part if total is None else total + part
            tap += count
        return total

    def enter(at):
        k = reach + at if at < reach else at - reach - rows
        keep = edge_keep(at, rows, reach)
        put_taps(taps_ref, taps(at)[1], mix(edge_ref[0, k], edge_ref[1, k]) * keep)

    for at in range(reach):
        enter(at)
    outside = [at for at in range(rows + 2 * reach - 2) if not reach <= at < reach + rows - 2]
    place = {at: k for k, at in enumerate(outside)}
    ready = reach + rows
    for at in outside:
        while ready < at + 3:
            enter(ready)
            ready += 1
        steered_ref[place[at]] = conv(at) + twice(cols_ref[5])

    def own_rows():
        for k in range(rows):
            at = reach - 1 + k
            yield steered_ref[place[at]] if at in place else inner_ref[at - reach]

    mean, square = channel_moments(own_rows, chans)
    put_rows([mean, square], out_ref)


def second_kernel(
    inner_ref, outer_ref, lat_ref, seen_ref, rows_ref, weight_ref,
    out_ref,
    taps_ref, cols_ref,
):
    rows, chans, cols = lat_ref.shape
    wide = padded_lanes(chans)
    size = chans // GROUPS
    peers = lax.axis_size("patch")
    mask = same_group(wide, size)
    mean_rows, var_rows = group_stats(
        [get_rows(seen_ref, 0, peers, 0, chans)], [get_rows(seen_ref, 0, peers, 1, chans)],
        float(rows * cols), mask, size,
    )
    scale_rows = lax.rsqrt(var_rows + EPS) * (0.5 * rows_ref[4:5])
    spread_columns(
        [mean_rows[0:1], scale_rows[0:1], 0.5 * rows_ref[5:6], rows_ref[6:7]], chans, cols_ref
    )
    line = 3 * chans
    inside = max(rows - 2, 0)
    half = outer_ref.shape[0] // 2
    for at in range(rows + 2):
        if half <= at < half + inside:
            value = inner_ref[at - half]
        else:
            value = outer_ref[at if at < half else at - inside]
        value = half_act(value, twice(cols_ref[0]), twice(cols_ref[1]), twice(cols_ref[2]))
        keep = edge_keep(at, rows, 1)
        put_taps(taps_ref, at, value if keep is None else value * keep)
        if at >= 2:
            total = matmul(weight_ref, taps_ref[(at - 2) * line : (at + 1) * line, :], 0)
            out_ref[at - 2] = (lat_ref[at - 2].astype(F32) + (total + twice(cols_ref[3]))).astype(BF16)


def everyone(tiles, axes):
    return lax.all_to_all(tiles, axes, 0, 0)


VMEM = pl.BlockSpec(memory_space=pltpu.VMEM)
ANY = pl.BlockSpec(memory_space=pl.ANY)
LIMIT = pltpu.CompilerParams(vmem_limit_bytes=12 * 1024 * 1024)


def in_hbm(value):
    return pltpu.with_memory_space_constraint(value, pltpu.HBM)


def body(
    latents, time_embed, steer_scale, gain_one, shift_one, conv_one, bias_one,
    time_weight, time_bias, gain_two, shift_two, conv_two, bias_two,
):
    own = jnp.swapaxes(latents[0, 0], 1, 2)
    rows, chans, cols = own.shape
    wide = padded_lanes(chans)
    deep = 9 * chans
    patches = lax.axis_size("patch")
    swap = [(0, 1), (1, 0)]
    line = lambda vector: vector.reshape(1, -1)

    tile_one = tile_height(chans, 3)
    held, sent, near_edge, next_edge = pl.pallas_call(
        stats_kernel,
        out_shape=[
            pltpu.VMEM((rows, chans, cols), BF16),
            pltpu.VMEM((2 * patches, tile_one, LANES), F32),
            pltpu.VMEM((REACH, chans, cols), BF16),
            pltpu.VMEM((REACH, chans, cols), BF16),
        ],
        in_specs=[ANY] * 3,
        out_specs=[VMEM] * 4,
        scratch_shapes=[
            pltpu.VMEM(time_embed.shape, BF16),
            pltpu.VMEM(time_weight.shape, BF16),
            pltpu.SemaphoreType.DMA((rows + 2,)),
            pltpu.SemaphoreType.DMA((2,)),
        ],
        compiler_params=LIMIT,
        name="stats",
    )(in_hbm(own), in_hbm(time_embed), in_hbm(time_weight))
    near = lax.ppermute(near_edge, "patch", [(i, i ^ 1) for i in range(patches)])
    steps = [(i, i + 1) for i in range(1, patches - 1, 2)]
    following = lax.ppermute(next_edge, "patch", steps + [(j, i) for i, j in steps])
    seen = everyone(sent, ("cfg", "patch"))

    weights = (conv_one.reshape(deep, chans), conv_two.reshape(deep, chans))
    source, *weights, _ = lax.optimization_barrier((own, *weights, sent))
    turned_one, turned_two, vectors = pl.pallas_call(
        prepare_kernel,
        out_shape=[pltpu.VMEM((chans, deep), BF16)] * 2 + [pltpu.VMEM((8, wide), F32)],
        in_specs=[ANY] * 9 + [VMEM],
        out_specs=[VMEM] * 3,
        scratch_shapes=[pltpu.VMEM((deep, chans), BF16)] * 2
        + [pltpu.SemaphoreType.DMA((2 * len(parts_of(deep)),)), pltpu.SemaphoreType.DMA((7,))]
        + [pltpu.VMEM((chans,), F32)] * 7,
        compiler_params=LIMIT,
        name="prepare",
    )(
        in_hbm(weights[0]), in_hbm(weights[1]), in_hbm(gain_one), in_hbm(shift_one), in_hbm(bias_one),
        in_hbm(time_bias), in_hbm(gain_two), in_hbm(shift_two), in_hbm(bias_two), line(steer_scale),
    )
    far = lax.ppermute(source, "cfg", swap)
    near, following, vectors, seen = lax.optimization_barrier((near, following, vectors, seen))
    far_near = lax.ppermute(near, "cfg", swap)
    far_next = lax.ppermute(following, "cfg", swap)

    inner, taps, columns = pl.pallas_call(
        inner_kernel,
        out_shape=[
            pltpu.VMEM((max(rows - 2, 1), chans, cols), F32),
            pltpu.VMEM((rows * 3 * chans, cols), BF16),
            pltpu.VMEM((6, chans, LANES), F32),
        ],
        in_specs=[VMEM] * 5,
        out_specs=[VMEM] * 3,
        compiler_params=LIMIT,
        name="inner",
    )(held, far, seen, vectors, turned_one)
    tile_two = tile_height(chans, 2)
    outer, sent = pl.pallas_call(
        outer_kernel,
        out_shape=[
            pltpu.VMEM((2 * REACH, chans, cols), F32),
            pltpu.VMEM((patches, tile_two, LANES), F32),
        ],
        in_specs=[VMEM] * 9,
        out_specs=[VMEM] * 2,
        scratch_shapes=[
            pltpu.VMEM((2 * REACH * 3 * chans, cols), BF16),
            pltpu.VMEM((2, 2 * REACH, chans, cols), BF16),
        ],
        compiler_params=LIMIT,
        name="outer",
    )(near, following, far_near, far_next, inner, taps, columns, vectors, turned_one)
    seen = everyone(sent, "patch")
    image = pl.pallas_call(
        second_kernel,
        out_shape=jax.ShapeDtypeStruct((rows, chans, cols), BF16),
        in_specs=[VMEM] * 6,
        out_specs=VMEM,
        scratch_shapes=[
            pltpu.VMEM(((rows + 2) * 3 * chans, cols), BF16),
            pltpu.VMEM((4, chans, LANES), F32),
        ],
        compiler_params=LIMIT,
        name="second",
    )(inner, outer, held, seen, vectors, turned_two)
    return jnp.swapaxes(image, 1, 2)[None, None]


def solution(mesh):
    placed = (
        P("cfg", "req", "patch", None, None), P("req", None), P("req"), P(), P(), P(), P(),
        P("patch", None), P(), P(), P(), P(), P(),
    )
    return jax.shard_map(
        body,
        mesh=mesh,
        in_specs=placed,
        out_specs=P("cfg", "req", "patch", None, None),
        check_vma=False,
    )
```

```python
import functools

import jax
import jax.numpy as jnp
from jax import lax
from jax.experimental import pallas as pl
from jax.experimental.pallas import tpu as pltpu
from jax.sharding import PartitionSpec as P

GROUPS = 32
EPS = 1e-05
REACH = 2
LANES = 128
F32 = jnp.float32
BF16 = jnp.bfloat16


def padded_lanes(chans):
    return -(-chans // LANES) * LANES


def widen(row, wide):
    short = wide - row.shape[1]
    if not short:
        return row
    return jnp.concatenate([row, jnp.zeros((row.shape[0], short), row.dtype)], axis=1)


def same_group(wide, size):
    left = lax.broadcasted_iota(jnp.int32, (wide, wide), 0).astype(F32)
    right = lax.broadcasted_iota(jnp.int32, (wide, wide), 1).astype(F32)
    group = lambda at: jnp.floor((at + 0.5) * (1.0 / size))
    return jnp.where(group(left) == group(right), 1.0, 0.0).astype(BF16)


def group_sum(rows, mask):
    high = rows.astype(BF16).astype(F32)
    rest = rows - high
    middle = rest.astype(BF16).astype(F32)
    pieces = jnp.concatenate([high, middle, rest - middle, jnp.zeros_like(rows)], axis=0).astype(BF16)
    sums = jnp.dot(pieces, mask, preferred_element_type=F32)
    return sums[0:8] + sums[8:16] + sums[16:24]


def stack_rows(rows, wide):
    filler = [jnp.zeros((8 - len(rows), wide), F32)] if len(rows) < 8 else []
    return jnp.concatenate(list(rows) + filler, axis=0)


def group_stats(means, squares, count, mask, size):
    wide = mask.shape[0]
    peers = means[0].shape[0]
    mean_rows = [jnp.sum(m, axis=0, keepdims=True) * (1.0 / peers) for m in means]
    mean_rows = group_sum(stack_rows(mean_rows, wide), mask) * (1.0 / size)
    spread = []
    for k, (m, q) in enumerate(zip(means, squares)):
        off = m - mean_rows[k : k + 1]
        spread.append(jnp.sum(q + count * (off * off), axis=0, keepdims=True))
    var_rows = group_sum(stack_rows(spread, wide), mask) * (1.0 / (size * count * peers))
    return mean_rows, var_rows


def fold(values):
    total = values[:, :LANES]
    for at in range(LANES, values.shape[1], LANES):
        total = total + values[:, at : at + LANES]
    return total


def channel_moments(rows, chans):
    count = 0
    total = None
    for row in rows():
        part = fold(row)
        count += row.shape[1]
        total = part if total is None else total + part
    mean = jnp.sum(total, axis=1, keepdims=True) * (1.0 / count)
    squares = None
    for row in rows():
        off = row - mean
        part = fold(off * off)
        squares = part if squares is None else squares + part
    squares = jnp.sum(squares, axis=1, keepdims=True)
    lane = lax.broadcasted_iota(jnp.int32, (chans, LANES), 1)
    both = jnp.where(lane == 0, mean, jnp.where(lane == 1, squares, 0.0))
    wide = padded_lanes(chans)
    both = jnp.concatenate([both, jnp.zeros((wide - chans, LANES), F32)], axis=0)
    turned = both.T
    return turned[0:1, :chans], turned[1:2, :chans]


def put_rows(tile_rows, out_ref):
    height = out_ref.shape[1]
    flat = widen(jnp.concatenate(tile_rows, axis=1), height * LANES)
    tile = jnp.concatenate([flat[:, at : at + LANES] for at in range(0, height * LANES, LANES)], axis=0)
    out_ref[...] = jnp.broadcast_to(tile[None], out_ref.shape)


def get_rows(seen_ref, first, peers, which, chans):
    start, end = which * chans, (which + 1) * chans
    lines = range(start // LANES, -(-end // LANES))
    flat = jnp.concatenate([seen_ref[pl.ds(first, peers), k, :] for k in lines], axis=1)
    start -= lines[0] * LANES
    return widen(flat[:, start : start + chans], padded_lanes(chans))


def tile_height(chans, rows):
    return -(-rows * chans // LANES // 8) * 8


def fetch(pairs, sems, first=0):
    copies = [pltpu.make_async_copy(a, b, sems.at[first + k]) for k, (a, b) in enumerate(pairs)]
    for copy in copies:
        copy.start()
    return copies


def stats_kernel(
    lat_hbm, embed_hbm, weight_hbm,
    out_ref, near_hbm, next_hbm,
    lat_ref, embed_ref, weight_ref, sems, edge_sems,
):
    rows, chans, _ = lat_ref.shape
    reach = near_hbm.shape[0]
    last = rows - reach
    near_at = jnp.where(lax.rem(lax.axis_index("patch"), 2) == 0, last, 0)
    copies = fetch(
        [(lat_hbm.at[k], lat_ref.at[k]) for k in range(rows)]
        + [(embed_hbm, embed_ref), (weight_hbm, weight_ref)],
        sems,
    )
    edges = []
    waits = list(copies[:rows])

    def values():
        for k in range(rows):
            if waits:
                waits.pop(0).wait()
                if not waits:
                    edges.extend(
                        fetch(
                            [
                                (lat_ref.at[pl.ds(near_at, reach)], near_hbm),
                                (lat_ref.at[pl.ds(last - near_at, reach)], next_hbm),
                            ],
                            edge_sems,
                        )
                    )
            yield lat_ref[k].astype(F32)

    mean, squares = channel_moments(values, chans)
    copies[rows].wait()
    copies[rows + 1].wait()
    own = weight_ref.shape[0]
    length = embed_ref.shape[1]
    embed = jnp.broadcast_to(embed_ref[...].astype(F32), (8, length))
    embed = pltpu.roll(embed, length - lax.axis_index("patch") * own, 1)[:, :own]
    act = (embed / (1.0 + jnp.exp(-embed))).astype(BF16)
    time_part = jnp.dot(act, weight_ref[...], preferred_element_type=F32)[0:1]
    put_rows([mean, squares, time_part], out_ref)
    for copy in edges:
        copy.wait()


def parts_of(deep, part=8 * LANES):
    return [(at, min(part, deep - at)) for at in range(0, deep, part)]


def prepare_kernel(
    one_hbm, two_hbm, gain_one, shift_one, bias_one, time_bias, gain_two, shift_two, bias_two, steer,
    one_out, two_hbm_out, rows_ref, one_ref, two_ref, two_out, sems, row_sems, out_sem, *vector_refs,
):
    vectors = (gain_one, shift_one, bias_one, time_bias, gain_two, shift_two, bias_two)
    lines = fetch(zip(vectors, vector_refs), row_sems)
    parts = parts_of(one_ref.shape[0])
    sides = ((two_hbm, two_ref, two_out), (one_hbm, one_ref, one_out))
    copies = [
        fetch([(a.at[pl.ds(*p)], b.at[pl.ds(*p)]) for p in parts], sems, k * len(parts))
        for k, (a, b, _) in enumerate(sides)
    ]
    for line in lines:
        line.wait()
    wide = rows_ref.shape[1]
    rows = [widen(v[...].reshape(1, -1), wide) for v in vector_refs]
    rows_ref[...] = jnp.concatenate(rows + [jnp.broadcast_to(steer[...], (1, wide))], axis=0)
    for waits, (_, held, target) in zip(copies, sides):
        for wait, (at, size) in zip(waits, parts):
            wait.wait()
            target[:, at : at + size] = held[at : at + size, :].T
        if target is two_out:
            out = pltpu.make_async_copy(two_out, two_hbm_out, out_sem)
            out.start()
    out.wait()


def spread_columns(rows, chans, cols_ref):
    turned = stack_rows(rows, rows[0].shape[1]).T
    for k in range(len(rows)):
        cols_ref[k] = jnp.broadcast_to(turned[:chans, k : k + 1], (chans, LANES))


def half_act(values, mean, scale, shift):
    half = (values - mean) * scale + shift
    return half * jnp.tanh(half) + half


def twice(column):
    return jnp.concatenate([column, column], axis=1)


def put_taps(taps_ref, at, row):
    chans, cols = row.shape
    lane = lax.broadcasted_iota(jnp.int32, (chans, cols), 1)
    before = jnp.where(lane == 0, 0.0, pltpu.roll(row, 1, 1))
    after = jnp.where(lane == cols - 1, 0.0, pltpu.roll(row, cols - 1, 1))
    for k, value in enumerate((before, row, after)):
        taps_ref[pl.ds((at * 3 + k) * chans, chans), :] = value.astype(BF16)


def edge_keep(at, rows, reach):
    patch, patches = lax.axis_index("patch"), lax.axis_size("patch")
    if at < reach:
        return jnp.where(patch == 0, 0.0, 1.0).astype(F32)
    if at >= reach + rows:
        return jnp.where(patch == patches - 1, 0.0, 1.0).astype(F32)
    return None


def mixer(cols_ref, rows_ref, chans):
    sign = jnp.where(lax.axis_index("cfg") == 0, 1.0, -1.0).astype(F32)
    steer = rows_ref[7:8, 0:1] * sign

    def mix(mine, other):
        shift = twice(cols_ref[4])
        mine = half_act(mine.astype(F32), twice(cols_ref[0]), twice(cols_ref[1]), shift)
        other = half_act(other.astype(F32), twice(cols_ref[2]), twice(cols_ref[3]), shift)
        return mine + steer * (mine - other)

    return mix


def matmul(weight_ref, taps, first_tap):
    depth = taps.shape[0]
    start = first_tap * (weight_ref.shape[1] // 3)
    return jnp.dot(weight_ref[:, start : start + depth], taps, preferred_element_type=F32)


def inner_kernel(
    own_hbm, far_ref, seen_ref, rows_ref, weight_ref,
    steered_ref, taps_ref, cols_ref,
    own_ref, sems,
):
    rows, chans, cols = own_ref.shape
    copies = fetch([(own_hbm.at[k], own_ref.at[k]) for k in range(rows)], sems)
    wide = padded_lanes(chans)
    size = chans // GROUPS
    cfg, peers = lax.axis_index("cfg"), lax.axis_size("patch")
    mask = same_group(wide, size)
    starts = (cfg * peers, (1 - cfg) * peers)
    means = [get_rows(seen_ref, s, peers, 0, chans) for s in starts]
    squares = [get_rows(seen_ref, s, peers, 1, chans) for s in starts]
    mean_rows, var_rows = group_stats(means, squares, float(rows * cols), mask, size)
    scale_rows = lax.rsqrt(var_rows + EPS) * (0.5 * rows_ref[0:1])
    times = jnp.sum(get_rows(seen_ref, 0, peers, 2, chans), axis=0, keepdims=True)
    added = times + (rows_ref[3:4] + rows_ref[2:3])
    spread_columns(
        [mean_rows[0:1], scale_rows[0:1], mean_rows[1:2], scale_rows[1:2], 0.5 * rows_ref[1:2], added],
        chans, cols_ref,
    )
    mix = mixer(cols_ref, rows_ref, chans)
    line = 3 * chans
    if rows < 3:
        steered_ref[...] = jnp.zeros_like(steered_ref)
    for at in range(rows):
        copies[at].wait()
        put_taps(taps_ref, at, mix(own_ref[at], far_ref[at]))
        if at >= 2:
            total = matmul(weight_ref, taps_ref[(at - 2) * line : (at + 1) * line, :], 0)
            steered_ref[at - 2] = total + twice(cols_ref[5])


def outer_kernel(
    near_ref, next_ref, far_near_ref, far_next_ref, inner_ref, inner_taps_ref, cols_ref, rows_ref, weight_ref,
    steered_ref, out_ref,
    taps_ref, edge_ref,
):
    reach, chans, cols = near_ref.shape
    line = 3 * chans
    rows = inner_taps_ref.shape[0] // line
    above = jnp.where(lax.rem(lax.axis_index("patch"), 2) == 0, reach, 0)
    edge_ref[0, pl.ds(above, reach)] = next_ref[...]
    edge_ref[1, pl.ds(above, reach)] = far_next_ref[...]
    edge_ref[0, pl.ds(reach - above, reach)] = near_ref[...]
    edge_ref[1, pl.ds(reach - above, reach)] = far_near_ref[...]
    mix = mixer(cols_ref, rows_ref, chans)

    def taps(at):
        if reach <= at < reach + rows:
            return inner_taps_ref, at - reach
        return taps_ref, at if at < reach else at - rows

    def rows_of(first, count):
        ref, at = taps(first)
        return ref[at * line : (at + count) * line, :]

    def conv(at):
        total, tap = None, 0
        while tap < 3:
            ref, _ = taps(at + tap)
            count = 1
            while tap + count < 3 and taps(at + tap + count)[0] is ref:
                count += 1
            part = matmul(weight_ref, rows_of(at + tap, count), tap)
            total = part if total is None else total + part
            tap += count
        return total

    def enter(at):
        k = reach + at if at < reach else at - reach - rows
        keep = edge_keep(at, rows, reach)
        put_taps(taps_ref, taps(at)[1], mix(edge_ref[0, k], edge_ref[1, k]) * keep)

    for at in range(reach):
        enter(at)
    outside = [at for at in range(rows + 2 * reach - 2) if not reach <= at < reach + rows - 2]
    place = {at: k for k, at in enumerate(outside)}
    ready = reach + rows
    for at in outside:
        while ready < at + 3:
            enter(ready)
            ready += 1
        steered_ref[place[at]] = conv(at) + twice(cols_ref[5])

    def own_rows():
        for k in range(rows):
            at = reach - 1 + k
            yield steered_ref[place[at]] if at in place else inner_ref[at - reach]

    mean, square = channel_moments(own_rows, chans)
    put_rows([mean, square], out_ref)


def second_kernel(
    inner_ref, outer_ref, lat_hbm, seen_ref, rows_ref, weight_ref,
    out_hbm,
    taps_ref, cols_ref, lat_ref, out_ref, sems, out_sems,
):
    rows, chans, cols = lat_ref.shape
    copies = fetch([(lat_hbm.at[k], lat_ref.at[k]) for k in range(rows)], sems)
    outs = []
    wide = padded_lanes(chans)
    size = chans // GROUPS
    peers = lax.axis_size("patch")
    mask = same_group(wide, size)
    mean_rows, var_rows = group_stats(
        [get_rows(seen_ref, 0, peers, 0, chans)], [get_rows(seen_ref, 0, peers, 1, chans)],
        float(rows * cols), mask, size,
    )
    scale_rows = lax.rsqrt(var_rows + EPS) * (0.5 * rows_ref[4:5])
    spread_columns(
        [mean_rows[0:1], scale_rows[0:1], 0.5 * rows_ref[5:6], rows_ref[6:7]], chans, cols_ref
    )
    line = 3 * chans
    inside = max(rows - 2, 0)
    half = outer_ref.shape[0] // 2
    for at in range(rows + 2):
        if half <= at < half + inside:
            value = inner_ref[at - half]
        else:
            value = outer_ref[at if at < half else at - inside]
        value = half_act(value, twice(cols_ref[0]), twice(cols_ref[1]), twice(cols_ref[2]))
        keep = edge_keep(at, rows, 1)
        put_taps(taps_ref, at, value if keep is None else value * keep)
        if at >= 2:
            total = matmul(weight_ref, taps_ref[(at - 2) * line : (at + 1) * line, :], 0)
            copies[at - 2].wait()
            out_ref[at - 2] = (lat_ref[at - 2].astype(F32) + (total + twice(cols_ref[3]))).astype(BF16)
            outs += fetch([(out_ref.at[at - 2], out_hbm.at[at - 2])], out_sems, at - 2)
    for copy in outs:
        copy.wait()


def everyone(tiles, axes):
    return lax.all_to_all(tiles, axes, 0, 0)


VMEM = pl.BlockSpec(memory_space=pltpu.VMEM)
ANY = pl.BlockSpec(memory_space=pl.ANY)
LIMIT = pltpu.CompilerParams(vmem_limit_bytes=12 * 1024 * 1024)


def in_hbm(value):
    return pltpu.with_memory_space_constraint(value, pltpu.HBM)


def body(
    latents, time_embed, steer_scale, gain_one, shift_one, conv_one, bias_one,
    time_weight, time_bias, gain_two, shift_two, conv_two, bias_two,
):
    own = jnp.swapaxes(latents[0, 0], 1, 2)
    rows, chans, cols = own.shape
    wide = padded_lanes(chans)
    deep = 9 * chans
    patches = lax.axis_size("patch")
    swap = [(0, 1), (1, 0)]
    line = lambda vector: vector.reshape(1, -1)

    tile_one = tile_height(chans, 3)
    sent, near_edge, next_edge = pl.pallas_call(
        stats_kernel,
        out_shape=[
            pltpu.VMEM((2 * patches, tile_one, LANES), F32),
            pltpu.HBM((REACH, chans, cols), BF16),
            pltpu.HBM((REACH, chans, cols), BF16),
        ],
        in_specs=[ANY] * 3,
        out_specs=[VMEM, ANY, ANY],
        scratch_shapes=[
            pltpu.VMEM((rows, chans, cols), BF16),
            pltpu.VMEM(time_embed.shape, BF16),
            pltpu.VMEM(time_weight.shape, BF16),
            pltpu.SemaphoreType.DMA((rows + 2,)),
            pltpu.SemaphoreType.DMA((2,)),
        ],
        compiler_params=LIMIT,
        name="stats",
    )(in_hbm(own), in_hbm(time_embed), in_hbm(time_weight))
    near = lax.ppermute(near_edge, "patch", [(i, i ^ 1) for i in range(patches)])
    steps = [(i, i + 1) for i in range(1, patches - 1, 2)]
    following = lax.ppermute(next_edge, "patch", steps + [(j, i) for i, j in steps])
    seen = everyone(sent, ("cfg", "patch"))

    weights = (conv_one.reshape(deep, chans), conv_two.reshape(deep, chans))
    source, *weights, _ = lax.optimization_barrier((own, *weights, sent))
    turned_one, turned_two, vectors = pl.pallas_call(
        prepare_kernel,
        out_shape=[
            pltpu.VMEM((chans, deep), BF16), pltpu.HBM((chans, deep), BF16), pltpu.VMEM((8, wide), F32),
        ],
        in_specs=[ANY] * 9 + [VMEM],
        out_specs=[VMEM, ANY, VMEM],
        scratch_shapes=[pltpu.VMEM((deep, chans), BF16)] * 2 + [pltpu.VMEM((chans, deep), BF16)]
        + [pltpu.SemaphoreType.DMA((2 * len(parts_of(deep)),)), pltpu.SemaphoreType.DMA((7,))]
        + [pltpu.SemaphoreType.DMA]
        + [pltpu.VMEM((chans,), F32)] * 7,
        compiler_params=LIMIT,
        name="prepare",
    )(
        in_hbm(weights[0]), in_hbm(weights[1]), in_hbm(gain_one), in_hbm(shift_one), in_hbm(bias_one),
        in_hbm(time_bias), in_hbm(gain_two), in_hbm(shift_two), in_hbm(bias_two), line(steer_scale),
    )
    far = lax.ppermute(source, "cfg", swap)
    near, following, vectors, seen = lax.optimization_barrier((near, following, vectors, seen))
    far_near = lax.ppermute(near, "cfg", swap)
    far_next = lax.ppermute(following, "cfg", swap)

    inner, taps, columns = pl.pallas_call(
        inner_kernel,
        out_shape=[
            pltpu.VMEM((max(rows - 2, 1), chans, cols), F32),
            pltpu.VMEM((rows * 3 * chans, cols), BF16),
            pltpu.VMEM((6, chans, LANES), F32),
        ],
        in_specs=[ANY] + [VMEM] * 4,
        out_specs=[VMEM] * 3,
        scratch_shapes=[pltpu.VMEM((rows, chans, cols), BF16), pltpu.SemaphoreType.DMA((rows,))],
        compiler_params=LIMIT,
        name="inner",
    )(in_hbm(own), far, seen, vectors, turned_one)
    tile_two = tile_height(chans, 2)
    outer, sent = pl.pallas_call(
        outer_kernel,
        out_shape=[
            pltpu.VMEM((2 * REACH, chans, cols), F32),
            pltpu.VMEM((patches, tile_two, LANES), F32),
        ],
        in_specs=[VMEM] * 9,
        out_specs=[VMEM] * 2,
        scratch_shapes=[
            pltpu.VMEM((2 * REACH * 3 * chans, cols), BF16),
            pltpu.VMEM((2, 2 * REACH, chans, cols), BF16),
        ],
        compiler_params=LIMIT,
        name="outer",
    )(near, following, far_near, far_next, inner, taps, columns, vectors, turned_one)
    seen = everyone(sent, "patch")
    image = pl.pallas_call(
        second_kernel,
        out_shape=pltpu.HBM((rows, chans, cols), BF16),
        in_specs=[VMEM] * 2 + [ANY] + [VMEM] * 3,
        out_specs=ANY,
        scratch_shapes=[
            pltpu.VMEM(((rows + 2) * 3 * chans, cols), BF16),
            pltpu.VMEM((4, chans, LANES), F32),
            pltpu.VMEM((rows, chans, cols), BF16),
            pltpu.VMEM((rows, chans, cols), BF16),
            pltpu.SemaphoreType.DMA((rows,)),
            pltpu.SemaphoreType.DMA((rows,)),
        ],
        compiler_params=LIMIT,
        name="second",
    )(inner, outer, in_hbm(own), seen, vectors, turned_two)
    return jnp.swapaxes(image, 1, 2)[None, None]


def solution(mesh):
    placed = (
        P("cfg", "req", "patch", None, None), P("req", None), P("req"), P(), P(), P(), P(),
        P("patch", None), P(), P(), P(), P(), P(),
    )
    return jax.shard_map(
        body,
        mesh=mesh,
        in_specs=placed,
        out_specs=P("cfg", "req", "patch", None, None),
        check_vma=False,
    )
```

```python
import functools

import jax
import jax.numpy as jnp
from jax import lax
from jax.experimental import pallas as pl
from jax.experimental.pallas import tpu as pltpu
from jax.sharding import PartitionSpec as P

GROUPS = 32
EPS = 1e-05
REACH = 2
LANES = 128
F32 = jnp.float32
BF16 = jnp.bfloat16


def padded_lanes(chans):
    return -(-chans // LANES) * LANES


def widen(row, wide):
    short = wide - row.shape[1]
    if not short:
        return row
    return jnp.concatenate([row, jnp.zeros((row.shape[0], short), row.dtype)], axis=1)


def same_group(wide, size):
    left = lax.broadcasted_iota(jnp.int32, (wide, wide), 0).astype(F32)
    right = lax.broadcasted_iota(jnp.int32, (wide, wide), 1).astype(F32)
    group = lambda at: jnp.floor((at + 0.5) * (1.0 / size))
    return jnp.where(group(left) == group(right), 1.0, 0.0).astype(BF16)


def group_sum(rows, mask):
    high = rows.astype(BF16).astype(F32)
    rest = rows - high
    middle = rest.astype(BF16).astype(F32)
    pieces = jnp.concatenate([high, middle, rest - middle, jnp.zeros_like(rows)], axis=0).astype(BF16)
    sums = jnp.dot(pieces, mask, preferred_element_type=F32)
    return sums[0:8] + sums[8:16] + sums[16:24]


def stack_rows(rows, wide):
    filler = [jnp.zeros((8 - len(rows), wide), F32)] if len(rows) < 8 else []
    return jnp.concatenate(list(rows) + filler, axis=0)


def group_stats(means, squares, count, mask, size):
    wide = mask.shape[0]
    peers = means[0].shape[0]
    mean_rows = [jnp.sum(m, axis=0, keepdims=True) * (1.0 / peers) for m in means]
    mean_rows = group_sum(stack_rows(mean_rows, wide), mask) * (1.0 / size)
    spread = []
    for k, (m, q) in enumerate(zip(means, squares)):
        off = m - mean_rows[k : k + 1]
        spread.append(jnp.sum(q + count * (off * off), axis=0, keepdims=True))
    var_rows = group_sum(stack_rows(spread, wide), mask) * (1.0 / (size * count * peers))
    return mean_rows, var_rows


def fold(values):
    total = values[:, :LANES]
    for at in range(LANES, values.shape[1], LANES):
        total = total + values[:, at : at + LANES]
    return total


def channel_moments(rows, chans):
    count = 0
    total = None
    for row in rows():
        part = fold(row)
        count += row.shape[1]
        total = part if total is None else total + part
    mean = jnp.sum(total, axis=1, keepdims=True) * (1.0 / count)
    squares = None
    for row in rows():
        off = row - mean
        part = fold(off * off)
        squares = part if squares is None else squares + part
    squares = jnp.sum(squares, axis=1, keepdims=True)
    lane = lax.broadcasted_iota(jnp.int32, (chans, LANES), 1)
    both = jnp.where(lane == 0, mean, jnp.where(lane == 1, squares, 0.0))
    wide = padded_lanes(chans)
    both = jnp.concatenate([both, jnp.zeros((wide - chans, LANES), F32)], axis=0)
    turned = both.T
    return turned[0:1, :chans], turned[1:2, :chans]


def put_rows(tile_rows, out_ref):
    height = out_ref.shape[1]
    flat = widen(jnp.concatenate(tile_rows, axis=1), height * LANES)
    tile = jnp.concatenate([flat[:, at : at + LANES] for at in range(0, height * LANES, LANES)], axis=0)
    out_ref[...] = jnp.broadcast_to(tile[None], out_ref.shape)


def get_rows(seen_ref, first, peers, which, chans):
    start, end = which * chans, (which + 1) * chans
    lines = range(start // LANES, -(-end // LANES))
    flat = jnp.concatenate([seen_ref[pl.ds(first, peers), k, :] for k in lines], axis=1)
    start -= lines[0] * LANES
    return widen(flat[:, start : start + chans], padded_lanes(chans))


def tile_height(chans, rows):
    return -(-rows * chans // LANES // 8) * 8


def fetch(pairs, sems, first=0):
    copies = [pltpu.make_async_copy(a, b, sems.at[first + k]) for k, (a, b) in enumerate(pairs)]
    for copy in copies:
        copy.start()
    return copies


def stats_kernel(
    lat_hbm, embed_hbm, weight_hbm,
    out_ref, near_hbm, next_hbm,
    lat_ref, embed_ref, weight_ref, sems, edge_sems,
):
    rows, chans, _ = lat_ref.shape
    reach = near_hbm.shape[0]
    last = rows - reach
    near_at = jnp.where(lax.rem(lax.axis_index("patch"), 2) == 0, last, 0)
    copies = fetch(
        [(lat_hbm.at[k], lat_ref.at[k]) for k in range(rows)]
        + [(embed_hbm, embed_ref), (weight_hbm, weight_ref)],
        sems,
    )
    edges = []
    waits = list(copies[:rows])

    def values():
        for k in range(rows):
            if waits:
                waits.pop(0).wait()
                if not waits:
                    edges.extend(
                        fetch(
                            [
                                (lat_ref.at[pl.ds(near_at, reach)], near_hbm),
                                (lat_ref.at[pl.ds(last - near_at, reach)], next_hbm),
                            ],
                            edge_sems,
                        )
                    )
            yield lat_ref[k].astype(F32)

    mean, squares = channel_moments(values, chans)
    copies[rows].wait()
    copies[rows + 1].wait()
    own = weight_ref.shape[0]
    length = embed_ref.shape[1]
    embed = jnp.broadcast_to(embed_ref[...].astype(F32), (8, length))
    embed = pltpu.roll(embed, length - lax.axis_index("patch") * own, 1)[:, :own]
    act = (embed / (1.0 + jnp.exp(-embed))).astype(BF16)
    time_part = jnp.dot(act, weight_ref[...], preferred_element_type=F32)[0:1]
    put_rows([mean, squares, time_part], out_ref)
    for copy in edges:
        copy.wait()


def parts_of(deep, part=8 * LANES):
    return [(at, min(part, deep - at)) for at in range(0, deep, part)]


def prepare_kernel(
    one_hbm, two_hbm, gain_one, shift_one, bias_one, time_bias, gain_two, shift_two, bias_two, steer,
    one_out, two_hbm_out, rows_ref, one_ref, two_ref, two_out, sems, row_sems, out_sem, *vector_refs,
):
    vectors = (gain_one, shift_one, bias_one, time_bias, gain_two, shift_two, bias_two)
    lines = fetch(zip(vectors, vector_refs), row_sems)
    parts = parts_of(one_ref.shape[0])
    sides = ((two_hbm, two_ref, two_out), (one_hbm, one_ref, one_out))
    copies = [
        fetch([(a.at[pl.ds(*p)], b.at[pl.ds(*p)]) for p in parts], sems, k * len(parts))
        for k, (a, b, _) in enumerate(sides)
    ]
    for line in lines:
        line.wait()
    wide = rows_ref.shape[1]
    rows = [widen(v[...].reshape(1, -1), wide) for v in vector_refs]
    rows_ref[...] = jnp.concatenate(rows + [jnp.broadcast_to(steer[...], (1, wide))], axis=0)
    for waits, (_, held, target) in zip(copies, sides):
        for wait, (at, size) in zip(waits, parts):
            wait.wait()
            target[:, at : at + size] = held[at : at + size, :].T
        if target is two_out:
            out = pltpu.make_async_copy(two_out, two_hbm_out, out_sem)
            out.start()
    out.wait()


def spread_columns(rows, chans, cols_ref):
    turned = stack_rows(rows, rows[0].shape[1]).T
    for k in range(len(rows)):
        cols_ref[k] = jnp.broadcast_to(turned[:chans, k : k + 1], (chans, LANES))


def half_act(values, mean, scale, shift):
    half = (values - mean) * scale + shift
    return half * jnp.tanh(half) + half


def twice(column):
    return jnp.concatenate([column, column], axis=1)


def put_taps(taps_ref, at, row):
    chans, cols = row.shape
    lane = lax.broadcasted_iota(jnp.int32, (chans, cols), 1)
    before = jnp.where(lane == 0, 0.0, pltpu.roll(row, 1, 1))
    after = jnp.where(lane == cols - 1, 0.0, pltpu.roll(row, cols - 1, 1))
    for k, value in enumerate((before, row, after)):
        taps_ref[pl.ds((at * 3 + k) * chans, chans), :] = value.astype(BF16)


def edge_keep(at, rows, reach):
    patch, patches = lax.axis_index("patch"), lax.axis_size("patch")
    if at < reach:
        return jnp.where(patch == 0, 0.0, 1.0).astype(F32)
    if at >= reach + rows:
        return jnp.where(patch == patches - 1, 0.0, 1.0).astype(F32)
    return None


def mixer(cols_ref, rows_ref, chans):
    sign = jnp.where(lax.axis_index("cfg") == 0, 1.0, -1.0).astype(F32)
    steer = rows_ref[7:8, 0:1] * sign

    def mix(mine, other):
        shift = twice(cols_ref[4])
        mine = half_act(mine.astype(F32), twice(cols_ref[0]), twice(cols_ref[1]), shift)
        other = half_act(other.astype(F32), twice(cols_ref[2]), twice(cols_ref[3]), shift)
        return mine + steer * (mine - other)

    return mix


def matmul(weight_ref, taps, first_tap):
    depth = taps.shape[0]
    start = first_tap * (weight_ref.shape[1] // 3)
    return jnp.dot(weight_ref[:, start : start + depth], taps, preferred_element_type=F32)


def inner_kernel(
    own_hbm, far_ref, seen_ref, rows_ref, weight_ref,
    steered_ref, taps_ref, cols_ref,
    own_ref, sems,
):
    rows, chans, cols = own_ref.shape
    copies = fetch([(own_hbm.at[k], own_ref.at[k]) for k in range(rows)], sems)
    wide = padded_lanes(chans)
    size = chans // GROUPS
    cfg, peers = lax.axis_index("cfg"), lax.axis_size("patch")
    mask = same_group(wide, size)
    starts = (cfg * peers, (1 - cfg) * peers)
    means = [get_rows(seen_ref, s, peers, 0, chans) for s in starts]
    squares = [get_rows(seen_ref, s, peers, 1, chans) for s in starts]
    mean_rows, var_rows = group_stats(means, squares, float(rows * cols), mask, size)
    scale_rows = lax.rsqrt(var_rows + EPS) * (0.5 * rows_ref[0:1])
    times = jnp.sum(get_rows(seen_ref, 0, peers, 2, chans), axis=0, keepdims=True)
    added = times + (rows_ref[3:4] + rows_ref[2:3])
    spread_columns(
        [mean_rows[0:1], scale_rows[0:1], mean_rows[1:2], scale_rows[1:2], 0.5 * rows_ref[1:2], added],
        chans, cols_ref,
    )
    mix = mixer(cols_ref, rows_ref, chans)
    line = 3 * chans
    for copy in copies:
        copy.wait()
    if rows < 3:
        steered_ref[...] = jnp.zeros_like(steered_ref)
    for at in range(rows):
        put_taps(taps_ref, at, mix(own_ref[at], far_ref[at]))
        if at >= 2:
            total = matmul(weight_ref, taps_ref[(at - 2) * line : (at + 1) * line, :], 0)
            steered_ref[at - 2] = total + twice(cols_ref[5])


def outer_kernel(
    near_ref, next_ref, far_near_ref, far_next_ref, inner_ref, inner_taps_ref, cols_ref, rows_ref, weight_ref,
    steered_ref, out_ref,
    taps_ref, edge_ref,
):
    reach, chans, cols = near_ref.shape
    line = 3 * chans
    rows = inner_taps_ref.shape[0] // line
    above = jnp.where(lax.rem(lax.axis_index("patch"), 2) == 0, reach, 0)
    edge_ref[0, pl.ds(above, reach)] = next_ref[...]
    edge_ref[1, pl.ds(above, reach)] = far_next_ref[...]
    edge_ref[0, pl.ds(reach - above, reach)] = near_ref[...]
    edge_ref[1, pl.ds(reach - above, reach)] = far_near_ref[...]
    mix = mixer(cols_ref, rows_ref, chans)

    def taps(at):
        if reach <= at < reach + rows:
            return inner_taps_ref, at - reach
        return taps_ref, at if at < reach else at - rows

    def rows_of(first, count):
        ref, at = taps(first)
        return ref[at * line : (at + count) * line, :]

    def conv(at):
        total, tap = None, 0
        while tap < 3:
            ref, _ = taps(at + tap)
            count = 1
            while tap + count < 3 and taps(at + tap + count)[0] is ref:
                count += 1
            part = matmul(weight_ref, rows_of(at + tap, count), tap)
            total = part if total is None else total + part
            tap += count
        return total

    def enter(at):
        k = reach + at if at < reach else at - reach - rows
        keep = edge_keep(at, rows, reach)
        put_taps(taps_ref, taps(at)[1], mix(edge_ref[0, k], edge_ref[1, k]) * keep)

    for at in range(reach):
        enter(at)
    outside = [at for at in range(rows + 2 * reach - 2) if not reach <= at < reach + rows - 2]
    place = {at: k for k, at in enumerate(outside)}
    ready = reach + rows
    for at in outside:
        while ready < at + 3:
            enter(ready)
            ready += 1
        steered_ref[place[at]] = conv(at) + twice(cols_ref[5])

    def own_rows():
        for k in range(rows):
            at = reach - 1 + k
            yield steered_ref[place[at]] if at in place else inner_ref[at - reach]

    mean, square = channel_moments(own_rows, chans)
    put_rows([mean, square], out_ref)


def second_kernel(
    inner_ref, outer_ref, lat_hbm, seen_ref, rows_ref, weight_ref,
    out_ref,
    taps_ref, cols_ref, lat_ref, sems,
):
    rows, chans, cols = lat_ref.shape
    copies = fetch([(lat_hbm.at[k], lat_ref.at[k]) for k in range(rows)], sems)
    wide = padded_lanes(chans)
    size = chans // GROUPS
    peers = lax.axis_size("patch")
    mask = same_group(wide, size)
    mean_rows, var_rows = group_stats(
        [get_rows(seen_ref, 0, peers, 0, chans)], [get_rows(seen_ref, 0, peers, 1, chans)],
        float(rows * cols), mask, size,
    )
    scale_rows = lax.rsqrt(var_rows + EPS) * (0.5 * rows_ref[4:5])
    spread_columns(
        [mean_rows[0:1], scale_rows[0:1], 0.5 * rows_ref[5:6], rows_ref[6:7]], chans, cols_ref
    )
    for copy in copies:
        copy.wait()
    line = 3 * chans
    inside = max(rows - 2, 0)
    half = outer_ref.shape[0] // 2
    for at in range(rows + 2):
        if half <= at < half + inside:
            value = inner_ref[at - half]
        else:
            value = outer_ref[at if at < half else at - inside]
        value = half_act(value, twice(cols_ref[0]), twice(cols_ref[1]), twice(cols_ref[2]))
        keep = edge_keep(at, rows, 1)
        put_taps(taps_ref, at, value if keep is None else value * keep)
        if at >= 2:
            total = matmul(weight_ref, taps_ref[(at - 2) * line : (at + 1) * line, :], 0)
            out_ref[at - 2] = (lat_ref[at - 2].astype(F32) + (total + twice(cols_ref[3]))).astype(BF16)


def everyone(tiles, axes):
    return lax.all_to_all(tiles, axes, 0, 0)


VMEM = pl.BlockSpec(memory_space=pltpu.VMEM)
ANY = pl.BlockSpec(memory_space=pl.ANY)
LIMIT = pltpu.CompilerParams(vmem_limit_bytes=12 * 1024 * 1024)


def in_hbm(value):
    return pltpu.with_memory_space_constraint(value, pltpu.HBM)


def body(
    latents, time_embed, steer_scale, gain_one, shift_one, conv_one, bias_one,
    time_weight, time_bias, gain_two, shift_two, conv_two, bias_two,
):
    own = jnp.swapaxes(latents[0, 0], 1, 2)
    rows, chans, cols = own.shape
    wide = padded_lanes(chans)
    deep = 9 * chans
    patches = lax.axis_size("patch")
    swap = [(0, 1), (1, 0)]
    line = lambda vector: vector.reshape(1, -1)

    tile_one = tile_height(chans, 3)
    sent, near_edge, next_edge = pl.pallas_call(
        stats_kernel,
        out_shape=[
            pltpu.VMEM((2 * patches, tile_one, LANES), F32),
            pltpu.HBM((REACH, chans, cols), BF16),
            pltpu.HBM((REACH, chans, cols), BF16),
        ],
        in_specs=[ANY] * 3,
        out_specs=[VMEM, ANY, ANY],
        scratch_shapes=[
            pltpu.VMEM((rows, chans, cols), BF16),
            pltpu.VMEM(time_embed.shape, BF16),
            pltpu.VMEM(time_weight.shape, BF16),
            pltpu.SemaphoreType.DMA((rows + 2,)),
            pltpu.SemaphoreType.DMA((2,)),
        ],
        compiler_params=LIMIT,
        name="stats",
    )(in_hbm(own), in_hbm(time_embed), in_hbm(time_weight))
    near = lax.ppermute(near_edge, "patch", [(i, i ^ 1) for i in range(patches)])
    steps = [(i, i + 1) for i in range(1, patches - 1, 2)]
    following = lax.ppermute(next_edge, "patch", steps + [(j, i) for i, j in steps])
    seen = everyone(sent, ("cfg", "patch"))

    weights = (conv_one.reshape(deep, chans), conv_two.reshape(deep, chans))
    source, *weights, _ = lax.optimization_barrier((own, *weights, sent))
    turned_one, turned_two, vectors = pl.pallas_call(
        prepare_kernel,
        out_shape=[
            pltpu.VMEM((chans, deep), BF16), pltpu.HBM((chans, deep), BF16), pltpu.VMEM((8, wide), F32),
        ],
        in_specs=[ANY] * 9 + [VMEM],
        out_specs=[VMEM, ANY, VMEM],
        scratch_shapes=[pltpu.VMEM((deep, chans), BF16)] * 2 + [pltpu.VMEM((chans, deep), BF16)]
        + [pltpu.SemaphoreType.DMA((2 * len(parts_of(deep)),)), pltpu.SemaphoreType.DMA((7,))]
        + [pltpu.SemaphoreType.DMA]
        + [pltpu.VMEM((chans,), F32)] * 7,
        compiler_params=LIMIT,
        name="prepare",
    )(
        in_hbm(weights[0]), in_hbm(weights[1]), in_hbm(gain_one), in_hbm(shift_one), in_hbm(bias_one),
        in_hbm(time_bias), in_hbm(gain_two), in_hbm(shift_two), in_hbm(bias_two), line(steer_scale),
    )
    far = lax.ppermute(source, "cfg", swap)
    near, following, vectors, seen = lax.optimization_barrier((near, following, vectors, seen))
    far_near = lax.ppermute(near, "cfg", swap)
    far_next = lax.ppermute(following, "cfg", swap)

    inner, taps, columns = pl.pallas_call(
        inner_kernel,
        out_shape=[
            pltpu.VMEM((max(rows - 2, 1), chans, cols), F32),
            pltpu.VMEM((rows * 3 * chans, cols), BF16),
            pltpu.VMEM((6, chans, LANES), F32),
        ],
        in_specs=[ANY] + [VMEM] * 4,
        out_specs=[VMEM] * 3,
        scratch_shapes=[pltpu.VMEM((rows, chans, cols), BF16), pltpu.SemaphoreType.DMA((rows,))],
        compiler_params=LIMIT,
        name="inner",
    )(in_hbm(own), far, seen, vectors, turned_one)
    tile_two = tile_height(chans, 2)
    outer, sent = pl.pallas_call(
        outer_kernel,
        out_shape=[
            pltpu.VMEM((2 * REACH, chans, cols), F32),
            pltpu.VMEM((patches, tile_two, LANES), F32),
        ],
        in_specs=[VMEM] * 9,
        out_specs=[VMEM] * 2,
        scratch_shapes=[
            pltpu.VMEM((2 * REACH * 3 * chans, cols), BF16),
            pltpu.VMEM((2, 2 * REACH, chans, cols), BF16),
        ],
        compiler_params=LIMIT,
        name="outer",
    )(near, following, far_near, far_next, inner, taps, columns, vectors, turned_one)
    seen = everyone(sent, "patch")
    image = pl.pallas_call(
        second_kernel,
        out_shape=jax.ShapeDtypeStruct((rows, chans, cols), BF16),
        in_specs=[VMEM] * 2 + [ANY] + [VMEM] * 3,
        out_specs=VMEM,
        scratch_shapes=[
            pltpu.VMEM(((rows + 2) * 3 * chans, cols), BF16),
            pltpu.VMEM((4, chans, LANES), F32),
            pltpu.VMEM((rows, chans, cols), BF16),
            pltpu.SemaphoreType.DMA((rows,)),
        ],
        compiler_params=LIMIT,
        name="second",
    )(inner, outer, in_hbm(own), seen, vectors, turned_two)
    return jnp.swapaxes(image, 1, 2)[None, None]


def solution(mesh):
    placed = (
        P("cfg", "req", "patch", None, None), P("req", None), P("req"), P(), P(), P(), P(),
        P("patch", None), P(), P(), P(), P(), P(),
    )
    return jax.shard_map(
        body,
        mesh=mesh,
        in_specs=placed,
        out_specs=P("cfg", "req", "patch", None, None),
        check_vma=False,
    )
```

```python
import functools

import jax
import jax.numpy as jnp
from jax import lax
from jax.experimental import pallas as pl
from jax.experimental.pallas import tpu as pltpu
from jax.sharding import PartitionSpec as P

GROUPS = 32
EPS = 1e-05
REACH = 2
LANES = 128
F32 = jnp.float32
BF16 = jnp.bfloat16


def padded_lanes(chans):
    return -(-chans // LANES) * LANES


def widen(row, wide):
    short = wide - row.shape[1]
    if not short:
        return row
    return jnp.concatenate([row, jnp.zeros((row.shape[0], short), row.dtype)], axis=1)


def same_group(wide, size):
    left = lax.broadcasted_iota(jnp.int32, (wide, wide), 0).astype(F32)
    right = lax.broadcasted_iota(jnp.int32, (wide, wide), 1).astype(F32)
    group = lambda at: jnp.floor((at + 0.5) * (1.0 / size))
    return jnp.where(group(left) == group(right), 1.0, 0.0).astype(BF16)


def group_sum(rows, mask):
    high = rows.astype(BF16).astype(F32)
    rest = rows - high
    middle = rest.astype(BF16).astype(F32)
    pieces = jnp.concatenate([high, middle, rest - middle, jnp.zeros_like(rows)], axis=0).astype(BF16)
    sums = jnp.dot(pieces, mask, preferred_element_type=F32)
    return sums[0:8] + sums[8:16] + sums[16:24]


def stack_rows(rows, wide):
    filler = [jnp.zeros((8 - len(rows), wide), F32)] if len(rows) < 8 else []
    return jnp.concatenate(list(rows) + filler, axis=0)


def group_stats(means, squares, count, mask, size):
    wide = mask.shape[0]
    peers = means[0].shape[0]
    mean_rows = [jnp.sum(m, axis=0, keepdims=True) * (1.0 / peers) for m in means]
    mean_rows = group_sum(stack_rows(mean_rows, wide), mask) * (1.0 / size)
    spread = []
    for k, (m, q) in enumerate(zip(means, squares)):
        off = m - mean_rows[k : k + 1]
        spread.append(jnp.sum(q + count * (off * off), axis=0, keepdims=True))
    var_rows = group_sum(stack_rows(spread, wide), mask) * (1.0 / (size * count * peers))
    return mean_rows, var_rows


def fold(values):
    total = values[:, :LANES]
    for at in range(LANES, values.shape[1], LANES):
        total = total + values[:, at : at + LANES]
    return total


def channel_moments(rows, chans):
    count = 0
    total = None
    for row in rows():
        part = fold(row)
        count += row.shape[1]
        total = part if total is None else total + part
    mean = jnp.sum(total, axis=1, keepdims=True) * (1.0 / count)
    squares = None
    for row in rows():
        off = row - mean
        part = fold(off * off)
        squares = part if squares is None else squares + part
    squares = jnp.sum(squares, axis=1, keepdims=True)
    lane = lax.broadcasted_iota(jnp.int32, (chans, LANES), 1)
    both = jnp.where(lane == 0, mean, jnp.where(lane == 1, squares, 0.0))
    wide = padded_lanes(chans)
    both = jnp.concatenate([both, jnp.zeros((wide - chans, LANES), F32)], axis=0)
    turned = both.T
    return turned[0:1, :chans], turned[1:2, :chans]


def put_rows(tile_rows, out_ref):
    height = out_ref.shape[1]
    flat = widen(jnp.concatenate(tile_rows, axis=1), height * LANES)
    tile = jnp.concatenate([flat[:, at : at + LANES] for at in range(0, height * LANES, LANES)], axis=0)
    out_ref[...] = jnp.broadcast_to(tile[None], out_ref.shape)


def get_rows(seen_ref, first, peers, which, chans):
    start, end = which * chans, (which + 1) * chans
    lines = range(start // LANES, -(-end // LANES))
    flat = jnp.concatenate([seen_ref[pl.ds(first, peers), k, :] for k in lines], axis=1)
    start -= lines[0] * LANES
    return widen(flat[:, start : start + chans], padded_lanes(chans))


def tile_height(chans, rows):
    return -(-rows * chans // LANES // 8) * 8


def fetch(pairs, sems, first=0):
    copies = [pltpu.make_async_copy(a, b, sems.at[first + k]) for k, (a, b) in enumerate(pairs)]
    for copy in copies:
        copy.start()
    return copies


def stats_kernel(
    lat_hbm, embed_hbm, weight_hbm, gain_one, shift_one, bias_one, time_bias, gain_two, shift_two, bias_two, steer, conv_hbm,
    lat_ref, out_ref, near_ref, next_ref, rows_ref, conv_ref,
    embed_ref, weight_ref, sems, edge_sems, row_sems, *vector_refs,
):
    rows, chans, _ = lat_ref.shape
    reach = near_ref.shape[0]
    last = rows - reach
    near_at = jnp.where(lax.rem(lax.axis_index("patch"), 2) == 0, last, 0)
    copies = fetch(
        [(lat_hbm.at[k], lat_ref.at[k]) for k in range(rows)]
        + [(embed_hbm, embed_ref), (weight_hbm, weight_ref)],
        sems,
    )
    vectors = (gain_one, shift_one, bias_one, time_bias, gain_two, shift_two, bias_two)
    copies += fetch(zip(vectors, vector_refs), row_sems)
    edges = fetch(
        [
            (lat_hbm.at[pl.ds(near_at, reach)], near_ref),
            (lat_hbm.at[pl.ds(last - near_at, reach)], next_ref),
            (conv_hbm, conv_ref),
        ],
        edge_sems,
    )
    for copy in copies:
        copy.wait()
    mean, squares = channel_moments(lambda: (lat_ref[k].astype(F32) for k in range(rows)), chans)
    own = weight_ref.shape[0]
    length = embed_ref.shape[1]
    embed = jnp.broadcast_to(embed_ref[...].astype(F32), (8, length))
    embed = pltpu.roll(embed, length - lax.axis_index("patch") * own, 1)[:, :own]
    act = (embed / (1.0 + jnp.exp(-embed))).astype(BF16)
    time_part = jnp.dot(act, weight_ref[...], preferred_element_type=F32)[0:1]
    put_rows([mean, squares, time_part], out_ref)
    wide = rows_ref.shape[1]
    lines = [widen(v[...].reshape(1, -1), wide) for v in vector_refs]
    rows_ref[...] = jnp.concatenate(lines + [jnp.full((1, wide), steer[0], F32)], axis=0)
    for copy in edges:
        copy.wait()


def turn(source, target, part=8 * LANES):
    deep = source.shape[0]
    for at in range(0, deep, part):
        size = min(part, deep - at)
        target[:, at : at + size] = source[at : at + size, :].T


def spread_columns(rows, chans, cols_ref):
    turned = stack_rows(rows, rows[0].shape[1]).T
    for k in range(len(rows)):
        cols_ref[k] = jnp.broadcast_to(turned[:chans, k : k + 1], (chans, LANES))


def half_act(values, mean, scale, shift):
    half = (values - mean) * scale + shift
    return half * jnp.tanh(half) + half


def twice(column):
    return jnp.concatenate([column, column], axis=1)


def put_taps(taps_ref, at, row):
    chans, cols = row.shape
    lane = lax.broadcasted_iota(jnp.int32, (chans, cols), 1)
    before = jnp.where(lane == 0, 0.0, pltpu.roll(row, 1, 1))
    after = jnp.where(lane == cols - 1, 0.0, pltpu.roll(row, cols - 1, 1))
    for k, value in enumerate((before, row, after)):
        taps_ref[pl.ds((at * 3 + k) * chans, chans), :] = value.astype(BF16)


def edge_keep(at, rows, reach):
    patch, patches = lax.axis_index("patch"), lax.axis_size("patch")
    if at < reach:
        return jnp.where(patch == 0, 0.0, 1.0).astype(F32)
    if at >= reach + rows:
        return jnp.where(patch == patches - 1, 0.0, 1.0).astype(F32)
    return None


def mixer(cols_ref, rows_ref, chans):
    sign = jnp.where(lax.axis_index("cfg") == 0, 1.0, -1.0).astype(F32)
    steer = rows_ref[7:8, 0:1] * sign

    def mix(mine, other):
        shift = twice(cols_ref[4])
        mine = half_act(mine.astype(F32), twice(cols_ref[0]), twice(cols_ref[1]), shift)
        other = half_act(other.astype(F32), twice(cols_ref[2]), twice(cols_ref[3]), shift)
        return mine + steer * (mine - other)

    return mix


def matmul(weight_ref, taps, first_tap):
    depth = taps.shape[0]
    start = first_tap * (weight_ref.shape[1] // 3)
    return jnp.dot(weight_ref[:, start : start + depth], taps, preferred_element_type=F32)


def inner_kernel(
    own_ref, far_ref, seen_ref, rows_ref, raw_ref,
    steered_ref, taps_ref, cols_ref, weight_ref,
):
    rows, chans, cols = own_ref.shape
    turn(raw_ref, weight_ref)
    wide = padded_lanes(chans)
    size = chans // GROUPS
    cfg, peers = lax.axis_index("cfg"), lax.axis_size("patch")
    mask = same_group(wide, size)
    starts = (cfg * peers, (1 - cfg) * peers)
    means = [get_rows(seen_ref, s, peers, 0, chans) for s in starts]
    squares = [get_rows(seen_ref, s, peers, 1, chans) for s in starts]
    mean_rows, var_rows = group_stats(means, squares, float(rows * cols), mask, size)
    scale_rows = lax.rsqrt(var_rows + EPS) * (0.5 * rows_ref[0:1])
    times = jnp.sum(get_rows(seen_ref, 0, peers, 2, chans), axis=0, keepdims=True)
    added = times + (rows_ref[3:4] + rows_ref[2:3])
    spread_columns(
        [mean_rows[0:1], scale_rows[0:1], mean_rows[1:2], scale_rows[1:2], 0.5 * rows_ref[1:2], added],
        chans, cols_ref,
    )
    mix = mixer(cols_ref, rows_ref, chans)
    line = 3 * chans
    if rows < 3:
        steered_ref[...] = jnp.zeros_like(steered_ref)
    for at in range(rows):
        put_taps(taps_ref, at, mix(own_ref[at], far_ref[at]))
        if at >= 2:
            total = matmul(weight_ref, taps_ref[(at - 2) * line : (at + 1) * line, :], 0)
            steered_ref[at - 2] = total + twice(cols_ref[5])


def outer_kernel(
    near_ref, next_ref, far_near_ref, far_next_ref, inner_ref, inner_taps_ref, cols_ref, rows_ref, weight_ref, raw_ref,
    steered_ref, out_ref, turned_ref,
    taps_ref, edge_ref,
):
    reach, chans, cols = near_ref.shape
    line = 3 * chans
    rows = inner_taps_ref.shape[0] // line
    above = jnp.where(lax.rem(lax.axis_index("patch"), 2) == 0, reach, 0)
    edge_ref[0, pl.ds(above, reach)] = next_ref[...]
    edge_ref[1, pl.ds(above, reach)] = far_next_ref[...]
    edge_ref[0, pl.ds(reach - above, reach)] = near_ref[...]
    edge_ref[1, pl.ds(reach - above, reach)] = far_near_ref[...]
    mix = mixer(cols_ref, rows_ref, chans)

    def taps(at):
        if reach <= at < reach + rows:
            return inner_taps_ref, at - reach
        return taps_ref, at if at < reach else at - rows

    def rows_of(first, count):
        ref, at = taps(first)
        return ref[at * line : (at + count) * line, :]

    def conv(at):
        total, tap = None, 0
        while tap < 3:
            ref, _ = taps(at + tap)
            count = 1
            while tap + count < 3 and taps(at + tap + count)[0] is ref:
                count += 1
            part = matmul(weight_ref, rows_of(at + tap, count), tap)
            total = part if total is None else total + part
            tap += count
        return total

    def enter(at):
        k = reach + at if at < reach else at - reach - rows
        keep = edge_keep(at, rows, reach)
        put_taps(taps_ref, taps(at)[1], mix(edge_ref[0, k], edge_ref[1, k]) * keep)

    for at in range(reach):
        enter(at)
    outside = [at for at in range(rows + 2 * reach - 2) if not reach <= at < reach + rows - 2]
    place = {at: k for k, at in enumerate(outside)}
    ready = reach + rows
    for at in outside:
        while ready < at + 3:
            enter(ready)
            ready += 1
        steered_ref[place[at]] = conv(at) + twice(cols_ref[5])
    turn(raw_ref, turned_ref)

    def own_rows():
        for k in range(rows):
            at = reach - 1 + k
            yield steered_ref[place[at]] if at in place else inner_ref[at - reach]

    mean, square = channel_moments(own_rows, chans)
    put_rows([mean, square], out_ref)


def second_kernel(
    inner_ref, outer_ref, lat_ref, seen_ref, rows_ref, weight_ref,
    out_ref,
    taps_ref, cols_ref,
):
    rows, chans, cols = lat_ref.shape
    wide = padded_lanes(chans)
    size = chans // GROUPS
    peers = lax.axis_size("patch")
    mask = same_group(wide, size)
    mean_rows, var_rows = group_stats(
        [get_rows(seen_ref, 0, peers, 0, chans)], [get_rows(seen_ref, 0, peers, 1, chans)],
        float(rows * cols), mask, size,
    )
    scale_rows = lax.rsqrt(var_rows + EPS) * (0.5 * rows_ref[4:5])
    spread_columns(
        [mean_rows[0:1], scale_rows[0:1], 0.5 * rows_ref[5:6], rows_ref[6:7]], chans, cols_ref
    )
    line = 3 * chans
    inside = max(rows - 2, 0)
    half = outer_ref.shape[0] // 2
    for at in range(rows + 2):
        if half <= at < half + inside:
            value = inner_ref[at - half]
        else:
            value = outer_ref[at if at < half else at - inside]
        value = half_act(value, twice(cols_ref[0]), twice(cols_ref[1]), twice(cols_ref[2]))
        keep = edge_keep(at, rows, 1)
        put_taps(taps_ref, at, value if keep is None else value * keep)
        if at >= 2:
            total = matmul(weight_ref, taps_ref[(at - 2) * line : (at + 1) * line, :], 0)
            out_ref[at - 2] = (lat_ref[at - 2].astype(F32) + (total + twice(cols_ref[3]))).astype(BF16)


def everyone(tiles, axes):
    return lax.all_to_all(tiles, axes, 0, 0)


VMEM = pl.BlockSpec(memory_space=pltpu.VMEM)
SMEM = pl.BlockSpec(memory_space=pltpu.SMEM)
ANY = pl.BlockSpec(memory_space=pl.ANY)
LIMIT = pltpu.CompilerParams(vmem_limit_bytes=12 * 1024 * 1024)


def in_hbm(value):
    return pltpu.with_memory_space_constraint(value, pltpu.HBM)


def body(
    latents, time_embed, steer_scale, gain_one, shift_one, conv_one, bias_one,
    time_weight, time_bias, gain_two, shift_two, conv_two, bias_two,
):
    own = jnp.swapaxes(latents[0, 0], 1, 2)
    rows, chans, cols = own.shape
    wide = padded_lanes(chans)
    deep = 9 * chans
    patches = lax.axis_size("patch")
    swap = [(0, 1), (1, 0)]
    tile_one = tile_height(chans, 3)
    held, sent, near_edge, next_edge, vectors, raw_one = pl.pallas_call(
        stats_kernel,
        out_shape=[
            pltpu.VMEM((rows, chans, cols), BF16),
            pltpu.VMEM((2 * patches, tile_one, LANES), F32),
            pltpu.VMEM((REACH, chans, cols), BF16),
            pltpu.VMEM((REACH, chans, cols), BF16),
            pltpu.VMEM((8, wide), F32),
            pltpu.VMEM((deep, chans), BF16),
        ],
        in_specs=[ANY] * 10 + [SMEM, ANY],
        out_specs=[VMEM] * 6,
        scratch_shapes=[
            pltpu.VMEM(time_embed.shape, BF16),
            pltpu.VMEM(time_weight.shape, BF16),
            pltpu.SemaphoreType.DMA((rows + 2,)),
            pltpu.SemaphoreType.DMA((3,)),
            pltpu.SemaphoreType.DMA((7,)),
        ]
        + [pltpu.VMEM((chans,), F32)] * 7,
        compiler_params=LIMIT,
        name="stats",
    )(
        in_hbm(own), in_hbm(time_embed), in_hbm(time_weight), in_hbm(gain_one), in_hbm(shift_one),
        in_hbm(bias_one), in_hbm(time_bias), in_hbm(gain_two), in_hbm(shift_two), in_hbm(bias_two), steer_scale,
        in_hbm(conv_one.reshape(deep, chans)),
    )
    near = lax.ppermute(near_edge, "patch", [(i, i ^ 1) for i in range(patches)])
    steps = [(i, i + 1) for i in range(1, patches - 1, 2)]
    following = lax.ppermute(next_edge, "patch", steps + [(j, i) for i, j in steps])
    seen = everyone(sent, ("cfg", "patch"))

    source, _ = lax.optimization_barrier((own, sent))
    far = lax.ppermute(source, "cfg", swap)
    near, following, seen = lax.optimization_barrier((near, following, seen))
    far_near = lax.ppermute(near, "cfg", swap)
    far_next = lax.ppermute(following, "cfg", swap)

    inner, taps, columns, turned_one = pl.pallas_call(
        inner_kernel,
        out_shape=[
            pltpu.VMEM((max(rows - 2, 1), chans, cols), F32),
            pltpu.VMEM((rows * 3 * chans, cols), BF16),
            pltpu.VMEM((6, chans, LANES), F32),
            pltpu.VMEM((chans, deep), BF16),
        ],
        in_specs=[VMEM] * 5,
        out_specs=[VMEM] * 4,
        compiler_params=LIMIT,
        name="inner",
    )(held, far, seen, vectors, raw_one)
    tile_two = tile_height(chans, 2)
    outer, sent, turned_two = pl.pallas_call(
        outer_kernel,
        out_shape=[
            pltpu.VMEM((2 * REACH, chans, cols), F32),
            pltpu.VMEM((patches, tile_two, LANES), F32),
            pltpu.VMEM((chans, deep), BF16),
        ],
        in_specs=[VMEM] * 10,
        out_specs=[VMEM] * 3,
        scratch_shapes=[
            pltpu.VMEM((2 * REACH * 3 * chans, cols), BF16),
            pltpu.VMEM((2, 2 * REACH, chans, cols), BF16),
        ],
        compiler_params=LIMIT,
        name="outer",
    )(
        near, following, far_near, far_next, inner, taps, columns, vectors, turned_one,
        conv_two.reshape(deep, chans),
    )
    seen = everyone(sent, "patch")
    image = pl.pallas_call(
        second_kernel,
        out_shape=jax.ShapeDtypeStruct((rows, chans, cols), BF16),
        in_specs=[VMEM] * 6,
        out_specs=VMEM,
        scratch_shapes=[
            pltpu.VMEM(((rows + 2) * 3 * chans, cols), BF16),
            pltpu.VMEM((4, chans, LANES), F32),
        ],
        compiler_params=LIMIT,
        name="second",
    )(inner, outer, held, seen, vectors, turned_two)
    return jnp.swapaxes(image, 1, 2)[None, None]


def solution(mesh):
    placed = (
        P("cfg", "req", "patch", None, None), P("req", None), P("req"), P(), P(), P(), P(),
        P("patch", None), P(), P(), P(), P(), P(),
    )
    return jax.shard_map(
        body,
        mesh=mesh,
        in_specs=placed,
        out_specs=P("cfg", "req", "patch", None, None),
        check_vma=False,
    )
```

```python
import functools

import jax
import jax.numpy as jnp
from jax import lax
from jax.experimental import pallas as pl
from jax.experimental.pallas import tpu as pltpu
from jax.sharding import PartitionSpec as P

GROUPS = 32
EPS = 1e-05
REACH = 2
LANES = 128
F32 = jnp.float32
BF16 = jnp.bfloat16


def padded_lanes(chans):
    return -(-chans // LANES) * LANES


def widen(row, wide):
    short = wide - row.shape[1]
    if not short:
        return row
    return jnp.concatenate([row, jnp.zeros((row.shape[0], short), row.dtype)], axis=1)


def same_group(wide, size):
    left = lax.broadcasted_iota(jnp.int32, (wide, wide), 0).astype(F32)
    right = lax.broadcasted_iota(jnp.int32, (wide, wide), 1).astype(F32)
    group = lambda at: jnp.floor((at + 0.5) * (1.0 / size))
    return jnp.where(group(left) == group(right), 1.0, 0.0).astype(BF16)


def group_sum(rows, mask):
    high = rows.astype(BF16).astype(F32)
    rest = rows - high
    middle = rest.astype(BF16).astype(F32)
    pieces = jnp.concatenate([high, middle, rest - middle, jnp.zeros_like(rows)], axis=0).astype(BF16)
    sums = jnp.dot(pieces, mask, preferred_element_type=F32)
    return sums[0:8] + sums[8:16] + sums[16:24]


def stack_rows(rows, wide):
    filler = [jnp.zeros((8 - len(rows), wide), F32)] if len(rows) < 8 else []
    return jnp.concatenate(list(rows) + filler, axis=0)


def group_stats(means, squares, count, mask, size):
    wide = mask.shape[0]
    peers = means[0].shape[0]
    mean_rows = [jnp.sum(m, axis=0, keepdims=True) * (1.0 / peers) for m in means]
    mean_rows = group_sum(stack_rows(mean_rows, wide), mask) * (1.0 / size)
    spread = []
    for k, (m, q) in enumerate(zip(means, squares)):
        off = m - mean_rows[k : k + 1]
        spread.append(jnp.sum(q + count * (off * off), axis=0, keepdims=True))
    var_rows = group_sum(stack_rows(spread, wide), mask) * (1.0 / (size * count * peers))
    return mean_rows, var_rows


def fold(values):
    total = values[:, :LANES]
    for at in range(LANES, values.shape[1], LANES):
        total = total + values[:, at : at + LANES]
    return total


def channel_moments(rows, chans):
    count = 0
    total = None
    for row in rows():
        part = fold(row)
        count += row.shape[1]
        total = part if total is None else total + part
    mean = jnp.sum(total, axis=1, keepdims=True) * (1.0 / count)
    squares = None
    for row in rows():
        off = row - mean
        part = fold(off * off)
        squares = part if squares is None else squares + part
    squares = jnp.sum(squares, axis=1, keepdims=True)
    lane = lax.broadcasted_iota(jnp.int32, (chans, LANES), 1)
    both = jnp.where(lane == 0, mean, jnp.where(lane == 1, squares, 0.0))
    wide = padded_lanes(chans)
    both = jnp.concatenate([both, jnp.zeros((wide - chans, LANES), F32)], axis=0)
    turned = both.T
    return turned[0:1, :chans], turned[1:2, :chans]


def put_rows(tile_rows, out_ref):
    height = out_ref.shape[1]
    flat = widen(jnp.concatenate(tile_rows, axis=1), height * LANES)
    tile = jnp.concatenate([flat[:, at : at + LANES] for at in range(0, height * LANES, LANES)], axis=0)
    out_ref[...] = jnp.broadcast_to(tile[None], out_ref.shape)


def get_rows(seen_ref, first, peers, which, chans):
    start, end = which * chans, (which + 1) * chans
    lines = range(start // LANES, -(-end // LANES))
    flat = jnp.concatenate([seen_ref[pl.ds(first, peers), k, :] for k in lines], axis=1)
    start -= lines[0] * LANES
    return widen(flat[:, start : start + chans], padded_lanes(chans))


def tile_height(chans, rows):
    return -(-rows * chans // LANES // 8) * 8


def fetch(pairs, sems, first=0):
    copies = [pltpu.make_async_copy(a, b, sems.at[first + k]) for k, (a, b) in enumerate(pairs)]
    for copy in copies:
        copy.start()
    return copies


def near_at(lat_hbm, reach):
    return jnp.where(lax.rem(lax.axis_index("patch"), 2) == 0, lat_hbm.shape[0] - reach, 0)


def edge_kernel(lat_hbm, next_ref, sem):
    reach = next_ref.shape[0]
    at = lat_hbm.shape[0] - reach - near_at(lat_hbm, reach)
    copy = pltpu.make_async_copy(lat_hbm.at[pl.ds(at, reach)], next_ref, sem)
    copy.start()
    copy.wait()


def stats_kernel(
    lat_hbm, embed_hbm, weight_hbm, gain_one, shift_one, bias_one, time_bias, gain_two, shift_two, bias_two, steer, conv_hbm,
    lat_ref, out_ref, near_ref, rows_ref, conv_ref,
    embed_ref, weight_ref, sems, late_sems, row_sems, *vector_refs,
):
    rows, chans, _ = lat_ref.shape
    copies = fetch(
        [(lat_hbm.at[k], lat_ref.at[k]) for k in range(rows)]
        + [(embed_hbm, embed_ref), (weight_hbm, weight_ref)],
        sems,
    )
    vectors = (gain_one, shift_one, bias_one, time_bias, gain_two, shift_two, bias_two)
    copies += fetch(zip(vectors, vector_refs), row_sems)
    reach = near_ref.shape[0]
    edge = lat_hbm.at[pl.ds(near_at(lat_hbm, reach), reach)]
    late = fetch([(edge, near_ref), (conv_hbm, conv_ref)], late_sems)
    for copy in copies:
        copy.wait()
    mean, squares = channel_moments(lambda: (lat_ref[k].astype(F32) for k in range(rows)), chans)
    own = weight_ref.shape[0]
    length = embed_ref.shape[1]
    embed = jnp.broadcast_to(embed_ref[...].astype(F32), (8, length))
    embed = pltpu.roll(embed, length - lax.axis_index("patch") * own, 1)[:, :own]
    act = (embed / (1.0 + jnp.exp(-embed))).astype(BF16)
    time_part = jnp.dot(act, weight_ref[...], preferred_element_type=F32)[0:1]
    put_rows([mean, squares, time_part], out_ref)
    wide = rows_ref.shape[1]
    lines = [widen(v[...].reshape(1, -1), wide) for v in vector_refs]
    rows_ref[...] = jnp.concatenate(lines + [jnp.full((1, wide), steer[0], F32)], axis=0)
    for copy in late:
        copy.wait()


def turn(source, target, part=8 * LANES):
    deep = source.shape[0]
    for at in range(0, deep, part):
        size = min(part, deep - at)
        target[:, at : at + size] = source[at : at + size, :].T


def spread_columns(rows, chans, cols_ref):
    turned = stack_rows(rows, rows[0].shape[1]).T
    for k in range(len(rows)):
        cols_ref[k] = jnp.broadcast_to(turned[:chans, k : k + 1], (chans, LANES))


def half_act(values, mean, scale, shift):
    half = (values - mean) * scale + shift
    return half * jnp.tanh(half) + half


def twice(column):
    return jnp.concatenate([column, column], axis=1)


def put_taps(taps_ref, at, row):
    chans, cols = row.shape
    lane = lax.broadcasted_iota(jnp.int32, (chans, cols), 1)
    before = jnp.where(lane == 0, 0.0, pltpu.roll(row, 1, 1))
    after = jnp.where(lane == cols - 1, 0.0, pltpu.roll(row, cols - 1, 1))
    for k, value in enumerate((before, row, after)):
        taps_ref[pl.ds((at * 3 + k) * chans, chans), :] = value.astype(BF16)


def edge_keep(at, rows, reach):
    patch, patches = lax.axis_index("patch"), lax.axis_size("patch")
    if at < reach:
        return jnp.where(patch == 0, 0.0, 1.0).astype(F32)
    if at >= reach + rows:
        return jnp.where(patch == patches - 1, 0.0, 1.0).astype(F32)
    return None


def mixer(cols_ref, rows_ref, chans):
    sign = jnp.where(lax.axis_index("cfg") == 0, 1.0, -1.0).astype(F32)
    steer = rows_ref[7:8, 0:1] * sign

    def mix(mine, other):
        shift = twice(cols_ref[4])
        mine = half_act(mine.astype(F32), twice(cols_ref[0]), twice(cols_ref[1]), shift)
        other = half_act(other.astype(F32), twice(cols_ref[2]), twice(cols_ref[3]), shift)
        return mine + steer * (mine - other)

    return mix


def matmul(weight_ref, taps, first_tap):
    depth = taps.shape[0]
    start = first_tap * (weight_ref.shape[1] // 3)
    return jnp.dot(weight_ref[:, start : start + depth], taps, preferred_element_type=F32)


def inner_kernel(
    own_ref, far_ref, seen_ref, rows_ref, raw_ref,
    steered_ref, taps_ref, cols_ref, weight_ref,
):
    rows, chans, cols = own_ref.shape
    turn(raw_ref, weight_ref)
    wide = padded_lanes(chans)
    size = chans // GROUPS
    cfg, peers = lax.axis_index("cfg"), lax.axis_size("patch")
    mask = same_group(wide, size)
    starts = (cfg * peers, (1 - cfg) * peers)
    means = [get_rows(seen_ref, s, peers, 0, chans) for s in starts]
    squares = [get_rows(seen_ref, s, peers, 1, chans) for s in starts]
    mean_rows, var_rows = group_stats(means, squares, float(rows * cols), mask, size)
    scale_rows = lax.rsqrt(var_rows + EPS) * (0.5 * rows_ref[0:1])
    times = jnp.sum(get_rows(seen_ref, 0, peers, 2, chans), axis=0, keepdims=True)
    added = times + (rows_ref[3:4] + rows_ref[2:3])
    spread_columns(
        [mean_rows[0:1], scale_rows[0:1], mean_rows[1:2], scale_rows[1:2], 0.5 * rows_ref[1:2], added],
        chans, cols_ref,
    )
    mix = mixer(cols_ref, rows_ref, chans)
    line = 3 * chans
    if rows < 3:
        steered_ref[...] = jnp.zeros_like(steered_ref)
    for at in range(rows):
        put_taps(taps_ref, at, mix(own_ref[at], far_ref[at]))
        if at >= 2:
            total = matmul(weight_ref, taps_ref[(at - 2) * line : (at + 1) * line, :], 0)
            steered_ref[at - 2] = total + twice(cols_ref[5])


def outer_kernel(
    next_ref, near_ref, far_next_ref, far_near_ref, inner_ref, inner_taps_ref, cols_ref, rows_ref, weight_ref, raw_ref,
    steered_ref, out_ref, turned_ref,
    taps_ref, edge_ref,
):
    reach, chans, cols = near_ref.shape
    line = 3 * chans
    rows = inner_taps_ref.shape[0] // line
    above = jnp.where(lax.rem(lax.axis_index("patch"), 2) == 0, reach, 0)
    edge_ref[0, pl.ds(above, reach)] = next_ref[...]
    edge_ref[1, pl.ds(above, reach)] = far_next_ref[...]
    edge_ref[0, pl.ds(reach - above, reach)] = near_ref[...]
    edge_ref[1, pl.ds(reach - above, reach)] = far_near_ref[...]
    mix = mixer(cols_ref, rows_ref, chans)

    def taps(at):
        if reach <= at < reach + rows:
            return inner_taps_ref, at - reach
        return taps_ref, at if at < reach else at - rows

    def rows_of(first, count):
        ref, at = taps(first)
        return ref[at * line : (at + count) * line, :]

    def conv(at):
        total, tap = None, 0
        while tap < 3:
            ref, _ = taps(at + tap)
            count = 1
            while tap + count < 3 and taps(at + tap + count)[0] is ref:
                count += 1
            part = matmul(weight_ref, rows_of(at + tap, count), tap)
            total = part if total is None else total + part
            tap += count
        return total

    def enter(at):
        k = reach + at if at < reach else at - reach - rows
        keep = edge_keep(at, rows, reach)
        put_taps(taps_ref, taps(at)[1], mix(edge_ref[0, k], edge_ref[1, k]) * keep)

    for at in range(reach):
        enter(at)
    outside = [at for at in range(rows + 2 * reach - 2) if not reach <= at < reach + rows - 2]
    place = {at: k for k, at in enumerate(outside)}
    ready = reach + rows
    for at in outside:
        while ready < at + 3:
            enter(ready)
            ready += 1
        steered_ref[place[at]] = conv(at) + twice(cols_ref[5])
    turn(raw_ref, turned_ref)

    def own_rows():
        for k in range(rows):
            at = reach - 1 + k
            yield steered_ref[place[at]] if at in place else inner_ref[at - reach]

    mean, square = channel_moments(own_rows, chans)
    put_rows([mean, square], out_ref)


def second_kernel(
    inner_ref, outer_ref, lat_ref, seen_ref, rows_ref, weight_ref,
    out_ref,
    taps_ref, cols_ref,
):
    rows, chans, cols = lat_ref.shape
    wide = padded_lanes(chans)
    size = chans // GROUPS
    peers = lax.axis_size("patch")
    mask = same_group(wide, size)
    mean_rows, var_rows = group_stats(
        [get_rows(seen_ref, 0, peers, 0, chans)], [get_rows(seen_ref, 0, peers, 1, chans)],
        float(rows * cols), mask, size,
    )
    scale_rows = lax.rsqrt(var_rows + EPS) * (0.5 * rows_ref[4:5])
    spread_columns(
        [mean_rows[0:1], scale_rows[0:1], 0.5 * rows_ref[5:6], rows_ref[6:7]], chans, cols_ref
    )
    line = 3 * chans
    inside = max(rows - 2, 0)
    half = outer_ref.shape[0] // 2
    for at in range(rows + 2):
        if half <= at < half + inside:
            value = inner_ref[at - half]
        else:
            value = outer_ref[at if at < half else at - inside]
        value = half_act(value, twice(cols_ref[0]), twice(cols_ref[1]), twice(cols_ref[2]))
        keep = edge_keep(at, rows, 1)
        put_taps(taps_ref, at, value if keep is None else value * keep)
        if at >= 2:
            total = matmul(weight_ref, taps_ref[(at - 2) * line : (at + 1) * line, :], 0)
            out_ref[at - 2] = (lat_ref[at - 2].astype(F32) + (total + twice(cols_ref[3]))).astype(BF16)


def everyone(tiles, axes):
    return lax.all_to_all(tiles, axes, 0, 0)


VMEM = pl.BlockSpec(memory_space=pltpu.VMEM)
SMEM = pl.BlockSpec(memory_space=pltpu.SMEM)
ANY = pl.BlockSpec(memory_space=pl.ANY)
LIMIT = pltpu.CompilerParams(vmem_limit_bytes=12 * 1024 * 1024)


def in_hbm(value):
    return pltpu.with_memory_space_constraint(value, pltpu.HBM)


def body(
    latents, time_embed, steer_scale, gain_one, shift_one, conv_one, bias_one,
    time_weight, time_bias, gain_two, shift_two, conv_two, bias_two,
):
    own = jnp.swapaxes(latents[0, 0], 1, 2)
    rows, chans, cols = own.shape
    wide = padded_lanes(chans)
    deep = 9 * chans
    patches = lax.axis_size("patch")
    swap = [(0, 1), (1, 0)]
    next_edge = pl.pallas_call(
        edge_kernel,
        out_shape=pltpu.VMEM((REACH, chans, cols), BF16),
        in_specs=[ANY],
        out_specs=VMEM,
        scratch_shapes=[pltpu.SemaphoreType.DMA],
        compiler_params=LIMIT,
        name="edge",
    )(in_hbm(own))
    steps = [(i, i + 1) for i in range(1, patches - 1, 2)]
    following = lax.ppermute(next_edge, "patch", steps + [(j, i) for i, j in steps])
    steer, _ = lax.optimization_barrier((steer_scale, next_edge))
    tile_one = tile_height(chans, 3)
    held, sent, near_edge, vectors, raw_one = pl.pallas_call(
        stats_kernel,
        out_shape=[
            pltpu.VMEM((rows, chans, cols), BF16),
            pltpu.VMEM((2 * patches, tile_one, LANES), F32),
            pltpu.VMEM((REACH, chans, cols), BF16),
            pltpu.VMEM((8, wide), F32),
            pltpu.VMEM((deep, chans), BF16),
        ],
        in_specs=[ANY] * 10 + [SMEM, ANY],
        out_specs=[VMEM] * 5,
        scratch_shapes=[
            pltpu.VMEM(time_embed.shape, BF16),
            pltpu.VMEM(time_weight.shape, BF16),
            pltpu.SemaphoreType.DMA((rows + 2,)),
            pltpu.SemaphoreType.DMA((2,)),
            pltpu.SemaphoreType.DMA((7,)),
        ]
        + [pltpu.VMEM((chans,), F32)] * 7,
        compiler_params=LIMIT,
        name="stats",
    )(
        in_hbm(own), in_hbm(time_embed), in_hbm(time_weight), in_hbm(gain_one), in_hbm(shift_one),
        in_hbm(bias_one), in_hbm(time_bias), in_hbm(gain_two), in_hbm(shift_two), in_hbm(bias_two), steer,
        in_hbm(conv_one.reshape(deep, chans)),
    )
    near = lax.ppermute(near_edge, "patch", [(i, i ^ 1) for i in range(patches)])
    source, _ = lax.optimization_barrier((own, sent))
    far = lax.ppermute(source, "cfg", swap)
    seen = everyone(sent, ("cfg", "patch"))

    following, near, seen = lax.optimization_barrier((following, near, seen))
    far_next = lax.ppermute(following, "cfg", swap)
    far_near = lax.ppermute(near, "cfg", swap)

    inner, taps, columns, turned_one = pl.pallas_call(
        inner_kernel,
        out_shape=[
            pltpu.VMEM((max(rows - 2, 1), chans, cols), F32),
            pltpu.VMEM((rows * 3 * chans, cols), BF16),
            pltpu.VMEM((6, chans, LANES), F32),
            pltpu.VMEM((chans, deep), BF16),
        ],
        in_specs=[VMEM] * 5,
        out_specs=[VMEM] * 4,
        compiler_params=LIMIT,
        name="inner",
    )(held, far, seen, vectors, raw_one)
    tile_two = tile_height(chans, 2)
    outer, sent, turned_two = pl.pallas_call(
        outer_kernel,
        out_shape=[
            pltpu.VMEM((2 * REACH, chans, cols), F32),
            pltpu.VMEM((patches, tile_two, LANES), F32),
            pltpu.VMEM((chans, deep), BF16),
        ],
        in_specs=[VMEM] * 10,
        out_specs=[VMEM] * 3,
        scratch_shapes=[
            pltpu.VMEM((2 * REACH * 3 * chans, cols), BF16),
            pltpu.VMEM((2, 2 * REACH, chans, cols), BF16),
        ],
        compiler_params=LIMIT,
        name="outer",
    )(
        following, near, far_next, far_near, inner, taps, columns, vectors, turned_one,
        conv_two.reshape(deep, chans),
    )
    seen = everyone(sent, "patch")
    image = pl.pallas_call(
        second_kernel,
        out_shape=jax.ShapeDtypeStruct((rows, chans, cols), BF16),
        in_specs=[VMEM] * 6,
        out_specs=VMEM,
        scratch_shapes=[
            pltpu.VMEM(((rows + 2) * 3 * chans, cols), BF16),
            pltpu.VMEM((4, chans, LANES), F32),
        ],
        compiler_params=LIMIT,
        name="second",
    )(inner, outer, held, seen, vectors, turned_two)
    return jnp.swapaxes(image, 1, 2)[None, None]


def solution(mesh):
    placed = (
        P("cfg", "req", "patch", None, None), P("req", None), P("req"), P(), P(), P(), P(),
        P("patch", None), P(), P(), P(), P(), P(),
    )
    return jax.shard_map(
        body,
        mesh=mesh,
        in_specs=placed,
        out_specs=P("cfg", "req", "patch", None, None),
        check_vma=False,
    )
```

```python
import functools

import jax
import jax.numpy as jnp
from jax import lax
from jax.experimental import pallas as pl
from jax.experimental.pallas import tpu as pltpu
from jax.sharding import PartitionSpec as P

GROUPS = 32
EPS = 1e-05
REACH = 2
LANES = 128
F32 = jnp.float32
BF16 = jnp.bfloat16


def padded_lanes(chans):
    return -(-chans // LANES) * LANES


def widen(row, wide):
    short = wide - row.shape[1]
    if not short:
        return row
    return jnp.concatenate([row, jnp.zeros((row.shape[0], short), row.dtype)], axis=1)


def same_group(wide, size):
    left = lax.broadcasted_iota(jnp.int32, (wide, wide), 0).astype(F32)
    right = lax.broadcasted_iota(jnp.int32, (wide, wide), 1).astype(F32)
    group = lambda at: jnp.floor((at + 0.5) * (1.0 / size))
    return jnp.where(group(left) == group(right), 1.0, 0.0).astype(BF16)


def group_sum(rows, mask):
    high = rows.astype(BF16).astype(F32)
    rest = rows - high
    middle = rest.astype(BF16).astype(F32)
    pieces = jnp.concatenate([high, middle, rest - middle, jnp.zeros_like(rows)], axis=0).astype(BF16)
    sums = jnp.dot(pieces, mask, preferred_element_type=F32)
    return sums[0:8] + sums[8:16] + sums[16:24]


def stack_rows(rows, wide):
    filler = [jnp.zeros((8 - len(rows), wide), F32)] if len(rows) < 8 else []
    return jnp.concatenate(list(rows) + filler, axis=0)


def group_stats(means, squares, count, mask, size):
    wide = mask.shape[0]
    peers = means[0].shape[0]
    mean_rows = [jnp.sum(m, axis=0, keepdims=True) * (1.0 / peers) for m in means]
    mean_rows = group_sum(stack_rows(mean_rows, wide), mask) * (1.0 / size)
    spread = []
    for k, (m, q) in enumerate(zip(means, squares)):
        off = m - mean_rows[k : k + 1]
        spread.append(jnp.sum(q + count * (off * off), axis=0, keepdims=True))
    var_rows = group_sum(stack_rows(spread, wide), mask) * (1.0 / (size * count * peers))
    return mean_rows, var_rows


def fold(values):
    total = values[:, :LANES]
    for at in range(LANES, values.shape[1], LANES):
        total = total + values[:, at : at + LANES]
    return total


def channel_moments(rows, chans):
    count = 0
    total = None
    for row in rows():
        part = fold(row)
        count += row.shape[1]
        total = part if total is None else total + part
    mean = jnp.sum(total, axis=1, keepdims=True) * (1.0 / count)
    squares = None
    for row in rows():
        off = row - mean
        part = fold(off * off)
        squares = part if squares is None else squares + part
    squares = jnp.sum(squares, axis=1, keepdims=True)
    lane = lax.broadcasted_iota(jnp.int32, (chans, LANES), 1)
    both = jnp.where(lane == 0, mean, jnp.where(lane == 1, squares, 0.0))
    wide = padded_lanes(chans)
    both = jnp.concatenate([both, jnp.zeros((wide - chans, LANES), F32)], axis=0)
    turned = both.T
    return turned[0:1, :chans], turned[1:2, :chans]


def put_rows(tile_rows, out_ref):
    height = out_ref.shape[-2]
    flat = widen(jnp.concatenate(tile_rows, axis=1), height * LANES)
    tile = jnp.concatenate([flat[:, at : at + LANES] for at in range(0, height * LANES, LANES)], axis=0)
    out_ref[...] = jnp.broadcast_to(tile, out_ref.shape)


def get_rows(seen_ref, which, chans, base=0):
    start, end = which * chans, (which + 1) * chans
    lines = range(start // LANES, -(-end // LANES))
    flat = jnp.concatenate([seen_ref[:, base + k, :] for k in lines], axis=1)
    start -= lines[0] * LANES
    return widen(flat[:, start : start + chans], padded_lanes(chans))


def tile_height(chans, rows):
    return -(-rows * chans // LANES // 8) * 8


def fetch(pairs, sems, first=0):
    copies = [pltpu.make_async_copy(a, b, sems.at[first + k]) for k, (a, b) in enumerate(pairs)]
    for copy in copies:
        copy.start()
    return copies


def stats_kernel(
    lat_hbm, embed_hbm, weight_hbm, gain_one, shift_one, bias_one, time_bias, gain_two, shift_two, bias_two, steer, conv_hbm,
    lat_ref, out_ref, near_ref, next_ref, rows_ref, conv_ref,
    embed_ref, weight_ref, sems, edge_sems, row_sems, *vector_refs,
):
    rows, chans, _ = lat_ref.shape
    reach = near_ref.shape[0]
    last = rows - reach
    near_at = jnp.where(lax.rem(lax.axis_index("patch"), 2) == 0, last, 0)
    copies = fetch(
        [(lat_hbm.at[k], lat_ref.at[k]) for k in range(rows)]
        + [(embed_hbm, embed_ref), (weight_hbm, weight_ref)],
        sems,
    )
    vectors = (gain_one, shift_one, bias_one, time_bias, gain_two, shift_two, bias_two)
    copies += fetch(zip(vectors, vector_refs), row_sems)
    edges = fetch(
        [
            (lat_hbm.at[pl.ds(near_at, reach)], near_ref),
            (lat_hbm.at[pl.ds(last - near_at, reach)], next_ref),
            (conv_hbm, conv_ref),
        ],
        edge_sems,
    )
    for copy in copies:
        copy.wait()
    mean, squares = channel_moments(lambda: (lat_ref[k].astype(F32) for k in range(rows)), chans)
    own = weight_ref.shape[0]
    length = embed_ref.shape[1]
    embed = jnp.broadcast_to(embed_ref[...].astype(F32), (8, length))
    embed = pltpu.roll(embed, length - lax.axis_index("patch") * own, 1)[:, :own]
    act = (embed / (1.0 + jnp.exp(-embed))).astype(BF16)
    time_part = jnp.dot(act, weight_ref[...], preferred_element_type=F32)[0:1]
    put_rows([mean, squares, time_part], out_ref)
    wide = rows_ref.shape[1]
    lines = [widen(v[...].reshape(1, -1), wide) for v in vector_refs]
    rows_ref[...] = jnp.concatenate(lines + [jnp.full((1, wide), steer[0], F32)], axis=0)
    for copy in edges:
        copy.wait()


def turn(source, target, part=8 * LANES):
    deep = source.shape[0]
    for at in range(0, deep, part):
        size = min(part, deep - at)
        target[:, at : at + size] = source[at : at + size, :].T


def spread_columns(rows, chans, cols_ref):
    turned = stack_rows(rows, rows[0].shape[1]).T
    for k in range(len(rows)):
        cols_ref[k] = jnp.broadcast_to(turned[:chans, k : k + 1], (chans, LANES))


def half_act(values, mean, scale, shift):
    half = (values - mean) * scale + shift
    return half * jnp.tanh(half) + half


def twice(column):
    return jnp.concatenate([column, column], axis=1)


def put_taps(taps_ref, at, row):
    chans, cols = row.shape
    lane = lax.broadcasted_iota(jnp.int32, (chans, cols), 1)
    before = jnp.where(lane == 0, 0.0, pltpu.roll(row, 1, 1))
    after = jnp.where(lane == cols - 1, 0.0, pltpu.roll(row, cols - 1, 1))
    for k, value in enumerate((before, row, after)):
        taps_ref[pl.ds((at * 3 + k) * chans, chans), :] = value.astype(BF16)


def edge_keep(at, rows, reach):
    patch, patches = lax.axis_index("patch"), lax.axis_size("patch")
    if at < reach:
        return jnp.where(patch == 0, 0.0, 1.0).astype(F32)
    if at >= reach + rows:
        return jnp.where(patch == patches - 1, 0.0, 1.0).astype(F32)
    return None


def mixer(cols_ref, rows_ref, chans):
    sign = jnp.where(lax.axis_index("cfg") == 0, 1.0, -1.0).astype(F32)
    steer = rows_ref[7:8, 0:1] * sign

    def mix(mine, other):
        shift = twice(cols_ref[4])
        mine = half_act(mine.astype(F32), twice(cols_ref[0]), twice(cols_ref[1]), shift)
        other = half_act(other.astype(F32), twice(cols_ref[2]), twice(cols_ref[3]), shift)
        return mine + steer * (mine - other)

    return mix


def matmul(weight_ref, taps, first_tap):
    depth = taps.shape[0]
    start = first_tap * (weight_ref.shape[1] // 3)
    return jnp.dot(weight_ref[:, start : start + depth], taps, preferred_element_type=F32)


def inner_kernel(
    own_ref, far_ref, seen_ref, rows_ref, raw_ref,
    steered_ref, taps_ref, cols_ref, weight_ref,
):
    rows, chans, cols = own_ref.shape
    turn(raw_ref, weight_ref)
    wide = padded_lanes(chans)
    size = chans // GROUPS
    mask = same_group(wide, size)
    bases = (0, seen_ref.shape[1] // 2)
    means = [get_rows(seen_ref, 0, chans, base) for base in bases]
    squares = [get_rows(seen_ref, 1, chans, base) for base in bases]
    mean_rows, var_rows = group_stats(means, squares, float(rows * cols), mask, size)
    scale_rows = lax.rsqrt(var_rows + EPS) * (0.5 * rows_ref[0:1])
    times = jnp.sum(get_rows(seen_ref, 2, chans), axis=0, keepdims=True)
    added = times + (rows_ref[3:4] + rows_ref[2:3])
    spread_columns(
        [mean_rows[0:1], scale_rows[0:1], mean_rows[1:2], scale_rows[1:2], 0.5 * rows_ref[1:2], added],
        chans, cols_ref,
    )
    mix = mixer(cols_ref, rows_ref, chans)
    line = 3 * chans
    if rows < 3:
        steered_ref[...] = jnp.zeros_like(steered_ref)
    for at in range(rows):
        put_taps(taps_ref, at, mix(own_ref[at], far_ref[at]))
        if at >= 2:
            total = matmul(weight_ref, taps_ref[(at - 2) * line : (at + 1) * line, :], 0)
            steered_ref[at - 2] = total + twice(cols_ref[5])


def outer_kernel(
    near_ref, next_ref, far_near_ref, far_next_ref, inner_ref, inner_taps_ref, cols_ref, rows_ref, weight_ref, raw_ref,
    steered_ref, out_ref, turned_ref,
    taps_ref, edge_ref,
):
    reach, chans, cols = near_ref.shape
    line = 3 * chans
    rows = inner_taps_ref.shape[0] // line
    above = jnp.where(lax.rem(lax.axis_index("patch"), 2) == 0, reach, 0)
    edge_ref[0, pl.ds(above, reach)] = next_ref[...]
    edge_ref[1, pl.ds(above, reach)] = far_next_ref[...]
    edge_ref[0, pl.ds(reach - above, reach)] = near_ref[...]
    edge_ref[1, pl.ds(reach - above, reach)] = far_near_ref[...]
    mix = mixer(cols_ref, rows_ref, chans)

    def taps(at):
        if reach <= at < reach + rows:
            return inner_taps_ref, at - reach
        return taps_ref, at if at < reach else at - rows

    def rows_of(first, count):
        ref, at = taps(first)
        return ref[at * line : (at + count) * line, :]

    def conv(at):
        total, tap = None, 0
        while tap < 3:
            ref, _ = taps(at + tap)
            count = 1
            while tap + count < 3 and taps(at + tap + count)[0] is ref:
                count += 1
            part = matmul(weight_ref, rows_of(at + tap, count), tap)
            total = part if total is None else total + part
            tap += count
        return total

    def enter(at):
        k = reach + at if at < reach else at - reach - rows
        keep = edge_keep(at, rows, reach)
        put_taps(taps_ref, taps(at)[1], mix(edge_ref[0, k], edge_ref[1, k]) * keep)

    for at in range(reach):
        enter(at)
    outside = [at for at in range(rows + 2 * reach - 2) if not reach <= at < reach + rows - 2]
    place = {at: k for k, at in enumerate(outside)}
    ready = reach + rows
    for at in outside:
        while ready < at + 3:
            enter(ready)
            ready += 1
        steered_ref[place[at]] = conv(at) + twice(cols_ref[5])
    turn(raw_ref, turned_ref)

    def own_rows():
        for k in range(rows):
            at = reach - 1 + k
            yield steered_ref[place[at]] if at in place else inner_ref[at - reach]

    mean, square = channel_moments(own_rows, chans)
    put_rows([mean, square], out_ref)


def second_kernel(
    inner_ref, outer_ref, lat_ref, seen_ref, rows_ref, weight_ref,
    out_ref,
    taps_ref, cols_ref,
):
    rows, chans, cols = lat_ref.shape
    wide = padded_lanes(chans)
    size = chans // GROUPS
    mask = same_group(wide, size)
    mean_rows, var_rows = group_stats(
        [get_rows(seen_ref, 0, chans)], [get_rows(seen_ref, 1, chans)],
        float(rows * cols), mask, size,
    )
    scale_rows = lax.rsqrt(var_rows + EPS) * (0.5 * rows_ref[4:5])
    spread_columns(
        [mean_rows[0:1], scale_rows[0:1], 0.5 * rows_ref[5:6], rows_ref[6:7]], chans, cols_ref
    )
    line = 3 * chans
    inside = max(rows - 2, 0)
    half = outer_ref.shape[0] // 2
    for at in range(rows + 2):
        if half <= at < half + inside:
            value = inner_ref[at - half]
        else:
            value = outer_ref[at if at < half else at - inside]
        value = half_act(value, twice(cols_ref[0]), twice(cols_ref[1]), twice(cols_ref[2]))
        keep = edge_keep(at, rows, 1)
        put_taps(taps_ref, at, value if keep is None else value * keep)
        if at >= 2:
            total = matmul(weight_ref, taps_ref[(at - 2) * line : (at + 1) * line, :], 0)
            out_ref[at - 2] = (lat_ref[at - 2].astype(F32) + (total + twice(cols_ref[3]))).astype(BF16)


def everyone(tiles, axes):
    return lax.all_to_all(tiles, axes, 0, 0)


VMEM = pl.BlockSpec(memory_space=pltpu.VMEM)
SMEM = pl.BlockSpec(memory_space=pltpu.SMEM)
ANY = pl.BlockSpec(memory_space=pl.ANY)
LIMIT = pltpu.CompilerParams(vmem_limit_bytes=12 * 1024 * 1024)


def in_hbm(value):
    return pltpu.with_memory_space_constraint(value, pltpu.HBM)


def body(
    latents, time_embed, steer_scale, gain_one, shift_one, conv_one, bias_one,
    time_weight, time_bias, gain_two, shift_two, conv_two, bias_two,
):
    own = jnp.swapaxes(latents[0, 0], 1, 2)
    rows, chans, cols = own.shape
    wide = padded_lanes(chans)
    deep = 9 * chans
    patches = lax.axis_size("patch")
    swap = [(0, 1), (1, 0)]
    tile_one = tile_height(chans, 3)
    held, tile, near_edge, next_edge, vectors, raw_one = pl.pallas_call(
        stats_kernel,
        out_shape=[
            pltpu.VMEM((rows, chans, cols), BF16),
            pltpu.VMEM((tile_one, LANES), F32),
            pltpu.VMEM((REACH, chans, cols), BF16),
            pltpu.VMEM((REACH, chans, cols), BF16),
            pltpu.VMEM((8, wide), F32),
            pltpu.VMEM((deep, chans), BF16),
        ],
        in_specs=[ANY] * 10 + [SMEM, ANY],
        out_specs=[VMEM] * 6,
        scratch_shapes=[
            pltpu.VMEM(time_embed.shape, BF16),
            pltpu.VMEM(time_weight.shape, BF16),
            pltpu.SemaphoreType.DMA((rows + 2,)),
            pltpu.SemaphoreType.DMA((3,)),
            pltpu.SemaphoreType.DMA((7,)),
        ]
        + [pltpu.VMEM((chans,), F32)] * 7,
        compiler_params=LIMIT,
        name="stats",
    )(
        in_hbm(own), in_hbm(time_embed), in_hbm(time_weight), in_hbm(gain_one), in_hbm(shift_one),
        in_hbm(bias_one), in_hbm(time_bias), in_hbm(gain_two), in_hbm(shift_two), in_hbm(bias_two), steer_scale,
        in_hbm(conv_one.reshape(deep, chans)),
    )
    near = lax.ppermute(near_edge, "patch", [(i, i ^ 1) for i in range(patches)])
    steps = [(i, i + 1) for i in range(1, patches - 1, 2)]
    following = lax.ppermute(next_edge, "patch", steps + [(j, i) for i, j in steps])
    both = jnp.concatenate([tile, lax.ppermute(tile, "cfg", swap)], axis=0)
    seen = everyone(jnp.broadcast_to(both, (patches,) + both.shape), "patch")

    source, _ = lax.optimization_barrier((own, tile))
    far = lax.ppermute(source, "cfg", swap)
    near, following, seen = lax.optimization_barrier((near, following, seen))
    far_near = lax.ppermute(near, "cfg", swap)
    far_next = lax.ppermute(following, "cfg", swap)

    inner, taps, columns, turned_one = pl.pallas_call(
        inner_kernel,
        out_shape=[
            pltpu.VMEM((max(rows - 2, 1), chans, cols), F32),
            pltpu.VMEM((rows * 3 * chans, cols), BF16),
            pltpu.VMEM((6, chans, LANES), F32),
            pltpu.VMEM((chans, deep), BF16),
        ],
        in_specs=[VMEM] * 5,
        out_specs=[VMEM] * 4,
        compiler_params=LIMIT,
        name="inner",
    )(held, far, seen, vectors, raw_one)
    tile_two = tile_height(chans, 2)
    outer, sent, turned_two = pl.pallas_call(
        outer_kernel,
        out_shape=[
            pltpu.VMEM((2 * REACH, chans, cols), F32),
            pltpu.VMEM((patches, tile_two, LANES), F32),
            pltpu.VMEM((chans, deep), BF16),
        ],
        in_specs=[VMEM] * 10,
        out_specs=[VMEM] * 3,
        scratch_shapes=[
            pltpu.VMEM((2 * REACH * 3 * chans, cols), BF16),
            pltpu.VMEM((2, 2 * REACH, chans, cols), BF16),
        ],
        compiler_params=LIMIT,
        name="outer",
    )(
        near, following, far_near, far_next, inner, taps, columns, vectors, turned_one,
        conv_two.reshape(deep, chans),
    )
    seen = everyone(sent, "patch")
    image = pl.pallas_call(
        second_kernel,
        out_shape=jax.ShapeDtypeStruct((rows, chans, cols), BF16),
        in_specs=[VMEM] * 6,
        out_specs=VMEM,
        scratch_shapes=[
            pltpu.VMEM(((rows + 2) * 3 * chans, cols), BF16),
            pltpu.VMEM((4, chans, LANES), F32),
        ],
        compiler_params=LIMIT,
        name="second",
    )(inner, outer, held, seen, vectors, turned_two)
    return jnp.swapaxes(image, 1, 2)[None, None]


def solution(mesh):
    placed = (
        P("cfg", "req", "patch", None, None), P("req", None), P("req"), P(), P(), P(), P(),
        P("patch", None), P(), P(), P(), P(), P(),
    )
    return jax.shard_map(
        body,
        mesh=mesh,
        in_specs=placed,
        out_specs=P("cfg", "req", "patch", None, None),
        check_vma=False,
    )
```

```python
import functools

import jax
import jax.numpy as jnp
from jax import lax
from jax.experimental import pallas as pl
from jax.experimental.pallas import tpu as pltpu
from jax.sharding import PartitionSpec as P

GROUPS = 32
EPS = 1e-05
REACH = 2
LANES = 128
F32 = jnp.float32
BF16 = jnp.bfloat16


def padded_lanes(chans):
    return -(-chans // LANES) * LANES


def widen(row, wide):
    short = wide - row.shape[1]
    if not short:
        return row
    return jnp.concatenate([row, jnp.zeros((row.shape[0], short), row.dtype)], axis=1)


def same_group(wide, size):
    left = lax.broadcasted_iota(jnp.int32, (wide, wide), 0).astype(F32)
    right = lax.broadcasted_iota(jnp.int32, (wide, wide), 1).astype(F32)
    group = lambda at: jnp.floor((at + 0.5) * (1.0 / size))
    return jnp.where(group(left) == group(right), 1.0, 0.0).astype(BF16)


def group_sum(rows, mask):
    high = rows.astype(BF16).astype(F32)
    rest = rows - high
    middle = rest.astype(BF16).astype(F32)
    pieces = jnp.concatenate([high, middle, rest - middle, jnp.zeros_like(rows)], axis=0).astype(BF16)
    sums = jnp.dot(pieces, mask, preferred_element_type=F32)
    return sums[0:8] + sums[8:16] + sums[16:24]


def stack_rows(rows, wide):
    filler = [jnp.zeros((8 - len(rows), wide), F32)] if len(rows) < 8 else []
    return jnp.concatenate(list(rows) + filler, axis=0)


def group_stats(means, squares, count, mask, size):
    wide = mask.shape[0]
    peers = means[0].shape[0]
    mean_rows = [jnp.sum(m, axis=0, keepdims=True) * (1.0 / peers) for m in means]
    mean_rows = group_sum(stack_rows(mean_rows, wide), mask) * (1.0 / size)
    spread = []
    for k, (m, q) in enumerate(zip(means, squares)):
        off = m - mean_rows[k : k + 1]
        spread.append(jnp.sum(q + count * (off * off), axis=0, keepdims=True))
    var_rows = group_sum(stack_rows(spread, wide), mask) * (1.0 / (size * count * peers))
    return mean_rows, var_rows


def fold(values):
    total = values[:, :LANES]
    for at in range(LANES, values.shape[1], LANES):
        total = total + values[:, at : at + LANES]
    return total


def channel_moments(rows, chans):
    count = 0
    total = None
    for row in rows():
        part = fold(row)
        count += row.shape[1]
        total = part if total is None else total + part
    mean = jnp.sum(total, axis=1, keepdims=True) * (1.0 / count)
    squares = None
    for row in rows():
        off = row - mean
        part = fold(off * off)
        squares = part if squares is None else squares + part
    squares = jnp.sum(squares, axis=1, keepdims=True)
    lane = lax.broadcasted_iota(jnp.int32, (chans, LANES), 1)
    both = jnp.where(lane == 0, mean, jnp.where(lane == 1, squares, 0.0))
    wide = padded_lanes(chans)
    both = jnp.concatenate([both, jnp.zeros((wide - chans, LANES), F32)], axis=0)
    turned = both.T
    return turned[0:1, :chans], turned[1:2, :chans]


def put_rows(tile_rows, out_ref):
    height = out_ref.shape[-2]
    flat = widen(jnp.concatenate(tile_rows, axis=1), height * LANES)
    tile = jnp.concatenate([flat[:, at : at + LANES] for at in range(0, height * LANES, LANES)], axis=0)
    out_ref[...] = jnp.broadcast_to(tile, out_ref.shape)


def get_rows(seen_ref, which, chans, base=0):
    start, end = which * chans, (which + 1) * chans
    lines = range(start // LANES, -(-end // LANES))
    flat = jnp.concatenate([seen_ref[:, base + k, :] for k in lines], axis=1)
    start -= lines[0] * LANES
    return widen(flat[:, start : start + chans], padded_lanes(chans))


def tile_height(chans, rows):
    return -(-(rows * chans + 1) // LANES // 8) * 8


def fetch(pairs, sems, first=0):
    copies = [pltpu.make_async_copy(a, b, sems.at[first + k]) for k, (a, b) in enumerate(pairs)]
    for copy in copies:
        copy.start()
    return copies


def stats_kernel(
    lat_hbm, embed_hbm, weight_hbm, gain_one, shift_one, bias_one, time_bias, gain_two, shift_two, bias_two, conv_hbm,
    lat_ref, out_ref, near_ref, next_ref, rows_ref, conv_ref,
    embed_ref, weight_ref, sems, edge_sems, row_sems, *vector_refs,
):
    rows, chans, _ = lat_ref.shape
    reach = near_ref.shape[0]
    last = rows - reach
    near_at = jnp.where(lax.rem(lax.axis_index("patch"), 2) == 0, last, 0)
    copies = fetch(
        [(lat_hbm.at[k], lat_ref.at[k]) for k in range(rows)]
        + [(embed_hbm, embed_ref), (weight_hbm, weight_ref)],
        sems,
    )
    vectors = (gain_one, shift_one, bias_one, time_bias, gain_two, shift_two, bias_two)
    copies += fetch(zip(vectors, vector_refs), row_sems)
    edges = fetch(
        [
            (lat_hbm.at[pl.ds(near_at, reach)], near_ref),
            (lat_hbm.at[pl.ds(last - near_at, reach)], next_ref),
            (conv_hbm, conv_ref),
        ],
        edge_sems,
    )
    for copy in copies:
        copy.wait()
    mean, squares = channel_moments(lambda: (lat_ref[k].astype(F32) for k in range(rows)), chans)
    own = weight_ref.shape[0]
    length = embed_ref.shape[1]
    embed = jnp.broadcast_to(embed_ref[...].astype(F32), (8, length))
    embed = pltpu.roll(embed, length - lax.axis_index("patch") * own, 1)[:, :own]
    act = (embed / (1.0 + jnp.exp(-embed))).astype(BF16)
    time_part = jnp.dot(act, weight_ref[...], preferred_element_type=F32)[0:1]
    put_rows([mean, squares, time_part], out_ref)
    wide = rows_ref.shape[1]
    lines = [widen(v[...].reshape(1, -1), wide) for v in vector_refs]
    rows_ref[...] = stack_rows(lines, wide)
    for copy in edges:
        copy.wait()


def turn(source, target, part=8 * LANES):
    deep = source.shape[0]
    for at in range(0, deep, part):
        size = min(part, deep - at)
        target[:, at : at + size] = source[at : at + size, :].T


def spread_columns(rows, chans, cols_ref):
    turned = stack_rows(rows, rows[0].shape[1]).T
    for k in range(len(rows)):
        cols_ref[k] = jnp.broadcast_to(turned[:chans, k : k + 1], (chans, LANES))


def half_act(values, mean, scale, shift):
    half = (values - mean) * scale + shift
    return half * jnp.tanh(half) + half


def twice(column):
    return jnp.concatenate([column, column], axis=1)


def put_taps(taps_ref, at, row):
    chans, cols = row.shape
    lane = lax.broadcasted_iota(jnp.int32, (chans, cols), 1)
    before = jnp.where(lane == 0, 0.0, pltpu.roll(row, 1, 1))
    after = jnp.where(lane == cols - 1, 0.0, pltpu.roll(row, cols - 1, 1))
    for k, value in enumerate((before, row, after)):
        taps_ref[pl.ds((at * 3 + k) * chans, chans), :] = value.astype(BF16)


def edge_keep(at, rows, reach):
    patch, patches = lax.axis_index("patch"), lax.axis_size("patch")
    if at < reach:
        return jnp.where(patch == 0, 0.0, 1.0).astype(F32)
    if at >= reach + rows:
        return jnp.where(patch == patches - 1, 0.0, 1.0).astype(F32)
    return None


def mixer(cols_ref, steer_ref):
    line = steer_ref.shape[1] // 2 - 1
    sign = jnp.where(lax.axis_index("cfg") == 0, 1.0, -1.0).astype(F32)
    steer = steer_ref[0, line : line + 1, LANES - 1 :] * sign

    def mix(mine, other):
        shift = twice(cols_ref[4])
        mine = half_act(mine.astype(F32), twice(cols_ref[0]), twice(cols_ref[1]), shift)
        other = half_act(other.astype(F32), twice(cols_ref[2]), twice(cols_ref[3]), shift)
        return mine + steer * (mine - other)

    return mix


def matmul(weight_ref, taps, first_tap):
    depth = taps.shape[0]
    start = first_tap * (weight_ref.shape[1] // 3)
    return jnp.dot(weight_ref[:, start : start + depth], taps, preferred_element_type=F32)


def inner_kernel(
    own_ref, far_ref, seen_ref, rows_ref, raw_ref,
    steered_ref, taps_ref, cols_ref, weight_ref,
):
    rows, chans, cols = own_ref.shape
    turn(raw_ref, weight_ref)
    wide = padded_lanes(chans)
    size = chans // GROUPS
    mask = same_group(wide, size)
    bases = (0, seen_ref.shape[1] // 2)
    means = [get_rows(seen_ref, 0, chans, base) for base in bases]
    squares = [get_rows(seen_ref, 1, chans, base) for base in bases]
    mean_rows, var_rows = group_stats(means, squares, float(rows * cols), mask, size)
    scale_rows = lax.rsqrt(var_rows + EPS) * (0.5 * rows_ref[0:1])
    times = jnp.sum(get_rows(seen_ref, 2, chans), axis=0, keepdims=True)
    added = times + (rows_ref[3:4] + rows_ref[2:3])
    spread_columns(
        [mean_rows[0:1], scale_rows[0:1], mean_rows[1:2], scale_rows[1:2], 0.5 * rows_ref[1:2], added],
        chans, cols_ref,
    )
    mix = mixer(cols_ref, seen_ref)
    line = 3 * chans
    if rows < 3:
        steered_ref[...] = jnp.zeros_like(steered_ref)
    for at in range(rows):
        put_taps(taps_ref, at, mix(own_ref[at], far_ref[at]))
        if at >= 2:
            total = matmul(weight_ref, taps_ref[(at - 2) * line : (at + 1) * line, :], 0)
            steered_ref[at - 2] = total + twice(cols_ref[5])


def outer_kernel(
    near_ref, next_ref, far_near_ref, far_next_ref, inner_ref, inner_taps_ref, cols_ref, weight_ref, raw_ref,
    steer_ref,
    steered_ref, out_ref, turned_ref,
    taps_ref, edge_ref,
):
    reach, chans, cols = near_ref.shape
    line = 3 * chans
    rows = inner_taps_ref.shape[0] // line
    above = jnp.where(lax.rem(lax.axis_index("patch"), 2) == 0, reach, 0)
    edge_ref[0, pl.ds(above, reach)] = next_ref[...]
    edge_ref[1, pl.ds(above, reach)] = far_next_ref[...]
    edge_ref[0, pl.ds(reach - above, reach)] = near_ref[...]
    edge_ref[1, pl.ds(reach - above, reach)] = far_near_ref[...]
    mix = mixer(cols_ref, steer_ref)

    def taps(at):
        if reach <= at < reach + rows:
            return inner_taps_ref, at - reach
        return taps_ref, at if at < reach else at - rows

    def rows_of(first, count):
        ref, at = taps(first)
        return ref[at * line : (at + count) * line, :]

    def conv(at):
        total, tap = None, 0
        while tap < 3:
            ref, _ = taps(at + tap)
            count = 1
            while tap + count < 3 and taps(at + tap + count)[0] is ref:
                count += 1
            part = matmul(weight_ref, rows_of(at + tap, count), tap)
            total = part if total is None else total + part
            tap += count
        return total

    def enter(at):
        k = reach + at if at < reach else at - reach - rows
        keep = edge_keep(at, rows, reach)
        put_taps(taps_ref, taps(at)[1], mix(edge_ref[0, k], edge_ref[1, k]) * keep)

    for at in range(reach):
        enter(at)
    outside = [at for at in range(rows + 2 * reach - 2) if not reach <= at < reach + rows - 2]
    place = {at: k for k, at in enumerate(outside)}
    ready = reach + rows
    for at in outside:
        while ready < at + 3:
            enter(ready)
            ready += 1
        steered_ref[place[at]] = conv(at) + twice(cols_ref[5])
    turn(raw_ref, turned_ref)

    def own_rows():
        for k in range(rows):
            at = reach - 1 + k
            yield steered_ref[place[at]] if at in place else inner_ref[at - reach]

    mean, square = channel_moments(own_rows, chans)
    put_rows([mean, square], out_ref)


def second_kernel(
    inner_ref, outer_ref, lat_ref, seen_ref, rows_ref, weight_ref,
    out_ref,
    taps_ref, cols_ref,
):
    rows, chans, cols = lat_ref.shape
    wide = padded_lanes(chans)
    size = chans // GROUPS
    mask = same_group(wide, size)
    mean_rows, var_rows = group_stats(
        [get_rows(seen_ref, 0, chans)], [get_rows(seen_ref, 1, chans)],
        float(rows * cols), mask, size,
    )
    scale_rows = lax.rsqrt(var_rows + EPS) * (0.5 * rows_ref[4:5])
    spread_columns(
        [mean_rows[0:1], scale_rows[0:1], 0.5 * rows_ref[5:6], rows_ref[6:7]], chans, cols_ref
    )
    line = 3 * chans
    inside = max(rows - 2, 0)
    half = outer_ref.shape[0] // 2
    for at in range(rows + 2):
        if half <= at < half + inside:
            value = inner_ref[at - half]
        else:
            value = outer_ref[at if at < half else at - inside]
        value = half_act(value, twice(cols_ref[0]), twice(cols_ref[1]), twice(cols_ref[2]))
        keep = edge_keep(at, rows, 1)
        put_taps(taps_ref, at, value if keep is None else value * keep)
        if at >= 2:
            total = matmul(weight_ref, taps_ref[(at - 2) * line : (at + 1) * line, :], 0)
            out_ref[at - 2] = (lat_ref[at - 2].astype(F32) + (total + twice(cols_ref[3]))).astype(BF16)


def everyone(tiles, axes):
    return lax.all_to_all(tiles, axes, 0, 0)


VMEM = pl.BlockSpec(memory_space=pltpu.VMEM)
SMEM = pl.BlockSpec(memory_space=pltpu.SMEM)
ANY = pl.BlockSpec(memory_space=pl.ANY)
LIMIT = pltpu.CompilerParams(vmem_limit_bytes=12 * 1024 * 1024)


def in_hbm(value):
    return pltpu.with_memory_space_constraint(value, pltpu.HBM)


def body(
    latents, time_embed, steer_scale, gain_one, shift_one, conv_one, bias_one,
    time_weight, time_bias, gain_two, shift_two, conv_two, bias_two,
):
    own = jnp.swapaxes(latents[0, 0], 1, 2)
    rows, chans, cols = own.shape
    wide = padded_lanes(chans)
    deep = 9 * chans
    patches = lax.axis_size("patch")
    swap = [(0, 1), (1, 0)]
    tile_one = tile_height(chans, 3)
    held, tile, near_edge, next_edge, vectors, raw_one = pl.pallas_call(
        stats_kernel,
        out_shape=[
            pltpu.VMEM((rows, chans, cols), BF16),
            pltpu.VMEM((tile_one, LANES), F32),
            pltpu.VMEM((REACH, chans, cols), BF16),
            pltpu.VMEM((REACH, chans, cols), BF16),
            pltpu.VMEM((8, wide), F32),
            pltpu.VMEM((deep, chans), BF16),
        ],
        in_specs=[ANY] * 11,
        out_specs=[VMEM] * 6,
        scratch_shapes=[
            pltpu.VMEM(time_embed.shape, BF16),
            pltpu.VMEM(time_weight.shape, BF16),
            pltpu.SemaphoreType.DMA((rows + 2,)),
            pltpu.SemaphoreType.DMA((3,)),
            pltpu.SemaphoreType.DMA((7,)),
        ]
        + [pltpu.VMEM((chans,), F32)] * 7,
        compiler_params=LIMIT,
        name="stats",
    )(
        in_hbm(own), in_hbm(time_embed), in_hbm(time_weight), in_hbm(gain_one), in_hbm(shift_one),
        in_hbm(bias_one), in_hbm(time_bias), in_hbm(gain_two), in_hbm(shift_two), in_hbm(bias_two),
        in_hbm(conv_one.reshape(deep, chans)),
    )
    other = lax.ppermute(tile, "cfg", swap)
    next_edge, other = lax.optimization_barrier((next_edge, other))
    near = lax.ppermute(near_edge, "patch", [(i, i ^ 1) for i in range(patches)])
    steps = [(i, i + 1) for i in range(1, patches - 1, 2)]
    following = lax.ppermute(next_edge, "patch", steps + [(j, i) for i, j in steps])
    both = jnp.concatenate([tile, other], axis=0)
    free = (jnp.arange(2 * tile_one) == tile_one - 1)[:, None] & (jnp.arange(LANES) == LANES - 1)
    both = jnp.where(free, steer_scale[0], both)
    seen = everyone(jnp.broadcast_to(both, (patches,) + both.shape), "patch")

    source, _ = lax.optimization_barrier((own, tile))
    far = lax.ppermute(source, "cfg", swap)
    near, following, seen = lax.optimization_barrier((near, following, seen))
    far_near = lax.ppermute(near, "cfg", swap)
    far_next = lax.ppermute(following, "cfg", swap)

    inner, taps, columns, turned_one = pl.pallas_call(
        inner_kernel,
        out_shape=[
            pltpu.VMEM((max(rows - 2, 1), chans, cols), F32),
            pltpu.VMEM((rows * 3 * chans, cols), BF16),
            pltpu.VMEM((6, chans, LANES), F32),
            pltpu.VMEM((chans, deep), BF16),
        ],
        in_specs=[VMEM] * 5,
        out_specs=[VMEM] * 4,
        compiler_params=LIMIT,
        name="inner",
    )(held, far, seen, vectors, raw_one)
    tile_two = tile_height(chans, 2)
    outer, sent, turned_two = pl.pallas_call(
        outer_kernel,
        out_shape=[
            pltpu.VMEM((2 * REACH, chans, cols), F32),
            pltpu.VMEM((patches, tile_two, LANES), F32),
            pltpu.VMEM((chans, deep), BF16),
        ],
        in_specs=[VMEM] * 10,
        out_specs=[VMEM] * 3,
        scratch_shapes=[
            pltpu.VMEM((2 * REACH * 3 * chans, cols), BF16),
            pltpu.VMEM((2, 2 * REACH, chans, cols), BF16),
        ],
        compiler_params=LIMIT,
        name="outer",
    )(
        near, following, far_near, far_next, inner, taps, columns, turned_one,
        conv_two.reshape(deep, chans), seen,
    )
    seen = everyone(sent, "patch")
    image = pl.pallas_call(
        second_kernel,
        out_shape=jax.ShapeDtypeStruct((rows, chans, cols), BF16),
        in_specs=[VMEM] * 6,
        out_specs=VMEM,
        scratch_shapes=[
            pltpu.VMEM(((rows + 2) * 3 * chans, cols), BF16),
            pltpu.VMEM((4, chans, LANES), F32),
        ],
        compiler_params=LIMIT,
        name="second",
    )(inner, outer, held, seen, vectors, turned_two)
    return jnp.swapaxes(image, 1, 2)[None, None]


def solution(mesh):
    placed = (
        P("cfg", "req", "patch", None, None), P("req", None), P("req"), P(), P(), P(), P(),
        P("patch", None), P(), P(), P(), P(), P(),
    )
    return jax.shard_map(
        body,
        mesh=mesh,
        in_specs=placed,
        out_specs=P("cfg", "req", "patch", None, None),
        check_vma=False,
    )
```

```python
import functools

import jax
import jax.numpy as jnp
from jax import lax
from jax.experimental import pallas as pl
from jax.experimental.pallas import tpu as pltpu
from jax.sharding import PartitionSpec as P

GROUPS = 32
EPS = 1e-05
REACH = 2
LANES = 128
F32 = jnp.float32
BF16 = jnp.bfloat16


def padded_lanes(chans):
    return -(-chans // LANES) * LANES


def widen(row, wide):
    short = wide - row.shape[1]
    if not short:
        return row
    return jnp.concatenate([row, jnp.zeros((row.shape[0], short), row.dtype)], axis=1)


def same_group(wide, size):
    left = lax.broadcasted_iota(jnp.int32, (wide, wide), 0).astype(F32)
    right = lax.broadcasted_iota(jnp.int32, (wide, wide), 1).astype(F32)
    group = lambda at: jnp.floor((at + 0.5) * (1.0 / size))
    return jnp.where(group(left) == group(right), 1.0, 0.0).astype(BF16)


def group_sum(rows, mask):
    high = rows.astype(BF16).astype(F32)
    rest = rows - high
    middle = rest.astype(BF16).astype(F32)
    pieces = jnp.concatenate([high, middle, rest - middle, jnp.zeros_like(rows)], axis=0).astype(BF16)
    sums = jnp.dot(pieces, mask, preferred_element_type=F32)
    return sums[0:8] + sums[8:16] + sums[16:24]


def stack_rows(rows, wide):
    filler = [jnp.zeros((8 - len(rows), wide), F32)] if len(rows) < 8 else []
    return jnp.concatenate(list(rows) + filler, axis=0)


def group_stats(means, squares, count, mask, size):
    wide = mask.shape[0]
    peers = means[0].shape[0]
    mean_rows = [jnp.sum(m, axis=0, keepdims=True) * (1.0 / peers) for m in means]
    mean_rows = group_sum(stack_rows(mean_rows, wide), mask) * (1.0 / size)
    spread = []
    for k, (m, q) in enumerate(zip(means, squares)):
        off = m - mean_rows[k : k + 1]
        spread.append(jnp.sum(q + count * (off * off), axis=0, keepdims=True))
    var_rows = group_sum(stack_rows(spread, wide), mask) * (1.0 / (size * count * peers))
    return mean_rows, var_rows


def fold(values):
    total = values[:, :LANES]
    for at in range(LANES, values.shape[1], LANES):
        total = total + values[:, at : at + LANES]
    return total


def channel_moments(rows, chans):
    count = 0
    total = None
    for row in rows():
        part = fold(row)
        count += row.shape[1]
        total = part if total is None else total + part
    mean = jnp.sum(total, axis=1, keepdims=True) * (1.0 / count)
    squares = None
    for row in rows():
        off = row - mean
        part = fold(off * off)
        squares = part if squares is None else squares + part
    squares = jnp.sum(squares, axis=1, keepdims=True)
    lane = lax.broadcasted_iota(jnp.int32, (chans, LANES), 1)
    both = jnp.where(lane == 0, mean, jnp.where(lane == 1, squares, 0.0))
    wide = padded_lanes(chans)
    both = jnp.concatenate([both, jnp.zeros((wide - chans, LANES), F32)], axis=0)
    turned = both.T
    return turned[0:1, :chans], turned[1:2, :chans]


def put_rows(tile_rows, out_ref):
    height = out_ref.shape[-2]
    flat = widen(jnp.concatenate(tile_rows, axis=1), height * LANES)
    tile = jnp.concatenate([flat[:, at : at + LANES] for at in range(0, height * LANES, LANES)], axis=0)
    out_ref[...] = jnp.broadcast_to(tile, out_ref.shape)


def get_rows(seen_ref, which, chans, base=0):
    start, end = which * chans, (which + 1) * chans
    lines = range(start // LANES, -(-end // LANES))
    flat = jnp.concatenate([seen_ref[:, base + k, :] for k in lines], axis=1)
    start -= lines[0] * LANES
    return widen(flat[:, start : start + chans], padded_lanes(chans))


def tile_height(chans, rows):
    return -(-(rows * chans + 1) // LANES // 8) * 8


def fetch(pairs, sems, first=0):
    copies = [pltpu.make_async_copy(a, b, sems.at[first + k]) for k, (a, b) in enumerate(pairs)]
    for copy in copies:
        copy.start()
    return copies


def near_at(lat_hbm, reach):
    return jnp.where(lax.rem(lax.axis_index("patch"), 2) == 0, lat_hbm.shape[0] - reach, 0)


def edge_kernel(lat_hbm, near_ref, sem):
    reach = near_ref.shape[0]
    copy = pltpu.make_async_copy(lat_hbm.at[pl.ds(near_at(lat_hbm, reach), reach)], near_ref, sem)
    copy.start()
    copy.wait()


def stats_kernel(
    lat_hbm, embed_hbm, weight_hbm, gain_one, shift_one, bias_one, time_bias, gain_two, shift_two, bias_two, conv_hbm,
    lat_ref, out_ref, next_ref, rows_ref, conv_ref,
    embed_ref, weight_ref, sems, edge_sems, row_sems, *vector_refs,
):
    rows, chans, _ = lat_ref.shape
    reach = next_ref.shape[0]
    next_at = rows - reach - near_at(lat_hbm, reach)
    copies = fetch(
        [(lat_hbm.at[k], lat_ref.at[k]) for k in range(rows)]
        + [(embed_hbm, embed_ref), (weight_hbm, weight_ref)],
        sems,
    )
    vectors = (gain_one, shift_one, bias_one, time_bias, gain_two, shift_two, bias_two)
    copies += fetch(zip(vectors, vector_refs), row_sems)
    edges = fetch(
        [
            (lat_hbm.at[pl.ds(next_at, reach)], next_ref),
            (conv_hbm, conv_ref),
        ],
        edge_sems,
    )
    for copy in copies:
        copy.wait()
    mean, squares = channel_moments(lambda: (lat_ref[k].astype(F32) for k in range(rows)), chans)
    own = weight_ref.shape[0]
    length = embed_ref.shape[1]
    embed = jnp.broadcast_to(embed_ref[...].astype(F32), (8, length))
    embed = pltpu.roll(embed, length - lax.axis_index("patch") * own, 1)[:, :own]
    act = (embed / (1.0 + jnp.exp(-embed))).astype(BF16)
    time_part = jnp.dot(act, weight_ref[...], preferred_element_type=F32)[0:1]
    put_rows([mean, squares, time_part], out_ref)
    wide = rows_ref.shape[1]
    lines = [widen(v[...].reshape(1, -1), wide) for v in vector_refs]
    rows_ref[...] = stack_rows(lines, wide)
    for copy in edges:
        copy.wait()


def turn(source, target, part=8 * LANES):
    deep = source.shape[0]
    for at in range(0, deep, part):
        size = min(part, deep - at)
        target[:, at : at + size] = source[at : at + size, :].T


def spread_columns(rows, chans, cols_ref):
    turned = stack_rows(rows, rows[0].shape[1]).T
    for k in range(len(rows)):
        cols_ref[k] = jnp.broadcast_to(turned[:chans, k : k + 1], (chans, LANES))


def half_act(values, mean, scale, shift):
    half = (values - mean) * scale + shift
    return half * jnp.tanh(half) + half


def twice(column):
    return jnp.concatenate([column, column], axis=1)


def put_taps(taps_ref, at, row):
    chans, cols = row.shape
    lane = lax.broadcasted_iota(jnp.int32, (chans, cols), 1)
    before = jnp.where(lane == 0, 0.0, pltpu.roll(row, 1, 1))
    after = jnp.where(lane == cols - 1, 0.0, pltpu.roll(row, cols - 1, 1))
    for k, value in enumerate((before, row, after)):
        taps_ref[pl.ds((at * 3 + k) * chans, chans), :] = value.astype(BF16)


def edge_keep(at, rows, reach):
    patch, patches = lax.axis_index("patch"), lax.axis_size("patch")
    if at < reach:
        return jnp.where(patch == 0, 0.0, 1.0).astype(F32)
    if at >= reach + rows:
        return jnp.where(patch == patches - 1, 0.0, 1.0).astype(F32)
    return None


def mixer(cols_ref, steer_ref):
    line = steer_ref.shape[1] // 2 - 1
    sign = jnp.where(lax.axis_index("cfg") == 0, 1.0, -1.0).astype(F32)
    steer = steer_ref[0, line : line + 1, LANES - 1 :] * sign

    def mix(mine, other):
        shift = twice(cols_ref[4])
        mine = half_act(mine.astype(F32), twice(cols_ref[0]), twice(cols_ref[1]), shift)
        other = half_act(other.astype(F32), twice(cols_ref[2]), twice(cols_ref[3]), shift)
        return mine + steer * (mine - other)

    return mix


def matmul(weight_ref, taps, first_tap):
    depth = taps.shape[0]
    start = first_tap * (weight_ref.shape[1] // 3)
    return jnp.dot(weight_ref[:, start : start + depth], taps, preferred_element_type=F32)


def inner_kernel(
    own_ref, far_ref, seen_ref, rows_ref, raw_ref,
    steered_ref, taps_ref, cols_ref, weight_ref,
):
    rows, chans, cols = own_ref.shape
    turn(raw_ref, weight_ref)
    wide = padded_lanes(chans)
    size = chans // GROUPS
    mask = same_group(wide, size)
    bases = (0, seen_ref.shape[1] // 2)
    means = [get_rows(seen_ref, 0, chans, base) for base in bases]
    squares = [get_rows(seen_ref, 1, chans, base) for base in bases]
    mean_rows, var_rows = group_stats(means, squares, float(rows * cols), mask, size)
    scale_rows = lax.rsqrt(var_rows + EPS) * (0.5 * rows_ref[0:1])
    times = jnp.sum(get_rows(seen_ref, 2, chans), axis=0, keepdims=True)
    added = times + (rows_ref[3:4] + rows_ref[2:3])
    spread_columns(
        [mean_rows[0:1], scale_rows[0:1], mean_rows[1:2], scale_rows[1:2], 0.5 * rows_ref[1:2], added],
        chans, cols_ref,
    )
    mix = mixer(cols_ref, seen_ref)
    line = 3 * chans
    if rows < 3:
        steered_ref[...] = jnp.zeros_like(steered_ref)
    for at in range(rows):
        put_taps(taps_ref, at, mix(own_ref[at], far_ref[at]))
        if at >= 2:
            total = matmul(weight_ref, taps_ref[(at - 2) * line : (at + 1) * line, :], 0)
            steered_ref[at - 2] = total + twice(cols_ref[5])


def outer_kernel(
    near_ref, next_ref, far_near_ref, far_next_ref, inner_ref, inner_taps_ref, cols_ref, weight_ref, raw_ref,
    steer_ref,
    steered_ref, out_ref, turned_ref,
    taps_ref, edge_ref,
):
    reach, chans, cols = near_ref.shape
    line = 3 * chans
    rows = inner_taps_ref.shape[0] // line
    above = jnp.where(lax.rem(lax.axis_index("patch"), 2) == 0, reach, 0)
    edge_ref[0, pl.ds(above, reach)] = next_ref[...]
    edge_ref[1, pl.ds(above, reach)] = far_next_ref[...]
    edge_ref[0, pl.ds(reach - above, reach)] = near_ref[...]
    edge_ref[1, pl.ds(reach - above, reach)] = far_near_ref[...]
    mix = mixer(cols_ref, steer_ref)

    def taps(at):
        if reach <= at < reach + rows:
            return inner_taps_ref, at - reach
        return taps_ref, at if at < reach else at - rows

    def rows_of(first, count):
        ref, at = taps(first)
        return ref[at * line : (at + count) * line, :]

    def conv(at):
        total, tap = None, 0
        while tap < 3:
            ref, _ = taps(at + tap)
            count = 1
            while tap + count < 3 and taps(at + tap + count)[0] is ref:
                count += 1
            part = matmul(weight_ref, rows_of(at + tap, count), tap)
            total = part if total is None else total + part
            tap += count
        return total

    def enter(at):
        k = reach + at if at < reach else at - reach - rows
        keep = edge_keep(at, rows, reach)
        put_taps(taps_ref, taps(at)[1], mix(edge_ref[0, k], edge_ref[1, k]) * keep)

    for at in range(reach):
        enter(at)
    outside = [at for at in range(rows + 2 * reach - 2) if not reach <= at < reach + rows - 2]
    place = {at: k for k, at in enumerate(outside)}
    ready = reach + rows
    for at in outside:
        while ready < at + 3:
            enter(ready)
            ready += 1
        steered_ref[place[at]] = conv(at) + twice(cols_ref[5])
    turn(raw_ref, turned_ref)

    def own_rows():
        for k in range(rows):
            at = reach - 1 + k
            yield steered_ref[place[at]] if at in place else inner_ref[at - reach]

    mean, square = channel_moments(own_rows, chans)
    put_rows([mean, square], out_ref)


def second_kernel(
    inner_ref, outer_ref, lat_ref, seen_ref, rows_ref, weight_ref,
    out_ref,
    taps_ref, cols_ref,
):
    rows, chans, cols = lat_ref.shape
    wide = padded_lanes(chans)
    size = chans // GROUPS
    mask = same_group(wide, size)
    mean_rows, var_rows = group_stats(
        [get_rows(seen_ref, 0, chans)], [get_rows(seen_ref, 1, chans)],
        float(rows * cols), mask, size,
    )
    scale_rows = lax.rsqrt(var_rows + EPS) * (0.5 * rows_ref[4:5])
    spread_columns(
        [mean_rows[0:1], scale_rows[0:1], 0.5 * rows_ref[5:6], rows_ref[6:7]], chans, cols_ref
    )
    line = 3 * chans
    inside = max(rows - 2, 0)
    half = outer_ref.shape[0] // 2
    for at in range(rows + 2):
        if half <= at < half + inside:
            value = inner_ref[at - half]
        else:
            value = outer_ref[at if at < half else at - inside]
        value = half_act(value, twice(cols_ref[0]), twice(cols_ref[1]), twice(cols_ref[2]))
        keep = edge_keep(at, rows, 1)
        put_taps(taps_ref, at, value if keep is None else value * keep)
        if at >= 2:
            total = matmul(weight_ref, taps_ref[(at - 2) * line : (at + 1) * line, :], 0)
            out_ref[at - 2] = (lat_ref[at - 2].astype(F32) + (total + twice(cols_ref[3]))).astype(BF16)


def everyone(tiles, axes):
    return lax.all_to_all(tiles, axes, 0, 0)


VMEM = pl.BlockSpec(memory_space=pltpu.VMEM)
SMEM = pl.BlockSpec(memory_space=pltpu.SMEM)
ANY = pl.BlockSpec(memory_space=pl.ANY)
LIMIT = pltpu.CompilerParams(vmem_limit_bytes=12 * 1024 * 1024)


def in_hbm(value):
    return pltpu.with_memory_space_constraint(value, pltpu.HBM)


def body(
    latents, time_embed, steer_scale, gain_one, shift_one, conv_one, bias_one,
    time_weight, time_bias, gain_two, shift_two, conv_two, bias_two,
):
    own = jnp.swapaxes(latents[0, 0], 1, 2)
    rows, chans, cols = own.shape
    wide = padded_lanes(chans)
    deep = 9 * chans
    patches = lax.axis_size("patch")
    swap = [(0, 1), (1, 0)]
    near_edge = pl.pallas_call(
        edge_kernel,
        out_shape=pltpu.VMEM((REACH, chans, cols), BF16),
        in_specs=[ANY],
        out_specs=VMEM,
        scratch_shapes=[pltpu.SemaphoreType.DMA],
        compiler_params=LIMIT,
        name="edge",
    )(in_hbm(own))
    near = lax.ppermute(near_edge, "patch", [(i, i ^ 1) for i in range(patches)])
    time_embed, _ = lax.optimization_barrier((time_embed, near_edge))
    tile_one = tile_height(chans, 3)
    held, tile, next_edge, vectors, raw_one = pl.pallas_call(
        stats_kernel,
        out_shape=[
            pltpu.VMEM((rows, chans, cols), BF16),
            pltpu.VMEM((tile_one, LANES), F32),
            pltpu.VMEM((REACH, chans, cols), BF16),
            pltpu.VMEM((8, wide), F32),
            pltpu.VMEM((deep, chans), BF16),
        ],
        in_specs=[ANY] * 11,
        out_specs=[VMEM] * 5,
        scratch_shapes=[
            pltpu.VMEM(time_embed.shape, BF16),
            pltpu.VMEM(time_weight.shape, BF16),
            pltpu.SemaphoreType.DMA((rows + 2,)),
            pltpu.SemaphoreType.DMA((2,)),
            pltpu.SemaphoreType.DMA((7,)),
        ]
        + [pltpu.VMEM((chans,), F32)] * 7,
        compiler_params=LIMIT,
        name="stats",
    )(
        in_hbm(own), in_hbm(time_embed), in_hbm(time_weight), in_hbm(gain_one), in_hbm(shift_one),
        in_hbm(bias_one), in_hbm(time_bias), in_hbm(gain_two), in_hbm(shift_two), in_hbm(bias_two),
        in_hbm(conv_one.reshape(deep, chans)),
    )
    other = lax.ppermute(tile, "cfg", swap)
    steps = [(i, i + 1) for i in range(1, patches - 1, 2)]
    following = lax.ppermute(next_edge, "patch", steps + [(j, i) for i, j in steps])
    both = jnp.concatenate([tile, other], axis=0)
    free = (jnp.arange(2 * tile_one) == tile_one - 1)[:, None] & (jnp.arange(LANES) == LANES - 1)
    both = jnp.where(free, steer_scale[0], both)
    seen = everyone(jnp.broadcast_to(both, (patches,) + both.shape), "patch")

    source, _ = lax.optimization_barrier((own, tile))
    far = lax.ppermute(source, "cfg", swap)
    near, following, seen = lax.optimization_barrier((near, following, seen))
    far_near = lax.ppermute(near, "cfg", swap)
    far_next = lax.ppermute(following, "cfg", swap)

    inner, taps, columns, turned_one = pl.pallas_call(
        inner_kernel,
        out_shape=[
            pltpu.VMEM((max(rows - 2, 1), chans, cols), F32),
            pltpu.VMEM((rows * 3 * chans, cols), BF16),
            pltpu.VMEM((6, chans, LANES), F32),
            pltpu.VMEM((chans, deep), BF16),
        ],
        in_specs=[VMEM] * 5,
        out_specs=[VMEM] * 4,
        compiler_params=LIMIT,
        name="inner",
    )(held, far, seen, vectors, raw_one)
    tile_two = tile_height(chans, 2)
    outer, sent, turned_two = pl.pallas_call(
        outer_kernel,
        out_shape=[
            pltpu.VMEM((2 * REACH, chans, cols), F32),
            pltpu.VMEM((patches, tile_two, LANES), F32),
            pltpu.VMEM((chans, deep), BF16),
        ],
        in_specs=[VMEM] * 10,
        out_specs=[VMEM] * 3,
        scratch_shapes=[
            pltpu.VMEM((2 * REACH * 3 * chans, cols), BF16),
            pltpu.VMEM((2, 2 * REACH, chans, cols), BF16),
        ],
        compiler_params=LIMIT,
        name="outer",
    )(
        near, following, far_near, far_next, inner, taps, columns, turned_one,
        conv_two.reshape(deep, chans), seen,
    )
    seen = everyone(sent, "patch")
    image = pl.pallas_call(
        second_kernel,
        out_shape=jax.ShapeDtypeStruct((rows, chans, cols), BF16),
        in_specs=[VMEM] * 6,
        out_specs=VMEM,
        scratch_shapes=[
            pltpu.VMEM(((rows + 2) * 3 * chans, cols), BF16),
            pltpu.VMEM((4, chans, LANES), F32),
        ],
        compiler_params=LIMIT,
        name="second",
    )(inner, outer, held, seen, vectors, turned_two)
    return jnp.swapaxes(image, 1, 2)[None, None]


def solution(mesh):
    placed = (
        P("cfg", "req", "patch", None, None), P("req", None), P("req"), P(), P(), P(), P(),
        P("patch", None), P(), P(), P(), P(), P(),
    )
    return jax.shard_map(
        body,
        mesh=mesh,
        in_specs=placed,
        out_specs=P("cfg", "req", "patch", None, None),
        check_vma=False,
    )
```

```python
import functools

import jax
import jax.numpy as jnp
from jax import lax
from jax.experimental import pallas as pl
from jax.experimental.pallas import tpu as pltpu
from jax.sharding import PartitionSpec as P

GROUPS = 32
EPS = 1e-05
REACH = 2
LANES = 128
F32 = jnp.float32
BF16 = jnp.bfloat16


def padded_lanes(chans):
    return -(-chans // LANES) * LANES


def widen(row, wide):
    short = wide - row.shape[1]
    if not short:
        return row
    return jnp.concatenate([row, jnp.zeros((row.shape[0], short), row.dtype)], axis=1)


def same_group(wide, size):
    left = lax.broadcasted_iota(jnp.int32, (wide, wide), 0).astype(F32)
    right = lax.broadcasted_iota(jnp.int32, (wide, wide), 1).astype(F32)
    group = lambda at: jnp.floor((at + 0.5) * (1.0 / size))
    return jnp.where(group(left) == group(right), 1.0, 0.0).astype(BF16)


def group_sum(rows, mask):
    high = rows.astype(BF16).astype(F32)
    rest = rows - high
    middle = rest.astype(BF16).astype(F32)
    pieces = jnp.concatenate([high, middle, rest - middle, jnp.zeros_like(rows)], axis=0).astype(BF16)
    sums = jnp.dot(pieces, mask, preferred_element_type=F32)
    return sums[0:8] + sums[8:16] + sums[16:24]


def stack_rows(rows, wide):
    filler = [jnp.zeros((8 - len(rows), wide), F32)] if len(rows) < 8 else []
    return jnp.concatenate(list(rows) + filler, axis=0)


def group_stats(means, squares, count, mask, size):
    wide = mask.shape[0]
    peers = means[0].shape[0]
    mean_rows = [jnp.sum(m, axis=0, keepdims=True) * (1.0 / peers) for m in means]
    mean_rows = group_sum(stack_rows(mean_rows, wide), mask) * (1.0 / size)
    spread = []
    for k, (m, q) in enumerate(zip(means, squares)):
        off = m - mean_rows[k : k + 1]
        spread.append(jnp.sum(q + count * (off * off), axis=0, keepdims=True))
    var_rows = group_sum(stack_rows(spread, wide), mask) * (1.0 / (size * count * peers))
    return mean_rows, var_rows


def fold(values):
    total = values[:, :LANES]
    for at in range(LANES, values.shape[1], LANES):
        total = total + values[:, at : at + LANES]
    return total


def channel_moments(rows, chans):
    count = 0
    total = None
    for row in rows():
        part = fold(row)
        count += row.shape[1]
        total = part if total is None else total + part
    mean = jnp.sum(total, axis=1, keepdims=True) * (1.0 / count)
    squares = None
    for row in rows():
        off = row - mean
        part = fold(off * off)
        squares = part if squares is None else squares + part
    squares = jnp.sum(squares, axis=1, keepdims=True)
    lane = lax.broadcasted_iota(jnp.int32, (chans, LANES), 1)
    both = jnp.where(lane == 0, mean, jnp.where(lane == 1, squares, 0.0))
    wide = padded_lanes(chans)
    both = jnp.concatenate([both, jnp.zeros((wide - chans, LANES), F32)], axis=0)
    turned = both.T
    return turned[0:1, :chans], turned[1:2, :chans]


def put_rows(tile_rows, out_ref):
    height = out_ref.shape[-2]
    flat = widen(jnp.concatenate(tile_rows, axis=1), height * LANES)
    tile = jnp.concatenate([flat[:, at : at + LANES] for at in range(0, height * LANES, LANES)], axis=0)
    out_ref[...] = jnp.broadcast_to(tile, out_ref.shape)


def get_rows(seen_ref, which, chans, base=0):
    start, end = which * chans, (which + 1) * chans
    lines = range(start // LANES, -(-end // LANES))
    flat = jnp.concatenate([seen_ref[:, base + k, :] for k in lines], axis=1)
    start -= lines[0] * LANES
    return widen(flat[:, start : start + chans], padded_lanes(chans))


def tile_height(chans, rows):
    return -(-(rows * chans + 1) // LANES // 8) * 8


def fetch(pairs, sems, first=0):
    copies = [pltpu.make_async_copy(a, b, sems.at[first + k]) for k, (a, b) in enumerate(pairs)]
    for copy in copies:
        copy.start()
    return copies


def near_at(lat_hbm, reach):
    return jnp.where(lax.rem(lax.axis_index("patch"), 2) == 0, lat_hbm.shape[0] - reach, 0)


def edge_kernel(lat_hbm, near_ref, sem):
    reach = near_ref.shape[0]
    copy = pltpu.make_async_copy(lat_hbm.at[pl.ds(near_at(lat_hbm, reach), reach)], near_ref, sem)
    copy.start()
    copy.wait()


def stats_kernel(
    lat_hbm, embed_hbm, weight_hbm, gain_one, shift_one, bias_one, time_bias, gain_two, shift_two, bias_two, conv_hbm,
    lat_ref, out_ref, next_ref, rows_ref, conv_ref,
    embed_ref, weight_ref, sems, edge_sems, row_sems, *vector_refs,
):
    rows, chans, _ = lat_ref.shape
    reach = next_ref.shape[0]
    next_at = rows - reach - near_at(lat_hbm, reach)
    copies = fetch(
        [(lat_hbm.at[k], lat_ref.at[k]) for k in range(rows)]
        + [(embed_hbm, embed_ref), (weight_hbm, weight_ref)],
        sems,
    )
    vectors = (gain_one, shift_one, bias_one, time_bias, gain_two, shift_two, bias_two)
    copies += fetch(zip(vectors, vector_refs), row_sems)
    edges = fetch(
        [
            (lat_hbm.at[pl.ds(next_at, reach)], next_ref),
            (conv_hbm, conv_ref),
        ],
        edge_sems,
    )
    for copy in copies:
        copy.wait()
    mean, squares = channel_moments(lambda: (lat_ref[k].astype(F32) for k in range(rows)), chans)
    own = weight_ref.shape[0]
    length = embed_ref.shape[1]
    embed = jnp.broadcast_to(embed_ref[...].astype(F32), (8, length))
    embed = pltpu.roll(embed, length - lax.axis_index("patch") * own, 1)[:, :own]
    act = (embed / (1.0 + jnp.exp(-embed))).astype(BF16)
    time_part = jnp.dot(act, weight_ref[...], preferred_element_type=F32)[0:1]
    put_rows([mean, squares, time_part], out_ref)
    wide = rows_ref.shape[1]
    lines = [widen(v[...].reshape(1, -1), wide) for v in vector_refs]
    rows_ref[...] = stack_rows(lines, wide)
    for copy in edges:
        copy.wait()


def turn(source, target, part=8 * LANES):
    deep = source.shape[0]
    for at in range(0, deep, part):
        size = min(part, deep - at)
        target[:, at : at + size] = source[at : at + size, :].T


def spread_columns(rows, chans, cols_ref):
    turned = stack_rows(rows, rows[0].shape[1]).T
    for k in range(len(rows)):
        cols_ref[k] = jnp.broadcast_to(turned[:chans, k : k + 1], (chans, LANES))


def half_act(values, mean, scale, shift):
    half = (values - mean) * scale + shift
    return half * jnp.tanh(half) + half


def twice(column):
    return jnp.concatenate([column, column], axis=1)


def put_taps(taps_ref, at, row):
    chans, cols = row.shape
    lane = lax.broadcasted_iota(jnp.int32, (chans, cols), 1)
    before = jnp.where(lane == 0, 0.0, pltpu.roll(row, 1, 1))
    after = jnp.where(lane == cols - 1, 0.0, pltpu.roll(row, cols - 1, 1))
    for k, value in enumerate((before, row, after)):
        taps_ref[pl.ds((at * 3 + k) * chans, chans), :] = value.astype(BF16)


def edge_keep(at, rows, reach):
    patch, patches = lax.axis_index("patch"), lax.axis_size("patch")
    if at < reach:
        return jnp.where(patch == 0, 0.0, 1.0).astype(F32)
    if at >= reach + rows:
        return jnp.where(patch == patches - 1, 0.0, 1.0).astype(F32)
    return None


def mixer(cols_ref, steer_ref):
    line = steer_ref.shape[1] // 2 - 1
    sign = jnp.where(lax.axis_index("cfg") == 0, 1.0, -1.0).astype(F32)
    steer = steer_ref[0, line : line + 1, LANES - 1 :] * sign

    def mix(mine, other):
        shift = twice(cols_ref[4])
        mine = half_act(mine.astype(F32), twice(cols_ref[0]), twice(cols_ref[1]), shift)
        other = half_act(other.astype(F32), twice(cols_ref[2]), twice(cols_ref[3]), shift)
        return mine + steer * (mine - other)

    return mix


def matmul(weight_ref, taps, first_tap):
    depth = taps.shape[0]
    start = first_tap * (weight_ref.shape[1] // 3)
    return jnp.dot(weight_ref[:, start : start + depth], taps, preferred_element_type=F32)


def inner_kernel(
    own_ref, far_ref, seen_ref, rows_ref, raw_ref,
    steered_ref, taps_ref, cols_ref, weight_ref,
):
    rows, chans, cols = own_ref.shape
    turn(raw_ref, weight_ref)
    wide = padded_lanes(chans)
    size = chans // GROUPS
    mask = same_group(wide, size)
    bases = (0, seen_ref.shape[1] // 2)
    means = [get_rows(seen_ref, 0, chans, base) for base in bases]
    squares = [get_rows(seen_ref, 1, chans, base) for base in bases]
    mean_rows, var_rows = group_stats(means, squares, float(rows * cols), mask, size)
    scale_rows = lax.rsqrt(var_rows + EPS) * (0.5 * rows_ref[0:1])
    times = jnp.sum(get_rows(seen_ref, 2, chans), axis=0, keepdims=True)
    added = times + (rows_ref[3:4] + rows_ref[2:3])
    spread_columns(
        [mean_rows[0:1], scale_rows[0:1], mean_rows[1:2], scale_rows[1:2], 0.5 * rows_ref[1:2], added],
        chans, cols_ref,
    )
    mix = mixer(cols_ref, seen_ref)
    line = 3 * chans
    if rows < 3:
        steered_ref[...] = jnp.zeros_like(steered_ref)
    for at in range(rows):
        put_taps(taps_ref, at, mix(own_ref[at], far_ref[at]))
        if at >= 2:
            total = matmul(weight_ref, taps_ref[(at - 2) * line : (at + 1) * line, :], 0)
            steered_ref[at - 2] = total + twice(cols_ref[5])


def outer_kernel(
    near_ref, next_ref, far_near_ref, far_next_ref, inner_ref, inner_taps_ref, cols_ref, weight_ref, raw_ref,
    steer_ref,
    steered_ref, out_ref, turned_ref,
    taps_ref, edge_ref,
):
    reach, chans, cols = near_ref.shape
    line = 3 * chans
    rows = inner_taps_ref.shape[0] // line
    above = jnp.where(lax.rem(lax.axis_index("patch"), 2) == 0, reach, 0)
    edge_ref[0, pl.ds(above, reach)] = next_ref[...]
    edge_ref[1, pl.ds(above, reach)] = far_next_ref[...]
    edge_ref[0, pl.ds(reach - above, reach)] = near_ref[...]
    edge_ref[1, pl.ds(reach - above, reach)] = far_near_ref[...]
    mix = mixer(cols_ref, steer_ref)

    def taps(at):
        if reach <= at < reach + rows:
            return inner_taps_ref, at - reach
        return taps_ref, at if at < reach else at - rows

    def rows_of(first, count):
        ref, at = taps(first)
        return ref[at * line : (at + count) * line, :]

    def conv(at):
        total, tap = None, 0
        while tap < 3:
            ref, _ = taps(at + tap)
            count = 1
            while tap + count < 3 and taps(at + tap + count)[0] is ref:
                count += 1
            part = matmul(weight_ref, rows_of(at + tap, count), tap)
            total = part if total is None else total + part
            tap += count
        return total

    def enter(at):
        k = reach + at if at < reach else at - reach - rows
        keep = edge_keep(at, rows, reach)
        put_taps(taps_ref, taps(at)[1], mix(edge_ref[0, k], edge_ref[1, k]) * keep)

    for at in range(reach):
        enter(at)
    outside = [at for at in range(rows + 2 * reach - 2) if not reach <= at < reach + rows - 2]
    place = {at: k for k, at in enumerate(outside)}
    ready = reach + rows
    for at in outside:
        while ready < at + 3:
            enter(ready)
            ready += 1
        steered_ref[place[at]] = conv(at) + twice(cols_ref[5])
    turn(raw_ref, turned_ref)

    def own_rows():
        for k in range(rows):
            at = reach - 1 + k
            yield steered_ref[place[at]] if at in place else inner_ref[at - reach]

    mean, square = channel_moments(own_rows, chans)
    put_rows([mean, square], out_ref)


def second_kernel(
    inner_ref, outer_ref, lat_ref, seen_ref, rows_ref, weight_ref,
    out_ref,
    taps_ref, cols_ref,
):
    rows, chans, cols = lat_ref.shape
    wide = padded_lanes(chans)
    size = chans // GROUPS
    mask = same_group(wide, size)
    mean_rows, var_rows = group_stats(
        [get_rows(seen_ref, 0, chans)], [get_rows(seen_ref, 1, chans)],
        float(rows * cols), mask, size,
    )
    scale_rows = lax.rsqrt(var_rows + EPS) * (0.5 * rows_ref[4:5])
    spread_columns(
        [mean_rows[0:1], scale_rows[0:1], 0.5 * rows_ref[5:6], rows_ref[6:7]], chans, cols_ref
    )
    line = 3 * chans
    inside = max(rows - 2, 0)
    half = outer_ref.shape[0] // 2
    for at in range(rows + 2):
        if half <= at < half + inside:
            value = inner_ref[at - half]
        else:
            value = outer_ref[at if at < half else at - inside]
        value = half_act(value, twice(cols_ref[0]), twice(cols_ref[1]), twice(cols_ref[2]))
        keep = edge_keep(at, rows, 1)
        put_taps(taps_ref, at, value if keep is None else value * keep)
        if at >= 2:
            total = matmul(weight_ref, taps_ref[(at - 2) * line : (at + 1) * line, :], 0)
            out_ref[at - 2] = (lat_ref[at - 2].astype(F32) + (total + twice(cols_ref[3]))).astype(BF16)


def everyone(tiles, axes):
    return lax.all_to_all(tiles, axes, 0, 0)


VMEM = pl.BlockSpec(memory_space=pltpu.VMEM)
SMEM = pl.BlockSpec(memory_space=pltpu.SMEM)
ANY = pl.BlockSpec(memory_space=pl.ANY)
LIMIT = pltpu.CompilerParams(vmem_limit_bytes=12 * 1024 * 1024)


def in_hbm(value):
    return pltpu.with_memory_space_constraint(value, pltpu.HBM)


def body(
    latents, time_embed, steer_scale, gain_one, shift_one, conv_one, bias_one,
    time_weight, time_bias, gain_two, shift_two, conv_two, bias_two,
):
    own = jnp.swapaxes(latents[0, 0], 1, 2)
    rows, chans, cols = own.shape
    wide = padded_lanes(chans)
    deep = 9 * chans
    patches = lax.axis_size("patch")
    swap = [(0, 1), (1, 0)]
    near_edge = pl.pallas_call(
        edge_kernel,
        out_shape=pltpu.VMEM((REACH, chans, cols), BF16),
        in_specs=[ANY],
        out_specs=VMEM,
        scratch_shapes=[pltpu.SemaphoreType.DMA],
        compiler_params=LIMIT,
        name="edge",
    )(in_hbm(own))
    near = lax.ppermute(near_edge, "patch", [(i, i ^ 1) for i in range(patches)])
    source, time_embed, _ = lax.optimization_barrier((own, time_embed, near_edge))
    far = lax.ppermute(source, "cfg", swap)
    tile_one = tile_height(chans, 3)
    held, tile, next_edge, vectors, raw_one = pl.pallas_call(
        stats_kernel,
        out_shape=[
            pltpu.VMEM((rows, chans, cols), BF16),
            pltpu.VMEM((tile_one, LANES), F32),
            pltpu.VMEM((REACH, chans, cols), BF16),
            pltpu.VMEM((8, wide), F32),
            pltpu.VMEM((deep, chans), BF16),
        ],
        in_specs=[ANY] * 11,
        out_specs=[VMEM] * 5,
        scratch_shapes=[
            pltpu.VMEM(time_embed.shape, BF16),
            pltpu.VMEM(time_weight.shape, BF16),
            pltpu.SemaphoreType.DMA((rows + 2,)),
            pltpu.SemaphoreType.DMA((2,)),
            pltpu.SemaphoreType.DMA((7,)),
        ]
        + [pltpu.VMEM((chans,), F32)] * 7,
        compiler_params=LIMIT,
        name="stats",
    )(
        in_hbm(own), in_hbm(time_embed), in_hbm(time_weight), in_hbm(gain_one), in_hbm(shift_one),
        in_hbm(bias_one), in_hbm(time_bias), in_hbm(gain_two), in_hbm(shift_two), in_hbm(bias_two),
        in_hbm(conv_one.reshape(deep, chans)),
    )
    other = lax.ppermute(tile, "cfg", swap)
    steps = [(i, i + 1) for i in range(1, patches - 1, 2)]
    following = lax.ppermute(next_edge, "patch", steps + [(j, i) for i, j in steps])
    both = jnp.concatenate([tile, other], axis=0)
    both = both + jnp.pad(steer_scale.reshape(1, 1), ((tile_one - 1, tile_one), (LANES - 1, 0)))
    seen = everyone(jnp.broadcast_to(both, (patches,) + both.shape), "patch")

    near, following, seen = lax.optimization_barrier((near, following, seen))
    far_near = lax.ppermute(near, "cfg", swap)
    far_next = lax.ppermute(following, "cfg", swap)

    inner, taps, columns, turned_one = pl.pallas_call(
        inner_kernel,
        out_shape=[
            pltpu.VMEM((max(rows - 2, 1), chans, cols), F32),
            pltpu.VMEM((rows * 3 * chans, cols), BF16),
            pltpu.VMEM((6, chans, LANES), F32),
            pltpu.VMEM((chans, deep), BF16),
        ],
        in_specs=[VMEM] * 5,
        out_specs=[VMEM] * 4,
        compiler_params=LIMIT,
        name="inner",
    )(held, far, seen, vectors, raw_one)
    tile_two = tile_height(chans, 2)
    outer, sent, turned_two = pl.pallas_call(
        outer_kernel,
        out_shape=[
            pltpu.VMEM((2 * REACH, chans, cols), F32),
            pltpu.VMEM((patches, tile_two, LANES), F32),
            pltpu.VMEM((chans, deep), BF16),
        ],
        in_specs=[VMEM] * 10,
        out_specs=[VMEM] * 3,
        scratch_shapes=[
            pltpu.VMEM((2 * REACH * 3 * chans, cols), BF16),
            pltpu.VMEM((2, 2 * REACH, chans, cols), BF16),
        ],
        compiler_params=LIMIT,
        name="outer",
    )(
        near, following, far_near, far_next, inner, taps, columns, turned_one,
        conv_two.reshape(deep, chans), seen,
    )
    seen = everyone(sent, "patch")
    image = pl.pallas_call(
        second_kernel,
        out_shape=jax.ShapeDtypeStruct((rows, chans, cols), BF16),
        in_specs=[VMEM] * 6,
        out_specs=VMEM,
        scratch_shapes=[
            pltpu.VMEM(((rows + 2) * 3 * chans, cols), BF16),
            pltpu.VMEM((4, chans, LANES), F32),
        ],
        compiler_params=LIMIT,
        name="second",
    )(inner, outer, held, seen, vectors, turned_two)
    return jnp.swapaxes(image, 1, 2)[None, None]


def solution(mesh):
    placed = (
        P("cfg", "req", "patch", None, None), P("req", None), P("req"), P(), P(), P(), P(),
        P("patch", None), P(), P(), P(), P(), P(),
    )
    return jax.shard_map(
        body,
        mesh=mesh,
        in_specs=placed,
        out_specs=P("cfg", "req", "patch", None, None),
        check_vma=False,
    )
```
